128 devices in a mesh: seq: 32 (over z, y, core), ch: 4 (over x).
Axes of the slice: x: 4, y: 4, z: 4, core: 2. Of those that a mesh axis runs over, the one named last changes fastest.
Arguments:
- hidden: bfloat16 [16384, 1024], P('seq'), may hold values from -6 to 6
- proj_x: bfloat16 [1024, 2048], P(None, 'ch'), may hold values from -0.1875 to 0.1875
- proj_z: bfloat16 [1024, 2048], P(None, 'ch'), may hold values from -0.1875 to 0.1875
- proj_b: bfloat16 [1024, 16], replicated, may hold values from -0.005859375 to 0.005859375
- proj_c: bfloat16 [1024, 16], replicated, may hold values from -0.046875 to 0.046875
- proj_dt: bfloat16 [1024, 32], P(None, 'ch'), may hold values from -0.1875 to 0.1875
- dt_bias: float32 [32], P('ch'), may hold values from -2 to 0.5
- decay_rate: float32 [32], P('ch'), may hold values from 0 to 1, as said below
- skip_gain: float32 [32], P('ch'), may hold values from 0.5 to 1.5
- proj_out: bfloat16 [2048, 1024], P('ch'), may hold values from -0.125 to 0.125
- cotangent: bfloat16 [16384, 1024], P('seq', 'ch'), may hold values from -6 to 6
Outputs:
- block_out: bfloat16 [16384, 1024], P('seq', 'ch')
- grad_hidden: float32 [16384, 1024], P('seq', 'ch')
- grad_proj_x: float32 [1024, 2048], P('seq', 'ch')
- grad_proj_z: float32 [1024, 2048], P('seq', 'ch')
- grad_proj_out: float32 [2048, 1024], P('ch', 'seq')
The draws below stay inside these ranges and needn't reach their ends.
Inputs may be any that keep to these rules, and one draw needn't show every extreme that they name: `decay_rate`: positive rates.
All inputs are finite; a program needn't handle non-finite values.
Results may differ from the reference program's by a relative error of at most 0.0055.
Values may be sent and summed in bfloat16 or wider, within the bound.
A program may use at most 256 MiB of HBM per device.

```python
import math
import jax
import jax.numpy as jnp
from jax import lax

D = 1024
E = 2048
HEAD = 64
HEADS = 32
NS = 16
Q = 256
TOKENS = 16384


def draw_decay_rate(key, part):
    key = jax.random.fold_in(key, 7)
    slow_key, fast_key, pick_key = jax.random.split(key, 3)
    slow_rate = jnp.exp(jax.random.uniform(slow_key, (HEADS,), jnp.float32, math.log(0.1 / TOKENS), math.log(2.0 / TOKENS)))
    fast_rate = jnp.exp(jax.random.uniform(fast_key, (HEADS,), jnp.float32, math.log(1.0 / 50.0), math.log(1.0 / 20.0)))
    picked = jax.random.randint(pick_key, (HEADS,), 0, 2) == 0
    return jnp.where(picked, fast_rate, slow_rate).astype(jnp.float32)


def steps_of(rng, dims, cuts, low, top_value):
    level, own = 1.0, jax.random.fold_in(rng, 6)
    for position, shards_of in cuts:
        heights = jnp.exp(jax.random.uniform(jax.random.fold_in(own, position), (shards_of,), jnp.float32, low / len(cuts), top_value / len(cuts)))
        level = level * jnp.repeat(heights, dims[position] // shards_of).reshape([-1 if axis == position else 1 for axis in range(len(dims))])
    return level


def bell_draw(own_key, extent, scale, bound, shards=(), held_as=jnp.bfloat16):
    level = steps_of(own_key, extent, shards, -0.22, 0.18) if shards else 1.0
    result = jax.random.normal(own_key, extent, jnp.float32) * scale * level
    return jnp.minimum(jnp.maximum(result, -bound), bound).astype(held_as)


def setup_inputs(seed: int = 0) -> dict:
    arg_keys = jax.random.split(jax.random.key(seed), 12)
    return {
        "hidden": bell_draw(arg_keys[0], (TOKENS, D), 1.0, 6.0, ((0, 32),)),
        "proj_x": bell_draw(arg_keys[1], (D, E), D ** -0.5, 0.1875, ((1, 4),)),
        "proj_z": bell_draw(arg_keys[2], (D, E), D ** -0.5, 0.1875, ((1, 4),)),
        "proj_b": bell_draw(arg_keys[3], (D, NS), (D * 1024) ** -0.5, 0.005859375),
        "proj_c": bell_draw(arg_keys[4], (D, NS), (D * NS) ** -0.5, 0.046875),
        "proj_dt": bell_draw(arg_keys[5], (D, HEADS), D ** -0.5, 0.1875, ((1, 4),)),
        "dt_bias": jnp.clip(-2.0 + 2.5 * jax.random.uniform(arg_keys[6], (HEADS,), jnp.float32) ** steps_of(arg_keys[6], (HEADS,), ((0, 4),), -0.2, 0.2), -2.0, 0.5),
        "decay_rate": draw_decay_rate(jax.random.fold_in(arg_keys[11], 71), 0),
        "skip_gain": jnp.clip(0.5 + 1.0 * jax.random.uniform(arg_keys[8], (HEADS,), jnp.float32) ** steps_of(arg_keys[8], (HEADS,), ((0, 4),), -0.2, 0.2), 0.5, 1.5),
        "proj_out": bell_draw(arg_keys[9], (E, D), E ** -0.5, 0.125, ((0, 4),)),
        "cotangent": bell_draw(arg_keys[10], (TOKENS, D), 1.0, 6.0, ((0, 32), (1, 4))),
    }


PRECISE = lax.Precision.HIGHEST

def group_scan(x_proj, b_proj, c_proj, dt_proj, dt_bias, decay_rate):
    length = x_proj.shape[0]
    head_count = dt_bias.shape[0]
    head_width = x_proj.shape[1] // head_count
    blocks = length // Q
    step_size = jax.nn.softplus(dt_proj + dt_bias[None, :])
    log_decay = -decay_rate[None, :] * step_size
    causal = jnp.arange(Q)[:, None] >= jnp.arange(Q)[None, :]

    @jax.checkpoint
    def advance(carried, pieces):
        x_block, b_block, c_block, step_block, decay_block = pieces
        cumulative = jnp.cumsum(decay_block, axis=0).T
        spread = cumulative[:, :, None] - cumulative[:, None, :]
        kernel = jnp.where(causal[None], jnp.exp(jnp.where(causal[None], spread, 0.0)), 0.0)
        scores = jnp.dot(c_block, b_block.T, precision=PRECISE)
        mixing = scores[None] * kernel * step_block.T[:, None, :]
        within = jnp.einsum('hts,shp->thp', mixing, x_block, precision=PRECISE)
        entering = jnp.einsum('tn,hpn->thp', c_block, carried, precision=PRECISE) * jnp.exp(cumulative).T[:, :, None]
        final_log = cumulative[:, -1]
        weights = jnp.exp(final_log[:, None] - cumulative) * step_block.T
        updated = jnp.exp(final_log)[:, None, None] * carried + jnp.einsum('hs,shp,sn->hpn', weights, x_block, b_block, precision=PRECISE)
        return (updated, within + entering)
    start_state = jnp.zeros((head_count, head_width, b_proj.shape[1]), jnp.float32)
    pieces = (x_proj.reshape(blocks, Q, head_count, head_width), b_proj.reshape(blocks, Q, -1), c_proj.reshape(blocks, Q, -1), step_size.reshape(blocks, Q, head_count), log_decay.reshape(blocks, Q, head_count))
    final_state, outputs = lax.scan(advance, start_state, pieces)
    return (outputs.reshape(length, head_count, head_width), final_state, lax.optimization_barrier(jnp.sum(log_decay, axis=0)))

def finish(within, state_in, x_proj, z_proj, c_proj, dt_proj, dt_bias, decay_rate, skip_gain):
    length, head_count, head_width = within.shape
    step_size = jax.nn.softplus(dt_proj + dt_bias[None, :])
    log_decay = -decay_rate[None, :] * step_size
    cumulative = jnp.cumsum(log_decay, axis=0)
    entering = jnp.einsum('tn,hpn->thp', c_proj, state_in, precision=PRECISE) * jnp.exp(cumulative)[:, :, None]
    gathered = within + entering + skip_gain[None, :, None] * x_proj.reshape(length, head_count, head_width)
    return gathered.reshape(length, head_count * head_width) * jax.nn.silu(z_proj)

def reference(hidden, proj_x, proj_z, proj_b, proj_c, proj_dt, dt_bias, decay_rate, skip_gain, proj_out, cotangent):
    rc_in = hidden[::-1, ::-1]

    def project(strand_in):
        return tuple((jnp.dot(strand_in, weight, preferred_element_type=jnp.float32) for weight in (proj_x, proj_z, proj_b, proj_c, proj_dt)))

    def strand(x_proj, z_proj, b_proj, c_proj, dt_proj):
        within, final_state, log_total = group_scan(x_proj, b_proj, c_proj, dt_proj, dt_bias, decay_rate)
        zero_state = jnp.zeros((HEADS, HEAD, NS), jnp.float32)
        return finish(within, zero_state, x_proj, z_proj, c_proj, dt_proj, dt_bias, decay_rate, skip_gain)
    out_fwd, back_fwd = jax.vjp(strand, *project(hidden))
    out_rc, back_rc = jax.vjp(strand, *project(rc_in))
    gated_fwd = out_fwd.astype(jnp.bfloat16)
    gated_rc = out_rc.astype(jnp.bfloat16)[::-1]
    proj_flip = proj_out[:, ::-1]
    block_out = (hidden.astype(jnp.float32) + jnp.dot(gated_fwd, proj_out, preferred_element_type=jnp.float32) + jnp.dot(gated_rc, proj_flip, preferred_element_type=jnp.float32)).astype(jnp.bfloat16)
    grad_proj_out = jnp.dot(gated_fwd.T, cotangent, preferred_element_type=jnp.float32) + jnp.dot(gated_rc.T, cotangent[:, ::-1], preferred_element_type=jnp.float32)
    d_out = jnp.dot(cotangent, proj_out.T, preferred_element_type=jnp.float32).astype(jnp.bfloat16)
    d_out_rc = jnp.dot(cotangent, proj_flip.T, preferred_element_type=jnp.float32).astype(jnp.bfloat16)

    def input_grads(grads):
        dx_val, dz_val, db_val, dc_val, ddt_val = grads
        dx_round = dx_val.astype(jnp.bfloat16)
        dz_round = dz_val.astype(jnp.bfloat16)
        d_strand = jnp.dot(dx_round, proj_x.T, preferred_element_type=jnp.float32) + jnp.dot(dz_round, proj_z.T, preferred_element_type=jnp.float32) + jnp.dot(db_val, proj_b.astype(jnp.float32).T, precision=PRECISE) + jnp.dot(dc_val, proj_c.astype(jnp.float32).T, precision=PRECISE) + jnp.dot(ddt_val, proj_dt.astype(jnp.float32).T, precision=PRECISE)
        return (d_strand, dx_round, dz_round)
    d_fwd, dx_fwd, dz_fwd = input_grads(back_fwd(d_out.astype(jnp.float32)))
    d_rc, dx_rc, dz_rc = input_grads(back_rc(d_out_rc[::-1].astype(jnp.float32)))
    grad_proj_x = jnp.dot(hidden.T, dx_fwd, preferred_element_type=jnp.float32) + jnp.dot(rc_in.T, dx_rc, preferred_element_type=jnp.float32)
    grad_proj_z = jnp.dot(hidden.T, dz_fwd, preferred_element_type=jnp.float32) + jnp.dot(rc_in.T, dz_rc, preferred_element_type=jnp.float32)
    grad_hidden = cotangent.astype(jnp.float32) + d_fwd + d_rc[::-1, ::-1]
    return (block_out, grad_hidden, grad_proj_x, grad_proj_z, grad_proj_out)
```

```python
import functools

import jax
import jax.numpy as jnp
from jax import lax
from jax.experimental import pallas as pl
from jax.experimental.pallas import tpu as pltpu
from jax.sharding import PartitionSpec as P

L = 512
D = 1024
W = 512
HEADS = 8
HEAD = 64
NS = 16
Q = 256
CHUNKS = L // Q
NSEQ = 32
F32 = jnp.float32
BF16 = jnp.bfloat16

LAST = (((1,), (1,)), ((), ()))
FIRST = (((0,), (0,)), ((), ()))


def mm(a, b):
    return jnp.dot(a, b, preferred_element_type=F32)


def mm_t(a, b):
    return lax.dot_general(a, b, LAST, preferred_element_type=F32)


def t_mm(a, b):
    return lax.dot_general(a, b, FIRST, preferred_element_type=F32)


def split2(v):
    high = v.astype(BF16)
    return high, (v - high.astype(F32)).astype(BF16)


def split3(v):
    high = v.astype(BF16)
    rest = v - high.astype(F32)
    mid = rest.astype(BF16)
    return high, mid, (rest - mid.astype(F32)).astype(BF16)


def iota(shape, dim):
    return lax.broadcasted_iota(jnp.int32, shape, dim)


def anti_identity():
    return jnp.where(iota((Q, Q), 0) + iota((Q, Q), 1) == Q - 1, 1.0, 0.0).astype(BF16)


def spread_matrix():
    return jnp.where(iota((HEADS, W), 1) // HEAD == iota((HEADS, W), 0), 1.0, 0.0).astype(BF16)


def spread(v, e):
    high, low = split2(v)
    return mm(high, e) + mm(low, e)


def gather_heads(v, e):
    high, low = split2(v)
    return mm_t(high, e) + mm_t(low, e)


def order(strand, transposed=False):
    rows, columns = iota((Q, Q), 0), iota((Q, Q), 1)
    later = strand == 0
    if transposed:
        later = not later
    return rows >= columns if later else rows <= columns


def running(v, mask):
    ones = jnp.where(mask, 1.0, 0.0).astype(BF16)
    return sum(mm(ones, part) for part in split3(v))


def softplus(v):
    return jnp.maximum(v, 0.0) + jnp.log1p(jnp.exp(-jnp.abs(v)))


def sigmoid(v):
    return 1.0 / (1.0 + jnp.exp(-v))


def flip_columns(src, dst, anti):
    n = src.shape[1] // Q
    for k in range(n):
        dst[:, k * Q : (k + 1) * Q] = mm(src[:, (n - 1 - k) * Q : (n - k) * Q], anti).astype(BF16)


def flip_rows(src, dst, anti):
    n = src.shape[0] // Q
    for k in range(n):
        dst[k * Q : (k + 1) * Q, :] = mm(anti, src[(n - 1 - k) * Q : (n - k) * Q, :]).astype(BF16)


def project_kernel(
    hidden, proj_x, proj_z, proj_b, proj_c, proj_dt, bias, rate, proj_out, cot,
    xs, zs, bs, cs, dts, dos, hidden_flip, cot_flip, px_flip, pz_flip, pb_flip, pc_flip, pd_flip, po_flip,
    state_out,
    decay_out,
):
    anti = anti_identity()
    e = spread_matrix()
    flip_rows(proj_x, px_flip, anti)
    flip_rows(proj_z, pz_flip, anti)
    flip_rows(proj_b, pb_flip, anti)
    flip_rows(proj_c, pc_flip, anti)
    flip_rows(proj_dt, pd_flip, anti)
    flip_columns(proj_out, po_flip, anti)
    flip_columns(hidden, hidden_flip, anti)
    flip_columns(cot, cot_flip, anti)
    weights = (
        (proj_x, proj_z, proj_b, proj_c, proj_dt, proj_out),
        (px_flip, pz_flip, pb_flip, pc_flip, pd_flip, po_flip),
    )
    for strand in range(2):
        w_x, w_z, w_b, w_c, w_dt, w_out = weights[strand]

        def rows_step(k, carry):
            rows = pl.ds(pl.multiple_of(k * Q, Q), Q)
            u = hidden[rows, :]
            xs[strand, rows, :] = mm(u, w_x[...])
            zs[strand, rows, :] = mm(u, w_z[...])
            bs[strand, rows, :] = mm(u, w_b[...])
            cs[strand, rows, :] = mm(u, w_c[...])
            dts[strand, rows, :] = mm(u, w_dt[...])
            dos[strand, rows, :] = mm_t(cot[rows, :], w_out[...]).astype(BF16)
            return carry

        lax.fori_loop(0, CHUNKS, rows_step, 0)

        def state_step(i, carry):
            k = i if strand == 0 else CHUNKS - 1 - i
            rows = pl.ds(pl.multiple_of(k * Q, Q), Q)
            state, grad, before = carry
            dt = softplus(dts[strand, rows, :] + bias[...])
            a = -rate[...] * dt
            cum = running(a, order(strand))
            total = jnp.sum(a, axis=0, keepdims=True)
            z = zs[strand, rows, :]
            dy = dos[strand, rows, :].astype(F32) * (z * sigmoid(z))
            weighted = (xs[strand, rows, :] * spread(jnp.exp(total - cum) * dt, e)).astype(BF16)
            local = t_mm(bs[strand, rows, :].astype(BF16), weighted)
            dyw = (dy * spread(jnp.exp(cum), e)).astype(BF16)
            local_grad = t_mm(cs[strand, rows, :].astype(BF16), dyw)
            here = jnp.exp(spread(total, e))
            return (here * state + local, grad + before * local_grad, before * here)

        zero = jnp.zeros((NS, W), F32)
        state, grad, decay = lax.fori_loop(
            0, CHUNKS, state_step, (zero, zero, jnp.ones((1, W), F32))
        )
        state_out[2 * strand] = state
        state_out[2 * strand + 1] = grad
        decay_out[strand] = jnp.broadcast_to(decay, (8, W))


def scan_kernel(
    hidden, proj_x, proj_z, proj_b, proj_c, proj_dt, bias, rate, skip, proj_out, cot,
    xs, zs, bs, cs, dts, dos, hidden_flip, cot_flip, px_flip, pz_flip, pb_flip, pc_flip, pd_flip, po_flip,
    states, decays,
    mix, grad_in, grad_w, grad_out,
    os, dxs, dzs, dbs, dcs, ddts, yi, gi, dyb, xdt, zacc, chunk_state, chunk_grad, chunk_decay,
):
    e = spread_matrix()
    me = lax.axis_index("seq")
    skip_wide = spread(skip[...], e)
    weights = (
        (proj_x, proj_z, proj_b, proj_c, proj_dt, proj_out),
        (px_flip, pz_flip, pb_flip, pc_flip, pd_flip, po_flip),
    )
    zero = jnp.zeros((NS, W), F32)
    for strand in range(2):
        w_x, w_z, w_b, w_c, w_dt, w_out = weights[strand]
        rising = strand == 0

        def up(j, carry, kind):
            new = carry * decays[j, strand, 0:1, :] + states[j, 2 * strand + kind]
            return jnp.where(j < me, new, carry)

        def down(i, carry, kind):
            j = NSEQ - 1 - i
            new = carry * decays[j, strand, 0:1, :] + states[j, 2 * strand + kind]
            return jnp.where(j > me, new, carry)

        state_in = lax.fori_loop(0, NSEQ, functools.partial(up if rising else down, kind=0), zero)
        grad_end = lax.fori_loop(0, NSEQ, functools.partial(down if rising else up, kind=1), zero)

        def inner_step(k, carry):
            rows = pl.ds(pl.multiple_of(k * Q, Q), Q)
            mask = order(strand)
            dt = softplus(dts[strand, rows, :] + bias[...])
            a = -rate[...] * dt
            cum = running(a, mask)
            cum_t = cum.T
            total = jnp.sum(a, axis=0, keepdims=True)
            z = zs[strand, rows, :]
            dy = dos[strand, rows, :].astype(F32) * (z * sigmoid(z))
            x = xs[strand, rows, :]
            xd = x * spread(dt, e)
            dyb[...] = dy.astype(BF16)
            xdt[...] = xd.astype(BF16)
            b = bs[strand, rows, :].astype(BF16)
            c = cs[strand, rows, :].astype(BF16)
            scores = mm_t(c, b)
            lane = iota((Q, 128), 1)
            for pair in range(HEADS // 2):
                columns = slice(pair * 128, (pair + 1) * 128)
                y_pair = None
                for half in range(2):
                    h = 2 * pair + half
                    own = (lane >= 64) if half else (lane < 64)
                    x_own = jnp.where(own, xdt[:, columns], jnp.zeros((), BF16))
                    dy_own = jnp.where(own, dyb[:, columns], jnp.zeros((), BF16))
                    decay = jnp.exp(
                        jnp.where(mask, cum[:, h : h + 1] - cum_t[h : h + 1, :], -1e30)
                    )
                    cross = mm_t(dy_own, xdt[:, columns])
                    mixing = (decay * scores).astype(BF16)
                    if h == 0:
                        zacc[...] = decay * cross
                    else:
                        zacc[...] += decay * cross
                    y_new, g_new = mm(mixing, x_own), t_mm(mixing, dy_own)
                    y_pair, g_pair = (
                        (y_new, g_new) if y_pair is None else (y_pair + y_new, g_pair + g_new)
                    )
                yi[rows, columns] = y_pair
                gi[rows, columns] = g_pair
            both = zacc[...].astype(BF16)
            dcs[rows, :] = mm(both, b)
            dbs[rows, :] = t_mm(both, c)
            e_cum = spread(jnp.exp(cum), e)
            e_rest = spread(jnp.exp(total - cum), e)
            here = jnp.exp(spread(total, e))
            chunk_state[k] = t_mm(b, (xd * e_rest).astype(BF16))
            chunk_grad[k] = t_mm(c, (dy * e_cum).astype(BF16))
            chunk_decay[k] = jnp.broadcast_to(here, (8, W))
            return carry

        lax.fori_loop(0, CHUNKS, inner_step, 0)

        times = list(range(CHUNKS)) if rising else list(range(CHUNKS))[::-1]
        entering, leaving, leaving_grad = {}, {}, {}
        state = state_in
        for k in times:
            entering[k] = state
            state = chunk_decay[k, 0:1, :] * state + chunk_state[k]
            leaving[k] = state
        grad = grad_end
        for k in times[::-1]:
            leaving_grad[k] = grad
            grad = chunk_decay[k, 0:1, :] * grad + chunk_grad[k]
        for k in range(CHUNKS):
            chunk_state[k] = entering[k]
            chunk_grad[k] = leaving_grad[k]
            chunk_decay[k] = jnp.broadcast_to(
                jnp.sum(leaving[k] * leaving_grad[k], axis=0, keepdims=True), (8, W)
            )

        def outer_step(k, carry):
            rows = pl.ds(pl.multiple_of(k * Q, Q), Q)
            mask = order(strand)
            raw = dts[strand, rows, :] + bias[...]
            dt = softplus(raw)
            a = -rate[...] * dt
            cum = running(a, mask)
            total = jnp.sum(a, axis=0, keepdims=True)
            e_cum = spread(jnp.exp(cum), e)
            e_rest = spread(jnp.exp(total - cum), e)
            dt_wide = spread(dt, e)
            b = bs[strand, rows, :].astype(BF16)
            c = cs[strand, rows, :].astype(BF16)
            state = chunk_state[k].astype(BF16)
            grad = chunk_grad[k].astype(BF16)
            x = xs[strand, rows, :]
            z = zs[strand, rows, :]
            d_o = dos[strand, rows, :].astype(F32)
            sig = sigmoid(z)
            silu = z * sig
            dy = d_o * silu
            y_part = yi[rows, :] + e_cum * mm(c, state)
            gb = gi[rows, :] + e_rest * mm(b, grad)
            y = y_part + skip_wide * x
            os[strand, rows, :] = (y * silu).astype(BF16)
            dzs[strand, rows, :] = (d_o * y * (sig + silu * (1.0 - sig))).astype(BF16)
            dxs[strand, rows, :] = (dt_wide * gb + skip_wide * dy).astype(BF16)
            d_c = dcs[rows, :] + mm_t((dy * e_cum).astype(BF16), state)
            d_b = dbs[rows, :] + mm_t((x * dt_wide * e_rest).astype(BF16), grad)
            direct = gather_heads(x * gb, e)
            d_cum = gather_heads(dy * y_part, e) - dt * direct
            d_a = running(d_cum, order(strand, True)) + gather_heads(
                chunk_decay[k], e
            )[0:1, :]
            d_raw = (direct - rate[...] * d_a) * sigmoid(raw)
            extra = (
                mm_t(d_b.astype(BF16), w_b[...])
                + mm_t(d_c.astype(BF16), w_c[...])
                + mm_t(d_raw.astype(BF16), w_dt[...])
            )
            if strand == 0:
                grad_in[rows, :] = extra
            else:
                grad_in[rows, :] += extra
            grad_in[rows, :] += mm_t(dxs[strand, rows, :], w_x[...]) + mm_t(
                dzs[strand, rows, :], w_z[...]
            )
            part = mm(os[strand, rows, :], w_out[...])
            if strand == 0:
                mix[rows, :] = part
            else:
                mix[rows, :] += part
            return carry

        lax.fori_loop(0, CHUNKS, outer_step, 0)

    def weight_step(k, carry):
        cols = pl.ds(pl.multiple_of(k * Q, Q), Q)
        grad_w[cols, 0:W] = t_mm(hidden[:, cols], dxs[0]) + t_mm(hidden_flip[:, cols], dxs[1])
        grad_w[cols, W:] = t_mm(hidden[:, cols], dzs[0]) + t_mm(hidden_flip[:, cols], dzs[1])
        grad_out[cols, :] = t_mm(cot[:, cols], os[0]) + t_mm(cot_flip[:, cols], os[1])
        return carry

    lax.fori_loop(0, D // Q, weight_step, 0)


def shape(*dims, dtype=F32):
    return jax.ShapeDtypeStruct(dims, dtype)


VMEM = pl.BlockSpec(memory_space=pltpu.VMEM)


def body(
    hidden, proj_x, proj_z, proj_b, proj_c, proj_dt, dt_bias, decay_rate, skip_gain, proj_out, cotangent
):
    cot = lax.all_gather(cotangent, "ch", axis=1, tiled=True)
    bias, rate, skip = (v[None, :] for v in (dt_bias, decay_rate, skip_gain))
    saved_shapes = (
        shape(2, L, W),
        shape(2, L, W),
        shape(2, L, NS),
        shape(2, L, NS),
        shape(2, L, HEADS),
        shape(2, L, W, dtype=BF16),
        shape(L, D, dtype=BF16),
        shape(L, D, dtype=BF16),
        shape(D, W, dtype=BF16),
        shape(D, W, dtype=BF16),
        shape(D, NS, dtype=BF16),
        shape(D, NS, dtype=BF16),
        shape(D, HEADS, dtype=BF16),
        shape(W, D, dtype=BF16),
    )
    *saved, state, decay = pl.pallas_call(
        project_kernel,
        out_shape=saved_shapes + (shape(4, NS, W), shape(2, 8, W)),
        in_specs=[VMEM] * 10,
        out_specs=[VMEM] * 16,
        compiler_params=pltpu.CompilerParams(vmem_limit_bytes=56 * 2**20),
        name="project",
    )(hidden, proj_x, proj_z, proj_b, proj_c, proj_dt, bias, rate, proj_out, cot)
    states = lax.all_gather(state, "seq")
    decays = lax.all_gather(decay, "seq")
    mix, grad_in, grad_w, grad_out = pl.pallas_call(
        scan_kernel,
        out_shape=(shape(L, D), shape(L, D), shape(D, 2 * W), shape(D, W)),
        in_specs=[VMEM] * 27,
        out_specs=[VMEM] * 4,
        scratch_shapes=[
            pltpu.VMEM((2, L, W), BF16),
            pltpu.VMEM((2, L, W), BF16),
            pltpu.VMEM((2, L, W), BF16),
            pltpu.VMEM((L, NS), F32),
            pltpu.VMEM((L, NS), F32),
            pltpu.VMEM((L, HEADS), F32),
            pltpu.VMEM((L, W), F32),
            pltpu.VMEM((L, W), F32),
            pltpu.VMEM((Q, W), BF16),
            pltpu.VMEM((Q, W), BF16),
            pltpu.VMEM((Q, Q), F32),
            pltpu.VMEM((CHUNKS, NS, W), F32),
            pltpu.VMEM((CHUNKS, NS, W), F32),
            pltpu.VMEM((CHUNKS, 8, W), F32),
        ],
        compiler_params=pltpu.CompilerParams(vmem_limit_bytes=60 * 2**20),
        name="scan",
    )(
        hidden, proj_x, proj_z, proj_b, proj_c, proj_dt, bias, rate, skip, proj_out, cot,
        *saved, states, decays,
    )
    width = cotangent.shape[1]
    residual = lax.dynamic_slice_in_dim(hidden, lax.axis_index("ch") * width, width, 1)
    mixed = lax.psum_scatter(mix, "ch", scatter_dimension=1, tiled=True)
    block_out = (residual.astype(F32) + mixed).astype(BF16)
    grad_hidden = cotangent.astype(F32) + lax.psum_scatter(
        grad_in, "ch", scatter_dimension=1, tiled=True
    )
    both = lax.psum_scatter(grad_w, "seq", scatter_dimension=0, tiled=True)
    grad_proj_out = lax.psum_scatter(grad_out, "seq", scatter_dimension=0, tiled=True).T
    return (block_out, grad_hidden, both[:, :W], both[:, W:], grad_proj_out)


def solution(mesh):
    return jax.shard_map(
        body,
        mesh=mesh,
        in_specs=(
            P("seq", None),
            P(None, "ch"),
            P(None, "ch"),
            P(),
            P(),
            P(None, "ch"),
            P("ch"),
            P("ch"),
            P("ch"),
            P("ch", None),
            P("seq", "ch"),
        ),
        out_specs=(P("seq", "ch"), P("seq", "ch"), P("seq", "ch"), P("seq", "ch"), P("ch", "seq")),
        check_vma=False,
    )
```

```python
import jax
import jax.numpy as jnp
from jax import lax
from jax.experimental import pallas as pl
from jax.experimental.pallas import tpu as pltpu
from jax.sharding import PartitionSpec as P

L = 512
D = 1024
W = 512
HEADS = 8
HEAD = 64
NS = 16
Q = 256
CHUNKS = L // Q
BLOCKS = D // Q
PEERS = 16
ROWS = 32
F32 = jnp.float32
BF16 = jnp.bfloat16
MESH = pl.DeviceIdType.MESH

LAST = (((1,), (1,)), ((), ()))
FIRST = (((0,), (0,)), ((), ()))

SMALL = ((0, 16, 32), (48, 64, 80))

S_COT, S_CORE, S_Y, S_Z = 0, 3, 4, 7
S_MIX, S_IN, S_GCORE, S_GPEER = 10, 16, 22, 25
S_ALL = S_GPEER + 3 * PEERS


def mm(a, b):
    return jnp.dot(a, b, preferred_element_type=F32)


def mm_t(a, b):
    return lax.dot_general(a, b, LAST, preferred_element_type=F32)


def t_mm(a, b):
    return lax.dot_general(a, b, FIRST, preferred_element_type=F32)


def split2(v):
    high = v.astype(BF16)
    return high, (v - high.astype(F32)).astype(BF16)


def split3(v):
    high = v.astype(BF16)
    rest = v - high.astype(F32)
    mid = rest.astype(BF16)
    return high, mid, (rest - mid.astype(F32)).astype(BF16)


def iota(shape, dim):
    return lax.broadcasted_iota(jnp.int32, shape, dim)


def anti_identity():
    return jnp.where(iota((Q, Q), 0) + iota((Q, Q), 1) == Q - 1, 1.0, 0.0).astype(BF16)


def spread_matrix():
    return jnp.where(iota((HEADS, W), 1) // HEAD == iota((HEADS, W), 0), 1.0, 0.0).astype(BF16)


def spread(v, e):
    high, low = split2(v)
    return mm(high, e) + mm(low, e)


def gather_heads(v, e):
    high, low = split2(v)
    return mm_t(high, e) + mm_t(low, e)


def order(sign):
    return (iota((Q, Q), 0) - iota((Q, Q), 1)) * sign >= 0


def running(v, mask):
    ones = jnp.where(mask, 1.0, 0.0).astype(BF16)
    return sum(mm(ones, part) for part in split3(v))


def softplus(v):
    return jnp.maximum(v, 0.0) + jnp.log1p(jnp.exp(-jnp.abs(v)))


def sigmoid(v):
    return 1.0 / (1.0 + jnp.exp(-v))


def rows_of(k):
    return pl.ds(pl.multiple_of(k * Q, Q), Q)


def block_kernel(
    hidden, proj_x, proj_z, proj_b, proj_c, proj_dt, bias, rate, skip, proj_out, cotangent,
    block_out, grad_hidden, grad_x, grad_z, grad_out,
    px_flip, pz_flip, po_flip, small, hidden_flip, cot, cot_flip,
    xs, zs, bs, cs, dts, dos, cums, dts_soft, e_cums, e_rests, dt_wides, dyb, xdt, zacc,
    yi, gi, dcs, dbs, ext, os, dxs, dzs,
    chunk_state, chunk_grad, chunk_decay, chunk_dot,
    msg, msg_core, ybuf, zbuf, pair_msg, y_msg,
    mix_own, mix_send, mix_recv, in_own, in_send, in_recv,
    g_own, g_send, g_recv, h_own, h_send, h_recv,
    send_sem, recv_sem,
):
    seq, ch = lax.axis_index("seq"), lax.axis_index("ch")
    core, y, z = lax.rem(seq, 2), lax.rem(seq // 2, 4), seq // 8
    other = 1 - core

    def x_peer(k):
        return (seq, lax.rem(ch + k, 4))

    def zy_peer(dz, dy):
        return (lax.rem(z + dz, 4) * 8 + lax.rem(y + dy, 4) * 2 + core, ch)

    core_peer = (seq + 1 - 2 * core, ch)
    shifts = [(k // 4, k % 4) for k in range(1, PEERS)]

    def remote(src, dst, sem, device):
        return pltpu.make_async_remote_copy(
            src_ref=src,
            dst_ref=dst,
            send_sem=send_sem.at[sem],
            recv_sem=recv_sem.at[sem],
            device_id=device,
            device_id_type=MESH,
        )

    barrier = pltpu.get_barrier_semaphore()
    for device in (
        [x_peer(k) for k in range(1, 4)] + [core_peer] + [zy_peer(dz, dy) for dz, dy in shifts]
    ):
        pl.semaphore_signal(barrier, inc=1, device_id=device, device_id_type=MESH)
    pl.semaphore_wait(barrier, 3 + 1 + PEERS - 1)

    def cot_copy(k):
        return remote(cotangent, cot.at[ch], S_COT + k - 1, x_peer(k))

    for k in range(1, 4):
        cot_copy(k).start()
    cot[ch] = cotangent[...]

    anti = anti_identity()
    e = spread_matrix()
    for k in range(BLOCKS):
        here, there = slice(k * Q, (k + 1) * Q), slice(D - (k + 1) * Q, D - k * Q)
        px_flip[here, :] = mm(anti, proj_x[there, :]).astype(BF16)
        pz_flip[here, :] = mm(anti, proj_z[there, :]).astype(BF16)
        po_flip[:, here] = mm(proj_out[:, there], anti).astype(BF16)
        hidden_flip[:, here] = mm(hidden[:, there], anti).astype(BF16)
    small[...] = jnp.zeros_like(small)
    for weight, at in zip((proj_b, proj_c, proj_dt), range(3)):
        n = weight.shape[0]
        small[SMALL[0][at] : SMALL[0][at] + n, :] = weight[...]
        for k in range(BLOCKS):
            here, there = slice(k * Q, (k + 1) * Q), slice(D - (k + 1) * Q, D - k * Q)
            small[SMALL[1][at] : SMALL[1][at] + n, here] = mm(weight[:, there], anti).astype(BF16)

    def project_step(k, carry):
        rows = rows_of(k)
        u = hidden[rows, :]
        xs[0, rows, :] = mm(u, proj_x[...])
        zs[0, rows, :] = mm(u, proj_z[...])
        xs[1, rows, :] = mm(u, px_flip[...])
        zs[1, rows, :] = mm(u, pz_flip[...])
        narrow = mm_t(u, small[...])
        for strand in range(2):
            at_b, at_c, at_dt = SMALL[strand]
            bs[strand, rows, :] = narrow[:, at_b : at_b + NS].astype(BF16)
            cs[strand, rows, :] = narrow[:, at_c : at_c + NS].astype(BF16)
            dts[strand, rows, :] = narrow[:, at_dt : at_dt + HEADS] + bias[...]
        return carry

    lax.fori_loop(0, CHUNKS, project_step, 0)

    for k in range(1, 4):
        cot_copy(k).wait_recv()

    def cot_step(k, carry):
        rows = rows_of(k)
        forward = backward = None
        for b in range(BLOCKS):
            cot_flip[b, rows, :] = mm(cot[BLOCKS - 1 - b, rows, :], anti).astype(BF16)
            columns = slice(b * Q, (b + 1) * Q)
            part = mm_t(cot[b, rows, :], proj_out[:, columns])
            part_flip = mm_t(cot[b, rows, :], po_flip[:, columns])
            forward = part if forward is None else forward + part
            backward = part_flip if backward is None else backward + part_flip
        dos[0, rows, :] = forward.astype(BF16)
        dos[1, rows, :] = backward.astype(BF16)
        return carry

    lax.fori_loop(0, CHUNKS, cot_step, 0)

    def chunk_step(i, carry):
        strand, k = i // CHUNKS, lax.rem(i, CHUNKS)
        rows = rows_of(k)
        dt = softplus(dts[strand, rows, :])
        a = -rate[...] * dt
        cum = running(a, order(1 - 2 * strand))
        total = jnp.sum(a, axis=0, keepdims=True)
        cums[strand, rows, :] = cum
        dts_soft[strand, rows, :] = dt
        e_cum = spread(jnp.exp(cum), e)
        e_rest = spread(jnp.exp(total - cum), e)
        dt_wide = spread(dt, e)
        e_cums[strand, rows, :] = e_cum
        e_rests[strand, rows, :] = e_rest
        dt_wides[strand, rows, :] = dt_wide
        gate = zs[strand, rows, :]
        dy = dos[strand, rows, :].astype(F32) * (gate * sigmoid(gate))
        xd = xs[strand, rows, :] * dt_wide
        dyb[strand, rows, :] = dy.astype(BF16)
        xdt[strand, rows, :] = xd.astype(BF16)
        chunk_state[strand, k] = t_mm(bs[strand, rows, :], (xd * e_rest).astype(BF16))
        chunk_grad[strand, k] = t_mm(cs[strand, rows, :], (dy * e_cum).astype(BF16))
        chunk_decay[strand, k] = jnp.broadcast_to(jnp.exp(spread(total, e)), (8, W))
        return carry

    lax.fori_loop(0, 2 * CHUNKS, chunk_step, 0)

    for strand in range(2):
        times = list(range(CHUNKS)) if strand == 0 else list(range(CHUNKS))[::-1]
        state = chunk_state[strand, times[0]]
        grad = chunk_grad[strand, times[-1]]
        decay = chunk_decay[strand, 0]
        for k in times[1:]:
            state = chunk_decay[strand, k, 0:1, :] * state + chunk_state[strand, k]
        for k in times[::-1][1:]:
            grad = chunk_decay[strand, k, 0:1, :] * grad + chunk_grad[strand, k]
        for k in range(1, CHUNKS):
            decay = decay * chunk_decay[strand, k]
        at = 32 * strand
        msg[at : at + NS, :] = state
        msg[48 - at : 48 - at + NS, :] = grad
        if strand == 0:
            decay_f = decay
        else:
            msg[64:72, :] = jnp.where(iota((8, W), 0) == 0, decay_f, decay)

    def pieces(ref):
        return (
            ref[0:16, :], ref[16:32, :], ref[32:48, :], ref[48:64, :], ref[64:65, :], ref[65:66, :]
        )

    def rising(acc, part):
        return acc[0] * part[4] + part[0], acc[1] * part[5] + part[1]

    def falling(acc, part):
        return acc[0] * part[5] + part[2], acc[1] * part[4] + part[3]

    def pick(flag, new, old):
        return tuple(jnp.where(flag, n, o) for n, o in zip(new, old))

    def store_message(dst, up, down, decay_f, decay_r):
        dst[0:16, :], dst[16:32, :] = up
        dst[32:48, :], dst[48:64, :] = down
        dst[64:72, :] = jnp.where(
            iota((8, W), 0) == 0,
            jnp.broadcast_to(decay_f, (8, W)),
            jnp.broadcast_to(decay_r, (8, W)),
        )

    zero = jnp.zeros((NS, W), F32)

    def core_copy():
        return remote(msg, msg_core, S_CORE, core_peer)

    def y_copy(k):
        return remote(pair_msg, ybuf.at[y], S_Y + k - 1, zy_peer(0, k))

    def z_copy(k):
        return remote(y_msg, zbuf.at[z], S_Z + k - 1, zy_peer(k, 0))

    core_copy().start()

    def pair_stage():
        core_copy().wait_recv()
        mine, theirs = pieces(msg), pieces(msg_core)
        first, second = pick(core == 0, mine, theirs), pick(core == 0, theirs, mine)
        up = rising(first[:2], second)
        down = falling(second[2:4], first)
        decay_f, decay_r = first[4] * second[4], first[5] * second[5]
        store_message(pair_msg, up, down, decay_f, decay_r)
        store_message(ybuf.at[y], up, down, decay_f, decay_r)
        for k in range(1, 4):
            y_copy(k).start()

    def y_stage():
        for k in range(1, 4):
            y_copy(k).wait_recv()
        up = down = (zero, zero)
        decay_f = decay_r = jnp.ones((1, W), F32)
        for j in range(4):
            part = pieces(ybuf.at[j])
            up = rising(up, part)
            down = falling(down, pieces(ybuf.at[3 - j]))
            decay_f, decay_r = decay_f * part[4], decay_r * part[5]
        store_message(y_msg, up, down, decay_f, decay_r)
        store_message(zbuf.at[z], up, down, decay_f, decay_r)
        for k in range(1, 4):
            z_copy(k).start()

    def inner_step(i, carry):
        strand, k = i // CHUNKS, lax.rem(i, CHUNKS)
        rows = rows_of(k)
        mask = order(1 - 2 * strand)
        cum = cums[strand, rows, :]
        cum_t = cum.T
        b = bs[strand, rows, :]
        c = cs[strand, rows, :]
        scores = mm_t(c, b)
        lane = iota((Q, 128), 1)
        for pair in range(HEADS // 2):
            columns = slice(pair * 128, (pair + 1) * 128)
            x_pair, dy_pair = xdt[strand, rows, columns], dyb[strand, rows, columns]
            y_sum = g_sum = None
            for half in range(2):
                h = 2 * pair + half
                own = (lane >= HEAD) if half else (lane < HEAD)
                x_own = jnp.where(own, x_pair, jnp.zeros((), BF16))
                dy_own = jnp.where(own, dy_pair, jnp.zeros((), BF16))
                decay = jnp.exp(
                    jnp.where(mask, cum[:, h : h + 1] - cum_t[h : h + 1, :], -1e30)
                )
                cross = mm_t(dy_own, x_pair)
                mixing = (decay * scores).astype(BF16)
                if h == 0:
                    zacc[...] = decay * cross
                else:
                    zacc[...] += decay * cross
                y_new, g_new = mm(mixing, x_own), t_mm(mixing, dy_own)
                y_sum, g_sum = (
                    (y_new, g_new) if y_sum is None else (y_sum + y_new, g_sum + g_new)
                )
            yi[strand, rows, columns] = y_sum
            gi[strand, rows, columns] = g_sum
        both = zacc[...].astype(BF16)
        dcs[strand, rows, :] = mm(both, b)
        dbs[strand, rows, :] = t_mm(both, c)

        @pl.when(i == 0)
        def _():
            pair_stage()

        @pl.when(i == 1)
        def _():
            y_stage()

        return carry

    lax.fori_loop(0, 2 * CHUNKS, inner_step, 0)

    for k in range(1, 4):
        z_copy(k).wait_recv()
    up = down = (zero, zero)
    for buffer, at in ((zbuf, z), (ybuf, y)):
        for j in range(4):
            up = pick(j < at, rising(up, pieces(buffer.at[j])), up)
            down = pick(3 - j > at, falling(down, pieces(buffer.at[3 - j])), down)
    theirs = pieces(msg_core)
    up = pick(core == 1, rising(up, theirs), up)
    down = pick(core == 0, falling(down, theirs), down)

    for strand, (state, grad) in enumerate(((up[0], down[1]), (down[0], up[1]))):
        times = list(range(CHUNKS)) if strand == 0 else list(range(CHUNKS))[::-1]
        entering, leaving, leaving_grad = {}, {}, {}
        for k in times:
            entering[k] = state
            state = chunk_decay[strand, k, 0:1, :] * state + chunk_state[strand, k]
            leaving[k] = state
        for k in times[::-1]:
            leaving_grad[k] = grad
            grad = chunk_decay[strand, k, 0:1, :] * grad + chunk_grad[strand, k]
        for k in range(CHUNKS):
            chunk_state[strand, k] = entering[k]
            chunk_grad[strand, k] = leaving_grad[k]
            chunk_dot[strand, k] = jnp.broadcast_to(
                jnp.sum(leaving[k] * leaving_grad[k], axis=0, keepdims=True), (8, W)
            )

    skip_wide = spread(skip[...], e)
    ext[...] = jnp.zeros_like(ext)

    def mix_copy(k, j):
        rows = rows_of(k)
        return remote(
            mix_send.at[lax.rem(ch + j, 4), rows], mix_recv.at[j - 1, rows],
            S_MIX + 3 * k + j - 1, x_peer(j),
        )

    def in_copy(k, j):
        rows = rows_of(k)
        return remote(
            in_send.at[lax.rem(ch + j, 4), rows], in_recv.at[j - 1, rows],
            S_IN + 3 * k + j - 1, x_peer(j),
        )

    def keep(own, b, rows, part):
        @pl.when(ch == b)
        def _():
            own[rows, :] = part

    def outer_step(k, carry):
        rows = rows_of(k)
        for strand in range(2):
            raw = dts[strand, rows, :]
            dt = dts_soft[strand, rows, :]
            e_cum = e_cums[strand, rows, :]
            e_rest = e_rests[strand, rows, :]
            dt_wide = dt_wides[strand, rows, :]
            state = chunk_state[strand, k].astype(BF16)
            grad = chunk_grad[strand, k].astype(BF16)
            x = xs[strand, rows, :]
            gate = zs[strand, rows, :]
            d_o = dos[strand, rows, :].astype(F32)
            sig = sigmoid(gate)
            silu = gate * sig
            dy = d_o * silu
            y_part = yi[strand, rows, :] + e_cum * mm(cs[strand, rows, :], state)
            gb = gi[strand, rows, :] + e_rest * mm(bs[strand, rows, :], grad)
            out = y_part + skip_wide * x
            os[strand, rows, :] = (out * silu).astype(BF16)
            dzs[strand, rows, :] = (d_o * out * (sig + silu * (1.0 - sig))).astype(BF16)
            dxs[strand, rows, :] = (dt_wide * gb + skip_wide * dy).astype(BF16)
            d_c = dcs[strand, rows, :] + mm_t((dy * e_cum).astype(BF16), state)
            d_b = dbs[strand, rows, :] + mm_t((x * dt_wide * e_rest).astype(BF16), grad)
            direct = gather_heads(x * gb, e)
            d_cum = gather_heads(dy * y_part, e) - dt * direct
            d_a = running(d_cum, order(2 * strand - 1)) + gather_heads(chunk_dot[strand, k], e)[0:1, :]
            d_raw = (direct - rate[...] * d_a) * sigmoid(raw)
            at_b, at_c, at_dt = SMALL[strand]
            ext[rows, at_b : at_b + NS] = d_b.astype(BF16)
            ext[rows, at_c : at_c + NS] = d_c.astype(BF16)
            ext[rows, at_dt : at_dt + HEADS] = d_raw.astype(BF16)
        for b in range(BLOCKS):
            columns = slice(b * Q, (b + 1) * Q)
            part = mm(os[0, rows, :], proj_out[:, columns]) + mm(os[1, rows, :], po_flip[:, columns])
            keep(mix_own, b, rows, part)
            mix_send[b, rows, :] = part.astype(BF16)
        for j in range(1, 4):
            mix_copy(k, j).start()
        for b in range(BLOCKS):
            columns = slice(b * Q, (b + 1) * Q)
            part = (
                mm_t(dxs[0, rows, :], proj_x[columns, :])
                + mm_t(dzs[0, rows, :], proj_z[columns, :])
                + mm_t(dxs[1, rows, :], px_flip[columns, :])
                + mm_t(dzs[1, rows, :], pz_flip[columns, :])
                + mm(ext[rows, :], small[:, columns])
            )
            keep(in_own, b, rows, part)
            in_send[b, rows, :] = part.astype(BF16)
        for j in range(1, 4):
            in_copy(k, j).start()
        return carry

    lax.fori_loop(0, CHUNKS, outer_step, 0)

    def g_core_copy(n):
        return remote(g_send.at[n, :, other], g_recv.at[n], S_GCORE + n, core_peer)

    def g_peer_copy(n, dz, dy):
        to = lax.rem(z + dz, 4) * 4 + lax.rem(y + dy, 4)
        at = 4 * dz + dy
        return remote(
            h_send.at[n, to], h_recv.at[n, at], S_GPEER + PEERS * n + at, zy_peer(dz, dy)
        )

    def weight_part(n, left, left_flip, right):
        def step(b, carry):
            value = t_mm(left(b), right[0]) + t_mm(left_flip(b), right[1])
            g_own[n, pl.ds(pl.multiple_of(b * 4, 4), 4)] = value.reshape(4, 2, ROWS, W)
            g_send[n, pl.ds(pl.multiple_of(b * 4, 4), 4)] = value.astype(BF16).reshape(
                4, 2, ROWS, W
            )
            return carry

        lax.fori_loop(0, BLOCKS, step, 0)
        g_core_copy(n).start()

    weight_part(0, lambda b: cot[b], lambda b: cot_flip[b], os)
    weight_part(1, lambda b: hidden[:, rows_of(b)], lambda b: hidden_flip[:, rows_of(b)], dzs)
    weight_part(2, lambda b: hidden[:, rows_of(b)], lambda b: hidden_flip[:, rows_of(b)], dxs)

    for n in range(3):
        g_core_copy(n).wait_recv()

        def pair_sum(i, carry):
            value = g_own[n, i, core] + g_recv[n, i].astype(F32)
            h_send[n, i] = value.astype(BF16)
            return carry

        lax.fori_loop(0, PEERS, pair_sum, 0)
        at = z * 4 + y
        h_own[n] = g_own[n, at, core] + g_recv[n, at].astype(F32)
        for dz, dy in shifts:
            g_peer_copy(n, dz, dy).start()

    def finish_step(k, carry):
        rows = rows_of(k)
        for j in range(1, 4):
            mix_copy(k, j).wait_recv()
        mine = hidden[rows, pl.ds(pl.multiple_of(ch * Q, Q), Q)].astype(F32)
        total = mine + mix_own[rows, :]
        for j in range(3):
            total = total + mix_recv[j, rows, :].astype(F32)
        block_out[rows, :] = total.astype(BF16)
        for j in range(1, 4):
            in_copy(k, j).wait_recv()
        total = cotangent[rows, :].astype(F32) + in_own[rows, :]
        for j in range(3):
            total = total + in_recv[j, rows, :].astype(F32)
        grad_hidden[rows, :] = total
        return carry

    lax.fori_loop(0, CHUNKS, finish_step, 0)

    for n, out in enumerate((grad_out, grad_z, grad_x)):
        total = h_own[n]
        for dz, dy in shifts:
            g_peer_copy(n, dz, dy).wait_recv()
            total = total + h_recv[n, 4 * dz + dy].astype(F32)
        out[...] = total

    for k in range(1, 4):
        cot_copy(k).wait_send()
        y_copy(k).wait_send()
        z_copy(k).wait_send()
    core_copy().wait_send()
    for k in range(CHUNKS):
        for j in range(1, 4):
            mix_copy(k, j).wait_send()
            in_copy(k, j).wait_send()
    for n in range(3):
        g_core_copy(n).wait_send()
        for dz, dy in shifts:
            g_peer_copy(n, dz, dy).wait_send()


def shape(*dims, dtype=F32):
    return jax.ShapeDtypeStruct(dims, dtype)


VMEM = pl.BlockSpec(memory_space=pltpu.VMEM)


def body(
    hidden, proj_x, proj_z, proj_b, proj_c, proj_dt, dt_bias, decay_rate, skip_gain, proj_out, cotangent
):
    bias, rate, skip = (v[None, :] for v in (dt_bias, decay_rate, skip_gain))
    vm = pltpu.VMEM
    block_out, grad_hidden, grad_x, grad_z, grad_out = pl.pallas_call(
        block_kernel,
        out_shape=(
            shape(L, Q, dtype=BF16),
            shape(L, Q),
            shape(ROWS, W),
            shape(ROWS, W),
            shape(ROWS, W),
        ),
        in_specs=[VMEM] * 11,
        out_specs=[VMEM] * 5,
        scratch_shapes=[
            vm((D, W), BF16), vm((D, W), BF16), vm((W, D), BF16), vm((128, D), BF16),
            vm((L, D), BF16), vm((BLOCKS, L, Q), BF16), vm((BLOCKS, L, Q), BF16),
            vm((2, L, W), F32), vm((2, L, W), F32), vm((2, L, NS), BF16), vm((2, L, NS), BF16),
            vm((2, L, HEADS), F32), vm((2, L, W), BF16), vm((2, L, HEADS), F32),
            vm((2, L, HEADS), F32), vm((2, L, W), F32), vm((2, L, W), F32), vm((2, L, W), F32),
            vm((2, L, W), BF16), vm((2, L, W), BF16), vm((Q, Q), F32),
            vm((2, L, W), F32), vm((2, L, W), F32), vm((2, L, NS), F32), vm((2, L, NS), F32),
            vm((L, 128), BF16), vm((2, L, W), BF16), vm((2, L, W), BF16), vm((2, L, W), BF16),
            vm((2, CHUNKS, NS, W), F32), vm((2, CHUNKS, NS, W), F32),
            vm((2, CHUNKS, 8, W), F32), vm((2, CHUNKS, 8, W), F32),
            vm((72, W), F32), vm((72, W), F32), vm((4, 72, W), F32), vm((4, 72, W), F32),
            vm((72, W), F32), vm((72, W), F32),
            vm((L, Q), F32), vm((BLOCKS, L, Q), BF16), vm((3, L, Q), BF16),
            vm((L, Q), F32), vm((BLOCKS, L, Q), BF16), vm((3, L, Q), BF16),
            vm((3, PEERS, 2, ROWS, W), F32), vm((3, PEERS, 2, ROWS, W), BF16),
            vm((3, PEERS, ROWS, W), BF16),
            vm((3, ROWS, W), F32), vm((3, PEERS, ROWS, W), BF16),
            vm((3, PEERS, ROWS, W), BF16),
            pltpu.SemaphoreType.DMA((S_ALL,)), pltpu.SemaphoreType.DMA((S_ALL,)),
        ],
        compiler_params=pltpu.CompilerParams(
            vmem_limit_bytes=60 * 2**20, collective_id=0, has_side_effects=True
        ),
        name="block",
    )(
        hidden, proj_x, proj_z, proj_b.T, proj_c.T, proj_dt.T, bias, rate, skip, proj_out, cotangent
    )
    return block_out, grad_hidden, grad_x, grad_z, grad_out.T


def solution(mesh):
    return jax.shard_map(
        body,
        mesh=mesh,
        in_specs=(
            P("seq", None),
            P(None, "ch"),
            P(None, "ch"),
            P(),
            P(),
            P(None, "ch"),
            P("ch"),
            P("ch"),
            P("ch"),
            P("ch", None),
            P("seq", "ch"),
        ),
        out_specs=(P("seq", "ch"), P("seq", "ch"), P("seq", "ch"), P("seq", "ch"), P("ch", "seq")),
        check_vma=False,
    )
```

```python
import jax
import jax.numpy as jnp
from jax import lax
from jax.experimental import pallas as pl
from jax.experimental.pallas import tpu as pltpu
from jax.sharding import PartitionSpec as P

L = 512
D = 1024
W = 512
HEADS = 8
HEAD = 64
NS = 16
Q = 256
CHUNKS = L // Q
BLOCKS = D // Q
PEERS = 16
ROWS = 32
F32 = jnp.float32
BF16 = jnp.bfloat16
MESH = pl.DeviceIdType.MESH

LAST = (((1,), (1,)), ((), ()))
FIRST = (((0,), (0,)), ((), ()))

SMALL = ((0, 16, 32), (48, 64, 80))

S_COT, S_MIX, S_IN, S_A, S_B = 0, 6, 12, 18, 36
S_GCORE, S_GPEER = 54, 57
S_ALL = S_GPEER + 3 * 16


def mm(a, b):
    return jnp.dot(a, b, preferred_element_type=F32)


def mm_t(a, b):
    return lax.dot_general(a, b, LAST, preferred_element_type=F32)


def t_mm(a, b):
    return lax.dot_general(a, b, FIRST, preferred_element_type=F32)


def split2(v):
    high = v.astype(BF16)
    return high, (v - high.astype(F32)).astype(BF16)


def split3(v):
    high = v.astype(BF16)
    rest = v - high.astype(F32)
    mid = rest.astype(BF16)
    return high, mid, (rest - mid.astype(F32)).astype(BF16)


def iota(shape, dim):
    return lax.broadcasted_iota(jnp.int32, shape, dim)


def anti_identity():
    return jnp.where(iota((Q, Q), 0) + iota((Q, Q), 1) == Q - 1, 1.0, 0.0).astype(BF16)


def spread_matrix():
    return jnp.where(iota((HEADS, W), 1) // HEAD == iota((HEADS, W), 0), 1.0, 0.0).astype(BF16)


def spread(v, e):
    high, low = split2(v)
    return mm(high, e) + mm(low, e)


def gather_heads(v, e):
    high, low = split2(v)
    return mm_t(high, e) + mm_t(low, e)


def order(sign):
    return (iota((Q, Q), 0) - iota((Q, Q), 1)) * sign >= 0


def running(v, mask):
    ones = jnp.where(mask, 1.0, 0.0).astype(BF16)
    return sum(mm(ones, part) for part in split3(v))


def softplus(v):
    return jnp.maximum(v, 0.0) + jnp.log1p(jnp.exp(-jnp.abs(v)))


def sigmoid(v):
    return 1.0 / (1.0 + jnp.exp(-v))


def rows_of(k):
    return pl.ds(pl.multiple_of(k * Q, Q), Q)


def block_kernel(
    hidden_hbm, proj_x_hbm, proj_z_hbm, proj_out_hbm, cot_hbm,
    proj_b, proj_c, proj_dt, bias, rate, skip,
    block_out, grad_hidden, grad_x, grad_z, grad_out,
    hidden, proj_x, proj_z, proj_out,
    px_flip, pz_flip, po_flip, small, hidden_flip, cot, cot_flip,
    xs, zs, bs, cs, dts, dos, cums, dts_soft, e_cums, e_rests, dt_wides, dyb, xdt, zacc,
    yi, gi, dcs, dbs, dyy, ext, os, dxs, dzs,
    chunk_state, chunk_grad, chunk_decay, chunk_dot,
    a_msg, a_core, a_pair, a_slots, a_back, a_in,
    b_msg, b_core, b_pair, b_slots, b_back, b_in,
    mix_own, mix_part, mix_send, mix_fwd, mix_recv,
    in_own, in_part, in_send, in_fwd, in_recv,
    g_own, g_send, g_recv, h_own, h_send, h_recv,
    load_sem, send_sem, recv_sem,
):
    seq, ch = lax.axis_index("seq"), lax.axis_index("ch")
    core, y, z = lax.rem(seq, 2), lax.rem(seq // 2, 4), seq // 8
    other = 1 - core
    place = z * 4 + y

    def x_peer(k):
        return (seq, lax.rem(ch + k, 4))

    def zy_peer(dz, dy):
        return (lax.rem(z + dz, 4) * 8 + lax.rem(y + dy, 4) * 2 + core, ch)

    core_peer = (seq + 1 - 2 * core, ch)
    shifts = [(k // 4, k % 4) for k in range(1, PEERS)]

    def remote(src, dst, sem, device):
        return pltpu.make_async_remote_copy(
            src_ref=src,
            dst_ref=dst,
            send_sem=send_sem.at[sem],
            recv_sem=recv_sem.at[sem],
            device_id=device,
            device_id_type=MESH,
        )

    barrier = pltpu.get_barrier_semaphore()
    for device in [x_peer(1), x_peer(3), core_peer] + [zy_peer(dz, dy) for dz, dy in shifts]:
        pl.semaphore_signal(barrier, inc=1, device_id=device, device_id_type=MESH)

    loads = [
        pltpu.make_async_copy(src, dst, load_sem.at[n])
        for n, (src, dst) in enumerate(
            (
                (cot_hbm, cot.at[ch]),
                (hidden_hbm, hidden),
                (proj_x_hbm, proj_x),
                (proj_z_hbm, proj_z),
                (proj_out_hbm, proj_out),
            )
        )
    ]
    for load in loads:
        load.start()
    anti = anti_identity()
    e = spread_matrix()
    small[...] = jnp.zeros_like(small)
    for weight, at in zip((proj_b, proj_c, proj_dt), range(3)):
        n = weight.shape[0]
        small[SMALL[0][at] : SMALL[0][at] + n, :] = weight[...]
        for k in range(BLOCKS):
            here, there = slice(k * Q, (k + 1) * Q), slice(D - (k + 1) * Q, D - k * Q)
            small[SMALL[1][at] : SMALL[1][at] + n, here] = mm(weight[:, there], anti).astype(BF16)
    loads[0].wait()
    pl.semaphore_wait(barrier, 2 + 1 + PEERS - 1)

    half = [slice(0, Q), slice(Q, L)]
    before, after = lax.rem(ch + 3, 4), lax.rem(ch + 1, 4)

    def cot_copy(n):
        block, rows, to = (
            (ch, half[0], 1), (ch, half[1], 3), (ch, half[1], 1), (ch, half[0], 3),
            (before, half[0], 1), (after, half[1], 3),
        )[n]
        return remote(cot.at[block, rows], cot.at[block, rows], S_COT + n, x_peer(to))

    for n in range(4):
        cot_copy(n).start()

    loads[1].wait()
    loads[2].wait()
    loads[3].wait()
    for k in range(BLOCKS):
        here, there = slice(k * Q, (k + 1) * Q), slice(D - (k + 1) * Q, D - k * Q)
        px_flip[here, :] = mm(anti, proj_x[there, :]).astype(BF16)
        pz_flip[here, :] = mm(anti, proj_z[there, :]).astype(BF16)
        hidden_flip[:, here] = mm(hidden[:, there], anti).astype(BF16)

    def project_step(k, carry):
        rows = rows_of(k)
        u = hidden[rows, :]
        xs[0, rows, :] = mm(u, proj_x[...])
        zs[0, rows, :] = mm(u, proj_z[...])
        xs[1, rows, :] = mm(u, px_flip[...])
        zs[1, rows, :] = mm(u, pz_flip[...])
        narrow = mm_t(u, small[...])
        for strand in range(2):
            at_b, at_c, at_dt = SMALL[strand]
            bs[strand, rows, :] = narrow[:, at_b : at_b + NS].astype(BF16)
            cs[strand, rows, :] = narrow[:, at_c : at_c + NS].astype(BF16)
            dts[strand, rows, :] = narrow[:, at_dt : at_dt + HEADS] + bias[...]
        return carry

    lax.fori_loop(0, CHUNKS, project_step, 0)

    for n in range(2):
        cot_copy(n).wait_recv()
        cot_copy(4 + n).start()

    def state_step(i, carry):
        strand, k = i // CHUNKS, lax.rem(i, CHUNKS)
        rows = rows_of(k)
        dt = softplus(dts[strand, rows, :])
        a = -rate[...] * dt
        cum = running(a, order(1 - 2 * strand))
        total = jnp.sum(a, axis=0, keepdims=True)
        cums[strand, rows, :] = cum
        dts_soft[strand, rows, :] = dt
        e_rest = spread(jnp.exp(total - cum), e)
        dt_wide = spread(dt, e)
        e_cums[strand, rows, :] = spread(jnp.exp(cum), e)
        e_rests[strand, rows, :] = e_rest
        dt_wides[strand, rows, :] = dt_wide
        xd = xs[strand, rows, :] * dt_wide
        xdt[strand, rows, :] = xd.astype(BF16)
        chunk_state[strand, k] = t_mm(bs[strand, rows, :], (xd * e_rest).astype(BF16))
        chunk_decay[strand, k] = jnp.broadcast_to(jnp.exp(spread(total, e)), (8, W))
        return carry

    lax.fori_loop(0, 2 * CHUNKS, state_step, 0)

    def times(strand):
        return list(range(CHUNKS)) if strand == 0 else list(range(CHUNKS))[::-1]

    def two_halves(dst, rows, value):
        dst[0, rows, :] = value[:, 0:Q]
        dst[1, rows, :] = value[:, Q:]

    decays = []
    for strand in range(2):
        state, decay = chunk_state[strand, times(strand)[0]], chunk_decay[strand, 0]
        for k in times(strand)[1:]:
            state = chunk_decay[strand, k, 0:1, :] * state + chunk_state[strand, k]
        for k in range(1, CHUNKS):
            decay = decay * chunk_decay[strand, k]
        two_halves(a_msg, slice(16 * strand, 16 * strand + NS), state)
        decays.append(decay)
    two_halves(a_msg, slice(32, 40), jnp.where(iota((8, W), 0) == 0, decays[0], decays[1]))

    zero = jnp.zeros((NS, Q), F32)
    a_slots[place] = jnp.zeros_like(a_slots[0])
    b_slots[place] = jnp.zeros_like(b_slots[0])

    class Exchange:
        def __init__(self, base, msg, from_core, pair, slots, back, result, swap):
            self.base, self.msg, self.from_core, self.pair = base, msg, from_core, pair
            self.slots, self.back, self.result, self.swap = slots, back, result, swap

        def to_core(self):
            return remote(self.msg.at[other], self.from_core, self.base, core_peer)

        def to_place(self, dz, dy):
            to = lax.rem(z + dz, 4) * 4 + lax.rem(y + dy, 4)
            kind = jnp.where(to > place, 0, 1)
            return remote(
                self.pair.at[kind], self.slots.at[place], self.base + 4 * dz + dy, zy_peer(dz, dy)
            )

        def to_back(self):
            return remote(self.back, self.result.at[core], self.base + PEERS, core_peer)

        def decay(self, ref, strand):
            return ref[strand : strand + 1, :]

        def both(self):
            mine = (
                self.msg[core, 0:16, :], self.msg[core, 16:32, :],
                a_msg[core, 32 + self.swap : 33 + self.swap, :],
                a_msg[core, 33 - self.swap : 34 - self.swap, :],
            )
            theirs = (
                self.from_core[0:16, :], self.from_core[16:32, :],
                a_core[32 + self.swap : 33 + self.swap, :],
                a_core[33 - self.swap : 34 - self.swap, :],
            )
            return mine, theirs

        def spread_out(self):
            self.to_core().wait_recv()
            mine, theirs = self.both()
            first = [jnp.where(core == 0, m, t) for m, t in zip(mine, theirs)]
            second = [jnp.where(core == 0, t, m) for m, t in zip(mine, theirs)]
            up = second[2] * first[0] + second[0]
            down = first[3] * second[1] + first[1]
            self.pair[0, 0:16, :] = up
            self.pair[1, 0:16, :] = down
            if not self.swap:
                product = jnp.where(
                    iota((8, Q), 0) == 0,
                    jnp.broadcast_to(first[2] * second[2], (8, Q)),
                    jnp.broadcast_to(first[3] * second[3], (8, Q)),
                )
                self.pair[0, 16:24, :] = product
                self.pair[1, 16:24, :] = product
            for dz, dy in shifts:
                self.to_place(dz, dy).start()

        def collect(self):
            for dz, dy in shifts:
                self.to_place(dz, dy).wait_recv()
            up = down = zero
            for j in range(PEERS):
                r = PEERS - 1 - j
                decay_up = a_slots[j, 16 + self.swap : 17 + self.swap, :]
                decay_down = a_slots[r, 17 - self.swap : 18 - self.swap, :]
                up = jnp.where(j < place, decay_up * up + self.slots[j, 0:16, :], up)
                down = jnp.where(r > place, decay_down * down + self.slots[r, 0:16, :], down)
            mine, theirs = self.both()
            self.back[0:16, :] = jnp.where(core == 0, mine[2] * up + mine[0], up)
            self.back[16:32, :] = jnp.where(core == 1, mine[3] * down + mine[1], down)
            self.to_back().start()
            self.result[core, 0:16, :] = jnp.where(core == 1, theirs[2] * up + theirs[0], up)
            self.result[core, 16:32, :] = jnp.where(core == 0, theirs[3] * down + theirs[1], down)

        def take(self):
            self.to_back().wait_recv()
            return [
                jnp.concatenate([self.result[0, rows, :], self.result[1, rows, :]], axis=1)
                for rows in (slice(0, 16), slice(16, 32))
            ]

        def drain(self):
            self.to_core().wait_send()
            self.to_back().wait_send()
            for dz, dy in shifts:
                self.to_place(dz, dy).wait_send()

    round_a = Exchange(S_A, a_msg, a_core, a_pair, a_slots, a_back, a_in, 0)
    round_b = Exchange(S_B, b_msg, b_core, b_pair, b_slots, b_back, b_in, 1)
    round_a.to_core().start()

    lane = iota((Q, 128), 1)

    def within_step(i, carry):
        strand, k = i // CHUNKS, lax.rem(i, CHUNKS)
        rows = rows_of(k)
        mask = order(1 - 2 * strand)
        cum = cums[strand, rows, :]
        cum_t = cum.T
        scores = mm_t(cs[strand, rows, :], bs[strand, rows, :])
        for pair in range(HEADS // 2):
            columns = slice(pair * 128, (pair + 1) * 128)
            x_pair = xdt[strand, rows, columns]
            y_sum = None
            for odd in range(2):
                h = 2 * pair + odd
                own = (lane >= HEAD) if odd else (lane < HEAD)
                x_own = jnp.where(own, x_pair, jnp.zeros((), BF16))
                decay = jnp.exp(
                    jnp.where(mask, cum[:, h : h + 1] - cum_t[h : h + 1, :], -1e30)
                )
                y_new = mm((decay * scores).astype(BF16), x_own)
                y_sum = y_new if y_sum is None else y_sum + y_new
            yi[strand, rows, columns] = y_sum

        @pl.when(i == 0)
        def _():
            round_a.spread_out()

        return carry

    lax.fori_loop(0, 2 * CHUNKS, within_step, 0)

    loads[4].wait()
    for k in range(BLOCKS):
        here, there = slice(k * Q, (k + 1) * Q), slice(D - (k + 1) * Q, D - k * Q)
        po_flip[:, here] = mm(proj_out[:, there], anti).astype(BF16)
    round_a.collect()

    for n in range(2, 6):
        cot_copy(n).wait_recv()

    def cot_step(k, carry):
        rows = rows_of(k)
        forward = backward = None
        for b in range(BLOCKS):
            cot_flip[b, rows, :] = mm(cot[BLOCKS - 1 - b, rows, :], anti).astype(BF16)
            columns = slice(b * Q, (b + 1) * Q)
            part = mm_t(cot[b, rows, :], proj_out[:, columns])
            part_flip = mm_t(cot[b, rows, :], po_flip[:, columns])
            forward = part if forward is None else forward + part
            backward = part_flip if backward is None else backward + part_flip
        dos[0, rows, :] = forward.astype(BF16)
        dos[1, rows, :] = backward.astype(BF16)
        return carry

    lax.fori_loop(0, CHUNKS, cot_step, 0)

    def grad_step(i, carry):
        strand, k = i // CHUNKS, lax.rem(i, CHUNKS)
        rows = rows_of(k)
        gate = zs[strand, rows, :]
        dy = dos[strand, rows, :].astype(F32) * (gate * sigmoid(gate))
        dyb[strand, rows, :] = dy.astype(BF16)
        chunk_grad[strand, k] = t_mm(
            cs[strand, rows, :], (dy * e_cums[strand, rows, :]).astype(BF16)
        )
        return carry

    lax.fori_loop(0, 2 * CHUNKS, grad_step, 0)

    for strand in range(2):
        falling = times(strand)[::-1]
        grad = chunk_grad[strand, falling[0]]
        for k in falling[1:]:
            grad = chunk_decay[strand, k, 0:1, :] * grad + chunk_grad[strand, k]
        two_halves(b_msg, slice(16 - 16 * strand, 32 - 16 * strand), grad)
    round_b.to_core().start()

    for strand, state in enumerate(round_a.take()):
        for k in times(strand):
            own_state = chunk_state[strand, k]
            chunk_state[strand, k] = state
            state = chunk_decay[strand, k, 0:1, :] * state + own_state
            chunk_dot[strand, k] = state

    skip_wide = spread(skip[...], e)

    def out_step(i, carry):
        strand, k = i // CHUNKS, lax.rem(i, CHUNKS)
        rows = rows_of(k)
        e_cum = e_cums[strand, rows, :]
        state = chunk_state[strand, k].astype(BF16)
        gate = zs[strand, rows, :]
        d_o = dos[strand, rows, :].astype(F32)
        sig = sigmoid(gate)
        silu = gate * sig
        dy = d_o * silu
        y_part = yi[strand, rows, :] + e_cum * mm(cs[strand, rows, :], state)
        out = y_part + skip_wide * xs[strand, rows, :]
        os[strand, rows, :] = (out * silu).astype(BF16)
        dzs[strand, rows, :] = (d_o * out * (sig + silu * (1.0 - sig))).astype(BF16)
        dcs[strand, rows, :] = mm_t((dy * e_cum).astype(BF16), state)
        dyy[strand, rows, :] = gather_heads(dy * y_part, e)
        yi[strand, rows, :] = skip_wide * dy

        @pl.when(i == 1)
        def _():
            round_b.spread_out()

        return carry

    lax.fori_loop(0, 2 * CHUNKS, out_step, 0)

    class ColumnSum:
        def __init__(self, base, compute, own, part, send, forward, recv):
            self.base, self.compute, self.own, self.part = base, compute, own, part
            self.send, self.forward, self.recv = send, forward, recv

        def copy(self, n):
            src, dst, to = (
                (self.send.at[1, half[0]], self.forward.at[0], 1),
                (self.send.at[1, half[1]], self.forward.at[1], 3),
                (self.send.at[0, half[1]], self.recv.at[0, half[1]], 1),
                (self.send.at[2, half[0]], self.recv.at[1, half[0]], 3),
                (self.send.at[0, half[0]], self.recv.at[0, half[0]], 1),
                (self.send.at[2, half[1]], self.recv.at[1, half[1]], 3),
            )[n]
            return remote(src, dst, self.base + n, x_peer(to))

        def columns(self, r):
            return pl.ds(pl.multiple_of(lax.rem(ch + r, 4) * Q, Q), Q)

        def begin(self):
            for n in range(2):
                self.send[1, half[n], :] = self.compute(half[n], self.columns(2)).astype(BF16)
                self.copy(n).start()
            self.send[0, half[1], :] = self.compute(half[1], self.columns(1)).astype(BF16)
            self.copy(2).start()
            self.send[2, half[0], :] = self.compute(half[0], self.columns(3)).astype(BF16)
            self.copy(3).start()
            self.part[0] = self.compute(half[0], self.columns(1))
            self.part[1] = self.compute(half[1], self.columns(3))

        def middle(self):
            for n, block in ((0, 0), (1, 2)):
                self.copy(n).wait_recv()
                self.send[block, half[n], :] = (
                    self.part[n] + self.forward[n].astype(F32)
                ).astype(BF16)
                self.copy(4 + n).start()

        def own_block(self):
            for n in range(2):
                self.own[half[n], :] = self.compute(half[n], self.columns(0))

        def finish(self, rows):
            return (
                self.own[rows, :]
                + self.recv[0, rows, :].astype(F32)
                + self.recv[1, rows, :].astype(F32)
            )

        def arrived(self):
            for n in range(2, 6):
                self.copy(n).wait_recv()

        def drain(self):
            for n in range(6):
                self.copy(n).wait_send()

    def mix_block(rows, columns):
        return mm(os[0, rows, :], proj_out[:, columns]) + mm(os[1, rows, :], po_flip[:, columns])

    def in_block(rows, columns):
        return (
            mm_t(dxs[0, rows, :], proj_x[columns, :])
            + mm_t(dzs[0, rows, :], proj_z[columns, :])
            + mm_t(dxs[1, rows, :], px_flip[columns, :])
            + mm_t(dzs[1, rows, :], pz_flip[columns, :])
            + mm(ext[rows, :], small[:, columns])
        )

    mix_sum = ColumnSum(S_MIX, mix_block, mix_own, mix_part, mix_send, mix_fwd, mix_recv)
    in_sum = ColumnSum(S_IN, in_block, in_own, in_part, in_send, in_fwd, in_recv)
    mix_sum.begin()

    def inner_step(i, carry):
        strand, k = i // CHUNKS, lax.rem(i, CHUNKS)
        rows = rows_of(k)
        mask = order(2 * strand - 1)
        cum = cums[strand, rows, :]
        cum_t = cum.T
        b = bs[strand, rows, :]
        c = cs[strand, rows, :]
        scores = mm_t(b, c)
        for pair in range(HEADS // 2):
            columns = slice(pair * 128, (pair + 1) * 128)
            x_pair, dy_pair = xdt[strand, rows, columns], dyb[strand, rows, columns]
            g_sum = None
            for odd in range(2):
                h = 2 * pair + odd
                own = (lane >= HEAD) if odd else (lane < HEAD)
                dy_own = jnp.where(own, dy_pair, jnp.zeros((), BF16))
                decay = jnp.exp(
                    jnp.where(mask, cum_t[h : h + 1, :] - cum[:, h : h + 1], -1e30)
                )
                cross = mm_t(x_pair, dy_own)
                if h == 0:
                    zacc[...] = decay * cross
                else:
                    zacc[...] += decay * cross
                g_new = mm((decay * scores).astype(BF16), dy_own)
                g_sum = g_new if g_sum is None else g_sum + g_new
            gi[strand, rows, columns] = g_sum
        pairs = zacc[...].astype(BF16)
        dbs[strand, rows, :] = mm(pairs, c)
        dcs[strand, rows, :] += t_mm(pairs, b)

        @pl.when(i == 1)
        def _():
            mix_sum.middle()

        @pl.when(i == 2)
        def _():
            round_b.collect()

        return carry

    lax.fori_loop(0, 2 * CHUNKS, inner_step, 0)

    def g_core_copy(n):
        return remote(g_send.at[n, :, other], g_recv.at[n], S_GCORE + n, core_peer)

    def g_peer_copy(n, dz, dy):
        to = lax.rem(z + dz, 4) * 4 + lax.rem(y + dy, 4)
        at = 4 * dz + dy
        return remote(
            h_send.at[n, to], h_recv.at[n, at], S_GPEER + PEERS * n + at, zy_peer(dz, dy)
        )

    def weight_part(n, left, left_flip, right):
        def step(b, carry):
            value = t_mm(left(b), right[0]) + t_mm(left_flip(b), right[1])
            g_own[n, pl.ds(pl.multiple_of(b * 4, 4), 4)] = value.reshape(4, 2, ROWS, W)
            g_send[n, pl.ds(pl.multiple_of(b * 4, 4), 4)] = value.astype(BF16).reshape(
                4, 2, ROWS, W
            )
            return carry

        lax.fori_loop(0, BLOCKS, step, 0)
        g_core_copy(n).start()

    def weight_pair(n):
        g_core_copy(n).wait_recv()

        def pair_sum(i, carry):
            value = g_own[n, i, core] + g_recv[n, i].astype(F32)
            h_send[n, i] = value.astype(BF16)
            return carry

        lax.fori_loop(0, PEERS, pair_sum, 0)
        h_own[n] = g_own[n, place, core] + g_recv[n, place].astype(F32)
        for dz, dy in shifts:
            g_peer_copy(n, dz, dy).start()

    weight_part(0, lambda b: cot[b], lambda b: cot_flip[b], os)
    weight_part(1, lambda b: hidden[:, rows_of(b)], lambda b: hidden_flip[:, rows_of(b)], dzs)
    mix_sum.own_block()
    weight_pair(0)

    up, down = round_b.take()
    for strand, grad in enumerate((down, up)):
        for k in times(strand)[::-1]:
            own_grad = chunk_grad[strand, k]
            chunk_grad[strand, k] = grad
            chunk_dot[strand, k, 0:8, :] = jnp.broadcast_to(
                jnp.sum(grad * chunk_dot[strand, k], axis=0, keepdims=True), (8, W)
            )
            grad = chunk_decay[strand, k, 0:1, :] * grad + own_grad
    ext[...] = jnp.zeros_like(ext)

    def back_step(k, carry):
        rows = rows_of(k)
        for strand in range(2):
            dt = dts_soft[strand, rows, :]
            e_rest = e_rests[strand, rows, :]
            dt_wide = dt_wides[strand, rows, :]
            grad = chunk_grad[strand, k].astype(BF16)
            x = xs[strand, rows, :]
            gb = gi[strand, rows, :] + e_rest * mm(bs[strand, rows, :], grad)
            dxs[strand, rows, :] = (dt_wide * gb + yi[strand, rows, :]).astype(BF16)
            d_b = dbs[strand, rows, :] + mm_t((x * dt_wide * e_rest).astype(BF16), grad)
            direct = gather_heads(x * gb, e)
            d_cum = dyy[strand, rows, :] - dt * direct
            d_a = running(d_cum, order(2 * strand - 1)) + gather_heads(
                chunk_dot[strand, k, 0:8, :], e
            )[0:1, :]
            d_raw = (direct - rate[...] * d_a) * sigmoid(dts[strand, rows, :])
            at_b, at_c, at_dt = SMALL[strand]
            ext[rows, at_b : at_b + NS] = d_b.astype(BF16)
            ext[rows, at_c : at_c + NS] = dcs[strand, rows, :].astype(BF16)
            ext[rows, at_dt : at_dt + HEADS] = d_raw.astype(BF16)
        return carry

    lax.fori_loop(0, CHUNKS, back_step, 0)

    weight_part(2, lambda b: hidden[:, rows_of(b)], lambda b: hidden_flip[:, rows_of(b)], dxs)
    in_sum.begin()
    weight_pair(1)
    weight_pair(2)
    in_sum.middle()
    in_sum.own_block()

    mix_sum.arrived()

    def mix_step(k, carry):
        rows = rows_of(k)
        mine = hidden[rows, pl.ds(pl.multiple_of(ch * Q, Q), Q)].astype(F32)
        block_out[rows, :] = (mine + mix_sum.finish(rows)).astype(BF16)
        return carry

    lax.fori_loop(0, CHUNKS, mix_step, 0)
    in_sum.arrived()

    def in_step(k, carry):
        rows = rows_of(k)
        grad_hidden[rows, :] = cot[ch, rows, :].astype(F32) + in_sum.finish(rows)
        return carry

    lax.fori_loop(0, CHUNKS, in_step, 0)

    for n, out in enumerate((grad_out, grad_z, grad_x)):
        total = h_own[n]
        for dz, dy in shifts:
            g_peer_copy(n, dz, dy).wait_recv()
            total = total + h_recv[n, 4 * dz + dy].astype(F32)
        out[...] = total

    for n in range(6):
        cot_copy(n).wait_send()
    round_a.drain()
    round_b.drain()
    mix_sum.drain()
    in_sum.drain()
    for n in range(3):
        g_core_copy(n).wait_send()
        for dz, dy in shifts:
            g_peer_copy(n, dz, dy).wait_send()


def shape(*dims, dtype=F32):
    return jax.ShapeDtypeStruct(dims, dtype)


VMEM = pl.BlockSpec(memory_space=pltpu.VMEM)


def body(
    hidden, proj_x, proj_z, proj_b, proj_c, proj_dt, dt_bias, decay_rate, skip_gain, proj_out, cotangent
):
    bias, rate, skip = (v[None, :] for v in (dt_bias, decay_rate, skip_gain))
    vm = pltpu.VMEM
    block_out, grad_hidden, grad_x, grad_z, grad_out = pl.pallas_call(
        block_kernel,
        out_shape=(
            shape(L, Q, dtype=BF16),
            shape(L, Q),
            shape(ROWS, W),
            shape(ROWS, W),
            shape(ROWS, W),
        ),
        in_specs=[pl.BlockSpec(memory_space=pl.ANY)] * 5 + [VMEM] * 6,
        out_specs=[VMEM] * 5,
        scratch_shapes=[
            vm((L, D), BF16), vm((D, W), BF16), vm((D, W), BF16), vm((W, D), BF16),
            vm((D, W), BF16), vm((D, W), BF16), vm((W, D), BF16), vm((128, D), BF16),
            vm((L, D), BF16), vm((BLOCKS, L, Q), BF16), vm((BLOCKS, L, Q), BF16),
            vm((2, L, W), F32), vm((2, L, W), F32), vm((2, L, NS), BF16), vm((2, L, NS), BF16),
            vm((2, L, HEADS), F32), vm((2, L, W), BF16), vm((2, L, HEADS), F32),
            vm((2, L, HEADS), F32), vm((2, L, W), F32), vm((2, L, W), F32), vm((2, L, W), F32),
            vm((2, L, W), BF16), vm((2, L, W), BF16), vm((Q, Q), F32),
            vm((2, L, W), F32), vm((2, L, W), F32), vm((2, L, NS), F32), vm((2, L, NS), F32),
            vm((2, L, HEADS), F32),
            vm((L, 128), BF16), vm((2, L, W), BF16), vm((2, L, W), BF16), vm((2, L, W), BF16),
            vm((2, CHUNKS, NS, W), F32), vm((2, CHUNKS, NS, W), F32),
            vm((2, CHUNKS, 8, W), F32), vm((2, CHUNKS, NS, W), F32),
            vm((2, 40, Q), F32), vm((40, Q), F32), vm((2, 24, Q), F32), vm((PEERS, 24, Q), F32),
            vm((32, Q), F32), vm((2, 32, Q), F32),
            vm((2, 32, Q), F32), vm((32, Q), F32), vm((2, 16, Q), F32), vm((PEERS, 16, Q), F32),
            vm((32, Q), F32), vm((2, 32, Q), F32),
            vm((L, Q), F32), vm((2, Q, Q), F32), vm((3, L, Q), BF16), vm((2, Q, Q), BF16),
            vm((2, L, Q), BF16),
            vm((L, Q), F32), vm((2, Q, Q), F32), vm((3, L, Q), BF16), vm((2, Q, Q), BF16),
            vm((2, L, Q), BF16),
            vm((3, PEERS, 2, ROWS, W), F32), vm((3, PEERS, 2, ROWS, W), BF16),
            vm((3, PEERS, ROWS, W), BF16),
            vm((3, ROWS, W), F32), vm((3, PEERS, ROWS, W), BF16),
            vm((3, PEERS, ROWS, W), BF16),
            pltpu.SemaphoreType.DMA((5,)),
            pltpu.SemaphoreType.DMA((S_ALL,)), pltpu.SemaphoreType.DMA((S_ALL,)),
        ],
        compiler_params=pltpu.CompilerParams(
            vmem_limit_bytes=60 * 2**20, collective_id=0, has_side_effects=True
        ),
        name="block",
    )(
        hidden, proj_x, proj_z, proj_out, cotangent,
        proj_b.T, proj_c.T, proj_dt.T, bias, rate, skip,
    )
    return block_out, grad_hidden, grad_x, grad_z, grad_out.T


def solution(mesh):
    return jax.shard_map(
        body,
        mesh=mesh,
        in_specs=(
            P("seq", None),
            P(None, "ch"),
            P(None, "ch"),
            P(),
            P(),
            P(None, "ch"),
            P("ch"),
            P("ch"),
            P("ch"),
            P("ch", None),
            P("seq", "ch"),
        ),
        out_specs=(P("seq", "ch"), P("seq", "ch"), P("seq", "ch"), P("seq", "ch"), P("ch", "seq")),
        check_vma=False,
    )
```

```python
import jax
import jax.numpy as jnp
from jax import lax
from jax.experimental import pallas as pl
from jax.experimental.pallas import tpu as pltpu
from jax.sharding import PartitionSpec as P

L = 512
D = 1024
W = 512
HEADS = 8
HEAD = 64
NS = 16
Q = 256
CHUNKS = L // Q
BLOCKS = D // Q
PEERS = 16
ROWS = 32
F32 = jnp.float32
BF16 = jnp.bfloat16
MESH = pl.DeviceIdType.MESH

LAST = (((1,), (1,)), ((), ()))
FIRST = (((0,), (0,)), ((), ()))

SMALL = ((0, 16, 32), (48, 64, 80))

S_COT, S_MIX, S_IN, S_A, S_B = 0, 6, 12, 18, 36
S_GCORE, S_GPEER = 54, 57
S_ALL = S_GPEER + 3 * 16


def mm(a, b):
    return jnp.dot(a, b, preferred_element_type=F32)


def mm_t(a, b):
    return lax.dot_general(a, b, LAST, preferred_element_type=F32)


def t_mm(a, b):
    return lax.dot_general(a, b, FIRST, preferred_element_type=F32)


def split2(v):
    high = v.astype(BF16)
    return high, (v - high.astype(F32)).astype(BF16)


def split3(v):
    high = v.astype(BF16)
    rest = v - high.astype(F32)
    mid = rest.astype(BF16)
    return high, mid, (rest - mid.astype(F32)).astype(BF16)


def iota(shape, dim):
    return lax.broadcasted_iota(jnp.int32, shape, dim)


def anti_identity():
    return jnp.where(iota((Q, Q), 0) + iota((Q, Q), 1) == Q - 1, 1.0, 0.0).astype(BF16)


def spread_matrix():
    return jnp.where(iota((HEADS, W), 1) // HEAD == iota((HEADS, W), 0), 1.0, 0.0).astype(BF16)


def spread(v, e):
    high, low = split2(v)
    return mm(high, e) + mm(low, e)


def gather_heads(v, e):
    high, low = split2(v)
    return mm_t(high, e) + mm_t(low, e)


def order(sign):
    return (iota((Q, Q), 0) - iota((Q, Q), 1)) * sign >= 0


def running(v, mask):
    ones = jnp.where(mask, 1.0, 0.0).astype(BF16)
    return sum(mm(ones, part) for part in split3(v))


def softplus(v):
    return jnp.maximum(v, 0.0) + jnp.log1p(jnp.exp(-jnp.abs(v)))


def sigmoid(v):
    return 1.0 / (1.0 + jnp.exp(-v))


def rows_of(k):
    return pl.ds(pl.multiple_of(k * Q, Q), Q)


def block_kernel(
    hidden_hbm, proj_x_hbm, proj_z_hbm, proj_out_hbm, cot_hbm,
    proj_b, proj_c, proj_dt, bias, rate, skip,
    block_out, grad_hidden, grad_x, grad_z, grad_out,
    hidden, proj_x, proj_z, proj_out,
    px_flip, pz_flip, po_flip, small, hidden_flip, cot, cot_flip,
    xs, zs, bs, cs, dts, dos, cums, dts_soft, e_cums, e_rests, dt_wides, dyb, xdt, zacc,
    yi, gi, dcs, dbs, dyy, ext, os, dxs, dzs,
    chunk_state, chunk_grad, chunk_decay, chunk_dot,
    a_msg, a_core, a_pair, a_slots, a_back, a_in,
    b_msg, b_core, b_pair, b_slots, b_back, b_in,
    mix_own, mix_part, mix_send, mix_fwd, mix_recv,
    in_own, in_part, in_send, in_fwd, in_recv,
    g_own, g_send, g_recv, h_own, h_send, h_recv,
    load_sem, send_sem, recv_sem, ready_sem,
):
    seq, ch = lax.axis_index("seq"), lax.axis_index("ch")
    core, y, z = lax.rem(seq, 2), lax.rem(seq // 2, 4), seq // 8
    other = 1 - core
    place = z * 4 + y

    def x_peer(k):
        return (seq, lax.rem(ch + k, 4))

    def zy_peer(dz, dy):
        return (lax.rem(z + dz, 4) * 8 + lax.rem(y + dy, 4) * 2 + core, ch)

    core_peer = (seq + 1 - 2 * core, ch)
    shifts = [(k // 4, k % 4) for k in range(1, PEERS)]

    def remote(src, dst, sem, device):
        return pltpu.make_async_remote_copy(
            src_ref=src,
            dst_ref=dst,
            send_sem=send_sem.at[sem],
            recv_sem=recv_sem.at[sem],
            device_id=device,
            device_id_type=MESH,
        )

    loads = [
        pltpu.make_async_copy(src, dst, load_sem.at[n])
        for n, (src, dst) in enumerate(
            (
                (cot_hbm, cot.at[ch]),
                (hidden_hbm, hidden),
                (proj_x_hbm, proj_x),
                (proj_z_hbm, proj_z),
                (proj_out_hbm, proj_out),
            )
        )
    ]
    for load in loads:
        load.start()

    barrier = pltpu.get_barrier_semaphore()
    y_peers = [zy_peer(0, k) for k in range(1, 4)]
    for device in [x_peer(1), x_peer(3), core_peer] + y_peers + [zy_peer(k, 0) for k in range(1, 4)]:
        pl.semaphore_signal(barrier, inc=1, device_id=device, device_id_type=MESH)
    anti = anti_identity()
    e = spread_matrix()
    small[...] = jnp.zeros_like(small)
    for weight, at in zip((proj_b, proj_c, proj_dt), range(3)):
        n = weight.shape[0]
        small[SMALL[0][at] : SMALL[0][at] + n, :] = weight[...]
        for k in range(BLOCKS):
            here, there = slice(k * Q, (k + 1) * Q), slice(D - (k + 1) * Q, D - k * Q)
            small[SMALL[1][at] : SMALL[1][at] + n, here] = mm(weight[:, there], anti).astype(BF16)
    for load in loads[:4]:
        load.wait()
    for k in range(BLOCKS):
        here, there = slice(k * Q, (k + 1) * Q), slice(D - (k + 1) * Q, D - k * Q)
        px_flip[here, :] = mm(anti, proj_x[there, :]).astype(BF16)
        pz_flip[here, :] = mm(anti, proj_z[there, :]).astype(BF16)
        hidden_flip[:, here] = mm(hidden[:, there], anti).astype(BF16)
    pl.semaphore_wait(barrier, 9)
    for device in y_peers:
        pl.semaphore_signal(ready_sem, inc=1, device_id=device, device_id_type=MESH)

    half = [slice(0, Q), slice(Q, L)]
    before, after = lax.rem(ch + 3, 4), lax.rem(ch + 1, 4)

    def cot_copy(n):
        block, rows, to = (
            (ch, half[0], 1), (ch, half[1], 3), (ch, half[1], 1), (ch, half[0], 3),
            (before, half[0], 1), (after, half[1], 3),
        )[n]
        return remote(cot.at[block, rows], cot.at[block, rows], S_COT + n, x_peer(to))

    for n in range(4):
        cot_copy(n).start()

    def project_step(k, carry):
        rows = rows_of(k)
        u = hidden[rows, :]
        xs[0, rows, :] = mm(u, proj_x[...])
        zs[0, rows, :] = mm(u, proj_z[...])
        xs[1, rows, :] = mm(u, px_flip[...])
        zs[1, rows, :] = mm(u, pz_flip[...])
        narrow = mm_t(u, small[...])
        for strand in range(2):
            at_b, at_c, at_dt = SMALL[strand]
            bs[strand, rows, :] = narrow[:, at_b : at_b + NS].astype(BF16)
            cs[strand, rows, :] = narrow[:, at_c : at_c + NS].astype(BF16)
            dts[strand, rows, :] = narrow[:, at_dt : at_dt + HEADS] + bias[...]
        return carry

    lax.fori_loop(0, CHUNKS, project_step, 0)

    def state_step(i, carry):
        strand, k = i // CHUNKS, lax.rem(i, CHUNKS)
        rows = rows_of(k)
        dt = softplus(dts[strand, rows, :])
        a = -rate[...] * dt
        cum = running(a, order(1 - 2 * strand))
        total = jnp.sum(a, axis=0, keepdims=True)
        cums[strand, rows, :] = cum
        dts_soft[strand, rows, :] = dt
        e_rest = spread(jnp.exp(total - cum), e)
        dt_wide = spread(dt, e)
        e_cums[strand, rows, :] = spread(jnp.exp(cum), e)
        e_rests[strand, rows, :] = e_rest
        dt_wides[strand, rows, :] = dt_wide
        xd = xs[strand, rows, :] * dt_wide
        xdt[strand, rows, :] = xd.astype(BF16)
        chunk_state[strand, k] = t_mm(bs[strand, rows, :], (xd * e_rest).astype(BF16))
        chunk_decay[strand, k] = jnp.broadcast_to(jnp.exp(spread(total, e)), (8, W))
        return carry

    lax.fori_loop(0, 2 * CHUNKS, state_step, 0)

    for n in range(2):
        cot_copy(n).wait_recv()
        cot_copy(4 + n).start()

    def times(strand):
        return list(range(CHUNKS)) if strand == 0 else list(range(CHUNKS))[::-1]

    def two_halves(dst, rows, value):
        dst[0, rows, :] = value[:, 0:Q]
        dst[1, rows, :] = value[:, Q:]

    decays = []
    for strand in range(2):
        state, decay = chunk_state[strand, times(strand)[0]], chunk_decay[strand, 0]
        for k in times(strand)[1:]:
            state = chunk_decay[strand, k, 0:1, :] * state + chunk_state[strand, k]
        for k in range(1, CHUNKS):
            decay = decay * chunk_decay[strand, k]
        two_halves(a_msg, slice(16 * strand, 16 * strand + NS), state)
        decays.append(decay)
    two_halves(a_msg, slice(32, 40), jnp.where(iota((8, W), 0) == 0, decays[0], decays[1]))

    zero = jnp.zeros((NS, Q), F32)
    a_slots[place] = jnp.zeros_like(a_slots[0])
    b_slots[place] = jnp.zeros_like(b_slots[0])

    class Exchange:
        def __init__(self, base, msg, from_core, pair, slots, back, result, swap):
            self.base, self.msg, self.from_core, self.pair = base, msg, from_core, pair
            self.slots, self.back, self.result, self.swap = slots, back, result, swap

        def to_core(self):
            return remote(self.msg.at[other], self.from_core, self.base, core_peer)

        def to_place(self, dz, dy):
            to = lax.rem(z + dz, 4) * 4 + lax.rem(y + dy, 4)
            kind = jnp.where(to > place, 0, 1)
            return remote(
                self.pair.at[kind], self.slots.at[place], self.base + 4 * dz + dy, zy_peer(dz, dy)
            )

        def to_back(self):
            return remote(self.back, self.result.at[core], self.base + PEERS, core_peer)

        def decay(self, ref, strand):
            return ref[strand : strand + 1, :]

        def both(self):
            mine = (
                self.msg[core, 0:16, :], self.msg[core, 16:32, :],
                a_msg[core, 32 + self.swap : 33 + self.swap, :],
                a_msg[core, 33 - self.swap : 34 - self.swap, :],
            )
            theirs = (
                self.from_core[0:16, :], self.from_core[16:32, :],
                a_core[32 + self.swap : 33 + self.swap, :],
                a_core[33 - self.swap : 34 - self.swap, :],
            )
            return mine, theirs

        def spread_out(self):
            self.to_core().wait_recv()
            mine, theirs = self.both()
            first = [jnp.where(core == 0, m, t) for m, t in zip(mine, theirs)]
            second = [jnp.where(core == 0, t, m) for m, t in zip(mine, theirs)]
            up = second[2] * first[0] + second[0]
            down = first[3] * second[1] + first[1]
            self.pair[0, 0:16, :] = up
            self.pair[1, 0:16, :] = down
            if not self.swap:
                product = jnp.where(
                    iota((8, Q), 0) == 0,
                    jnp.broadcast_to(first[2] * second[2], (8, Q)),
                    jnp.broadcast_to(first[3] * second[3], (8, Q)),
                )
                self.pair[0, 16:24, :] = product
                self.pair[1, 16:24, :] = product
            for dz, dy in shifts:
                self.to_place(dz, dy).start()

        def collect(self):
            for dz, dy in shifts:
                self.to_place(dz, dy).wait_recv()
            up = down = zero
            for j in range(PEERS):
                r = PEERS - 1 - j
                decay_up = a_slots[j, 16 + self.swap : 17 + self.swap, :]
                decay_down = a_slots[r, 17 - self.swap : 18 - self.swap, :]
                up = jnp.where(j < place, decay_up * up + self.slots[j, 0:16, :], up)
                down = jnp.where(r > place, decay_down * down + self.slots[r, 0:16, :], down)
            mine, theirs = self.both()
            self.back[0:16, :] = jnp.where(core == 0, mine[2] * up + mine[0], up)
            self.back[16:32, :] = jnp.where(core == 1, mine[3] * down + mine[1], down)
            self.to_back().start()
            self.result[core, 0:16, :] = jnp.where(core == 1, theirs[2] * up + theirs[0], up)
            self.result[core, 16:32, :] = jnp.where(core == 0, theirs[3] * down + theirs[1], down)

        def take(self):
            self.to_back().wait_recv()
            return [
                jnp.concatenate([self.result[0, rows, :], self.result[1, rows, :]], axis=1)
                for rows in (slice(0, 16), slice(16, 32))
            ]

        def drain(self):
            self.to_core().wait_send()
            self.to_back().wait_send()
            for dz, dy in shifts:
                self.to_place(dz, dy).wait_send()

    round_a = Exchange(S_A, a_msg, a_core, a_pair, a_slots, a_back, a_in, 0)
    round_b = Exchange(S_B, b_msg, b_core, b_pair, b_slots, b_back, b_in, 1)
    round_a.to_core().start()

    lane = iota((Q, 128), 1)

    def within_step(i, carry):
        strand, k = i // CHUNKS, lax.rem(i, CHUNKS)
        rows = rows_of(k)
        mask = order(1 - 2 * strand)
        cum = cums[strand, rows, :]
        cum_t = cum.T
        scores = mm_t(cs[strand, rows, :], bs[strand, rows, :])
        for pair in range(HEADS // 2):
            columns = slice(pair * 128, (pair + 1) * 128)
            x_pair = xdt[strand, rows, columns]
            y_sum = None
            for odd in range(2):
                h = 2 * pair + odd
                own = (lane >= HEAD) if odd else (lane < HEAD)
                x_own = jnp.where(own, x_pair, jnp.zeros((), BF16))
                decay = jnp.exp(
                    jnp.where(mask, cum[:, h : h + 1] - cum_t[h : h + 1, :], -1e30)
                )
                y_new = mm((decay * scores).astype(BF16), x_own)
                y_sum = y_new if y_sum is None else y_sum + y_new
            yi[strand, rows, columns] = y_sum

        @pl.when(i == 0)
        def _():
            pl.semaphore_wait(ready_sem, 3)
            round_a.spread_out()

        return carry

    lax.fori_loop(0, 2 * CHUNKS, within_step, 0)

    loads[4].wait()
    for k in range(BLOCKS):
        here, there = slice(k * Q, (k + 1) * Q), slice(D - (k + 1) * Q, D - k * Q)
        po_flip[:, here] = mm(proj_out[:, there], anti).astype(BF16)
    round_a.collect()

    for n in range(2, 6):
        cot_copy(n).wait_recv()

    def cot_step(k, carry):
        rows = rows_of(k)
        forward = backward = None
        for b in range(BLOCKS):
            cot_flip[b, rows, :] = mm(cot[BLOCKS - 1 - b, rows, :], anti).astype(BF16)
            columns = slice(b * Q, (b + 1) * Q)
            part = mm_t(cot[b, rows, :], proj_out[:, columns])
            part_flip = mm_t(cot[b, rows, :], po_flip[:, columns])
            forward = part if forward is None else forward + part
            backward = part_flip if backward is None else backward + part_flip
        dos[0, rows, :] = forward.astype(BF16)
        dos[1, rows, :] = backward.astype(BF16)
        return carry

    lax.fori_loop(0, CHUNKS, cot_step, 0)

    def grad_step(i, carry):
        strand, k = i // CHUNKS, lax.rem(i, CHUNKS)
        rows = rows_of(k)
        gate = zs[strand, rows, :]
        dy = dos[strand, rows, :].astype(F32) * (gate * sigmoid(gate))
        dyb[strand, rows, :] = dy.astype(BF16)
        chunk_grad[strand, k] = t_mm(
            cs[strand, rows, :], (dy * e_cums[strand, rows, :]).astype(BF16)
        )
        return carry

    lax.fori_loop(0, 2 * CHUNKS, grad_step, 0)

    for strand in range(2):
        falling = times(strand)[::-1]
        grad = chunk_grad[strand, falling[0]]
        for k in falling[1:]:
            grad = chunk_decay[strand, k, 0:1, :] * grad + chunk_grad[strand, k]
        two_halves(b_msg, slice(16 - 16 * strand, 32 - 16 * strand), grad)
    round_b.to_core().start()

    for strand, state in enumerate(round_a.take()):
        for k in times(strand):
            own_state = chunk_state[strand, k]
            chunk_state[strand, k] = state
            state = chunk_decay[strand, k, 0:1, :] * state + own_state
            chunk_dot[strand, k] = state

    skip_wide = spread(skip[...], e)

    def out_step(i, carry):
        strand, k = i // CHUNKS, lax.rem(i, CHUNKS)
        rows = rows_of(k)
        e_cum = e_cums[strand, rows, :]
        state = chunk_state[strand, k].astype(BF16)
        gate = zs[strand, rows, :]
        d_o = dos[strand, rows, :].astype(F32)
        sig = sigmoid(gate)
        silu = gate * sig
        dy = d_o * silu
        y_part = yi[strand, rows, :] + e_cum * mm(cs[strand, rows, :], state)
        out = y_part + skip_wide * xs[strand, rows, :]
        os[strand, rows, :] = (out * silu).astype(BF16)
        dzs[strand, rows, :] = (d_o * out * (sig + silu * (1.0 - sig))).astype(BF16)
        dcs[strand, rows, :] = mm_t((dy * e_cum).astype(BF16), state)
        dyy[strand, rows, :] = gather_heads(dy * y_part, e)
        yi[strand, rows, :] = skip_wide * dy

        @pl.when(i == 1)
        def _():
            round_b.spread_out()

        return carry

    lax.fori_loop(0, 2 * CHUNKS, out_step, 0)

    class ColumnSum:
        def __init__(self, base, compute, own, part, send, forward, recv):
            self.base, self.compute, self.own, self.part = base, compute, own, part
            self.send, self.forward, self.recv = send, forward, recv

        def copy(self, n):
            src, dst, to = (
                (self.send.at[1, half[0]], self.forward.at[0], 1),
                (self.send.at[1, half[1]], self.forward.at[1], 3),
                (self.send.at[0, half[1]], self.recv.at[0, half[1]], 1),
                (self.send.at[2, half[0]], self.recv.at[1, half[0]], 3),
                (self.send.at[0, half[0]], self.recv.at[0, half[0]], 1),
                (self.send.at[2, half[1]], self.recv.at[1, half[1]], 3),
            )[n]
            return remote(src, dst, self.base + n, x_peer(to))

        def columns(self, r):
            return pl.ds(pl.multiple_of(lax.rem(ch + r, 4) * Q, Q), Q)

        def far(self):
            for n in range(2):
                self.send[1, half[n], :] = self.compute(half[n], self.columns(2)).astype(BF16)
                self.copy(n).start()

        def near(self):
            self.send[0, half[1], :] = self.compute(half[1], self.columns(1)).astype(BF16)
            self.copy(2).start()
            self.send[2, half[0], :] = self.compute(half[0], self.columns(3)).astype(BF16)
            self.copy(3).start()
            self.part[0] = self.compute(half[0], self.columns(1))
            self.part[1] = self.compute(half[1], self.columns(3))

        def middle(self):
            for n, block in ((0, 0), (1, 2)):
                self.copy(n).wait_recv()
                self.send[block, half[n], :] = (
                    self.part[n] + self.forward[n].astype(F32)
                ).astype(BF16)
                self.copy(4 + n).start()

        def own_block(self):
            for n in range(2):
                self.own[half[n], :] = self.compute(half[n], self.columns(0))

        def finish(self, rows):
            return (
                self.own[rows, :]
                + self.recv[0, rows, :].astype(F32)
                + self.recv[1, rows, :].astype(F32)
            )

        def arrived(self):
            for n in range(2, 6):
                self.copy(n).wait_recv()

        def drain(self):
            for n in range(6):
                self.copy(n).wait_send()

    def mix_block(rows, columns):
        return mm(os[0, rows, :], proj_out[:, columns]) + mm(os[1, rows, :], po_flip[:, columns])

    def in_block(rows, columns):
        return (
            mm_t(dxs[0, rows, :], proj_x[columns, :])
            + mm_t(dzs[0, rows, :], proj_z[columns, :])
            + mm_t(dxs[1, rows, :], px_flip[columns, :])
            + mm_t(dzs[1, rows, :], pz_flip[columns, :])
            + mm(ext[rows, :], small[:, columns])
        )

    mix_sum = ColumnSum(S_MIX, mix_block, mix_own, mix_part, mix_send, mix_fwd, mix_recv)
    in_sum = ColumnSum(S_IN, in_block, in_own, in_part, in_send, in_fwd, in_recv)
    mix_sum.far()
    mix_sum.near()

    def g_core_copy(n):
        return remote(g_send.at[n, :, other], g_recv.at[n], S_GCORE + n, core_peer)

    def g_peer_copy(n, dz, dy):
        to = lax.rem(z + dz, 4) * 4 + lax.rem(y + dy, 4)
        at = 4 * dz + dy
        return remote(
            h_send.at[n, to], h_recv.at[n, at], S_GPEER + PEERS * n + at, zy_peer(dz, dy)
        )

    def weight_part(n, left, left_flip, right):
        def step(b, carry):
            value = t_mm(left(b), right[0]) + t_mm(left_flip(b), right[1])
            g_own[n, pl.ds(pl.multiple_of(b * 4, 4), 4)] = value.reshape(4, 2, ROWS, W)
            g_send[n, pl.ds(pl.multiple_of(b * 4, 4), 4)] = value.astype(BF16).reshape(
                4, 2, ROWS, W
            )
            return carry

        lax.fori_loop(0, BLOCKS, step, 0)
        g_core_copy(n).start()

    def weight_pair(n):
        g_core_copy(n).wait_recv()

        def pair_sum(i, carry):
            value = g_own[n, i, core] + g_recv[n, i].astype(F32)
            h_send[n, i] = value.astype(BF16)
            return carry

        lax.fori_loop(0, PEERS, pair_sum, 0)
        h_own[n] = g_own[n, place, core] + g_recv[n, place].astype(F32)
        for dz, dy in shifts:
            g_peer_copy(n, dz, dy).start()

    weight_part(0, lambda b: cot[b], lambda b: cot_flip[b], os)
    weight_part(1, lambda b: hidden[:, rows_of(b)], lambda b: hidden_flip[:, rows_of(b)], dzs)

    def inner_step(i, carry):
        strand, k = i // CHUNKS, lax.rem(i, CHUNKS)
        rows = rows_of(k)
        mask = order(2 * strand - 1)
        cum = cums[strand, rows, :]
        cum_t = cum.T
        b = bs[strand, rows, :]
        c = cs[strand, rows, :]
        scores = mm_t(b, c)
        for pair in range(HEADS // 2):
            columns = slice(pair * 128, (pair + 1) * 128)
            x_pair, dy_pair = xdt[strand, rows, columns], dyb[strand, rows, columns]
            g_sum = None
            for odd in range(2):
                h = 2 * pair + odd
                own = (lane >= HEAD) if odd else (lane < HEAD)
                dy_own = jnp.where(own, dy_pair, jnp.zeros((), BF16))
                decay = jnp.exp(
                    jnp.where(mask, cum_t[h : h + 1, :] - cum[:, h : h + 1], -1e30)
                )
                cross = mm_t(x_pair, dy_own)
                if h == 0:
                    zacc[...] = decay * cross
                else:
                    zacc[...] += decay * cross
                g_new = mm((decay * scores).astype(BF16), dy_own)
                g_sum = g_new if g_sum is None else g_sum + g_new
            gi[strand, rows, columns] = g_sum
        pairs = zacc[...].astype(BF16)
        dbs[strand, rows, :] = mm(pairs, c)
        dcs[strand, rows, :] += t_mm(pairs, b)

        @pl.when(i == 0)
        def _():
            mix_sum.middle()
            weight_pair(0)

        @pl.when(i == 1)
        def _():
            round_b.collect()

        return carry

    lax.fori_loop(0, 2 * CHUNKS, inner_step, 0)

    mix_sum.own_block()
    weight_pair(1)

    up, down = round_b.take()
    for strand, grad in enumerate((down, up)):
        for k in times(strand)[::-1]:
            own_grad = chunk_grad[strand, k]
            chunk_grad[strand, k] = grad
            chunk_dot[strand, k, 0:8, :] = jnp.broadcast_to(
                jnp.sum(grad * chunk_dot[strand, k], axis=0, keepdims=True), (8, W)
            )
            grad = chunk_decay[strand, k, 0:1, :] * grad + own_grad
    ext[...] = jnp.zeros_like(ext)

    def back_step(k, carry):
        rows = rows_of(k)
        for strand in range(2):
            dt = dts_soft[strand, rows, :]
            e_rest = e_rests[strand, rows, :]
            dt_wide = dt_wides[strand, rows, :]
            grad = chunk_grad[strand, k].astype(BF16)
            x = xs[strand, rows, :]
            gb = gi[strand, rows, :] + e_rest * mm(bs[strand, rows, :], grad)
            dxs[strand, rows, :] = (dt_wide * gb + yi[strand, rows, :]).astype(BF16)
            d_b = dbs[strand, rows, :] + mm_t((x * dt_wide * e_rest).astype(BF16), grad)
            direct = gather_heads(x * gb, e)
            d_cum = dyy[strand, rows, :] - dt * direct
            d_a = running(d_cum, order(2 * strand - 1)) + gather_heads(
                chunk_dot[strand, k, 0:8, :], e
            )[0:1, :]
            d_raw = (direct - rate[...] * d_a) * sigmoid(dts[strand, rows, :])
            at_b, at_c, at_dt = SMALL[strand]
            ext[rows, at_b : at_b + NS] = d_b.astype(BF16)
            ext[rows, at_c : at_c + NS] = dcs[strand, rows, :].astype(BF16)
            ext[rows, at_dt : at_dt + HEADS] = d_raw.astype(BF16)
        return carry

    lax.fori_loop(0, CHUNKS, back_step, 0)

    in_sum.far()
    weight_part(2, lambda b: hidden[:, rows_of(b)], lambda b: hidden_flip[:, rows_of(b)], dxs)
    in_sum.near()
    weight_pair(2)
    in_sum.middle()
    in_sum.own_block()

    mix_sum.arrived()

    def mix_step(k, carry):
        rows = rows_of(k)
        mine = hidden[rows, pl.ds(pl.multiple_of(ch * Q, Q), Q)].astype(F32)
        block_out[rows, :] = (mine + mix_sum.finish(rows)).astype(BF16)
        return carry

    lax.fori_loop(0, CHUNKS, mix_step, 0)
    in_sum.arrived()

    def in_step(k, carry):
        rows = rows_of(k)
        grad_hidden[rows, :] = cot[ch, rows, :].astype(F32) + in_sum.finish(rows)
        return carry

    lax.fori_loop(0, CHUNKS, in_step, 0)

    for n, out in enumerate((grad_out, grad_z, grad_x)):
        total = h_own[n]
        for dz, dy in shifts:
            g_peer_copy(n, dz, dy).wait_recv()
            total = total + h_recv[n, 4 * dz + dy].astype(F32)
        out[...] = total

    for n in range(6):
        cot_copy(n).wait_send()
    round_a.drain()
    round_b.drain()
    mix_sum.drain()
    in_sum.drain()
    for n in range(3):
        g_core_copy(n).wait_send()
        for dz, dy in shifts:
            g_peer_copy(n, dz, dy).wait_send()


def hand_over(*refs):
    sems = refs[10]
    copies = [pltpu.make_async_copy(refs[n], refs[5 + n], sems.at[n]) for n in range(5)]
    for copy in copies:
        copy.start()
    for copy in copies:
        copy.wait()


def shape(*dims, dtype=F32):
    return jax.ShapeDtypeStruct(dims, dtype)


VMEM = pl.BlockSpec(memory_space=pltpu.VMEM)


def body(
    hidden, proj_x, proj_z, proj_b, proj_c, proj_dt, dt_bias, decay_rate, skip_gain, proj_out, cotangent
):
    bias, rate, skip = (v[None, :] for v in (dt_bias, decay_rate, skip_gain))
    vm = pltpu.VMEM
    results = (
        shape(L, Q, dtype=BF16),
        shape(L, Q),
        shape(ROWS, W),
        shape(ROWS, W),
        shape(ROWS, W),
    )
    made = pl.pallas_call(
        block_kernel,
        out_shape=results,
        in_specs=[pl.BlockSpec(memory_space=pl.ANY)] * 5 + [VMEM] * 6,
        out_specs=[VMEM] * 5,
        scratch_shapes=[
            vm((L, D), BF16), vm((D, W), BF16), vm((D, W), BF16), vm((W, D), BF16),
            vm((D, W), BF16), vm((D, W), BF16), vm((W, D), BF16), vm((128, D), BF16),
            vm((L, D), BF16), vm((BLOCKS, L, Q), BF16), vm((BLOCKS, L, Q), BF16),
            vm((2, L, W), F32), vm((2, L, W), F32), vm((2, L, NS), BF16), vm((2, L, NS), BF16),
            vm((2, L, HEADS), F32), vm((2, L, W), BF16), vm((2, L, HEADS), F32),
            vm((2, L, HEADS), F32), vm((2, L, W), F32), vm((2, L, W), F32), vm((2, L, W), F32),
            vm((2, L, W), BF16), vm((2, L, W), BF16), vm((Q, Q), F32),
            vm((2, L, W), F32), vm((2, L, W), F32), vm((2, L, NS), F32), vm((2, L, NS), F32),
            vm((2, L, HEADS), F32),
            vm((L, 128), BF16), vm((2, L, W), BF16), vm((2, L, W), BF16), vm((2, L, W), BF16),
            vm((2, CHUNKS, NS, W), F32), vm((2, CHUNKS, NS, W), F32),
            vm((2, CHUNKS, 8, W), F32), vm((2, CHUNKS, NS, W), F32),
            vm((2, 40, Q), F32), vm((40, Q), F32), vm((2, 24, Q), F32), vm((PEERS, 24, Q), F32),
            vm((32, Q), F32), vm((2, 32, Q), F32),
            vm((2, 32, Q), F32), vm((32, Q), F32), vm((2, 16, Q), F32), vm((PEERS, 16, Q), F32),
            vm((32, Q), F32), vm((2, 32, Q), F32),
            vm((L, Q), F32), vm((2, Q, Q), F32), vm((3, L, Q), BF16), vm((2, Q, Q), BF16),
            vm((2, L, Q), BF16),
            vm((L, Q), F32), vm((2, Q, Q), F32), vm((3, L, Q), BF16), vm((2, Q, Q), BF16),
            vm((2, L, Q), BF16),
            vm((3, PEERS, 2, ROWS, W), F32), vm((3, PEERS, 2, ROWS, W), BF16),
            vm((3, PEERS, ROWS, W), BF16),
            vm((3, ROWS, W), F32), vm((3, PEERS, ROWS, W), BF16),
            vm((3, PEERS, ROWS, W), BF16),
            pltpu.SemaphoreType.DMA((5,)),
            pltpu.SemaphoreType.DMA((S_ALL,)), pltpu.SemaphoreType.DMA((S_ALL,)),
            pltpu.SemaphoreType.REGULAR,
        ],
        compiler_params=pltpu.CompilerParams(
            vmem_limit_bytes=60 * 2**20, collective_id=0, has_side_effects=True
        ),
        name="block",
    )(
        hidden, proj_x, proj_z, proj_out, cotangent,
        proj_b.T, proj_c.T, proj_dt.T, bias, rate, skip,
    )
    *most, grad_out = pl.pallas_call(
        hand_over,
        out_shape=results,
        in_specs=[pl.BlockSpec(memory_space=pl.ANY)] * 5,
        out_specs=[pl.BlockSpec(memory_space=pl.ANY)] * 5,
        scratch_shapes=[pltpu.SemaphoreType.DMA((5,))],
        name="hand_over",
    )(*made)
    return *most, grad_out.T


def solution(mesh):
    return jax.shard_map(
        body,
        mesh=mesh,
        in_specs=(
            P("seq", None),
            P(None, "ch"),
            P(None, "ch"),
            P(),
            P(),
            P(None, "ch"),
            P("ch"),
            P("ch"),
            P("ch"),
            P("ch", None),
            P("seq", "ch"),
        ),
        out_specs=(P("seq", "ch"), P("seq", "ch"), P("seq", "ch"), P("seq", "ch"), P("ch", "seq")),
        check_vma=False,
    )
```

```python
import jax
import jax.numpy as jnp
from jax import lax
from jax.experimental import pallas as pl
from jax.experimental.pallas import tpu as pltpu
from jax.sharding import PartitionSpec as P

L = 512
D = 1024
W = 512
HEADS = 8
HEAD = 64
NS = 16
Q = 256
CHUNKS = L // Q
BLOCKS = D // Q
PEERS = 16
ROWS = 32
F32 = jnp.float32
BF16 = jnp.bfloat16
MESH = pl.DeviceIdType.MESH

LAST = (((1,), (1,)), ((), ()))
FIRST = (((0,), (0,)), ((), ()))

SMALL = ((0, 16, 32), (48, 64, 80))

S_COT, S_MIX, S_IN, S_A, S_B = 0, 6, 12, 18, 36
S_GCORE, S_GPEER = 54, 57
S_ALL = S_GPEER + 3 * 16


def mm(a, b):
    return jnp.dot(a, b, preferred_element_type=F32)


def mm_t(a, b):
    return lax.dot_general(a, b, LAST, preferred_element_type=F32)


def t_mm(a, b):
    return lax.dot_general(a, b, FIRST, preferred_element_type=F32)


def split2(v):
    high = v.astype(BF16)
    return high, (v - high.astype(F32)).astype(BF16)


def split3(v):
    high = v.astype(BF16)
    rest = v - high.astype(F32)
    mid = rest.astype(BF16)
    return high, mid, (rest - mid.astype(F32)).astype(BF16)


def iota(shape, dim):
    return lax.broadcasted_iota(jnp.int32, shape, dim)


def identity():
    return jnp.where(iota((Q, Q), 0) == iota((Q, Q), 1), 1.0, 0.0).astype(BF16)


def anti_identity():
    return jnp.where(iota((Q, Q), 0) + iota((Q, Q), 1) == Q - 1, 1.0, 0.0).astype(BF16)


def spread_matrix():
    head = iota((2 * HEADS, W), 0)
    head = jnp.where(head >= HEADS, head - HEADS, head)
    return jnp.where(iota((2 * HEADS, W), 1) // HEAD == head, 1.0, 0.0).astype(BF16)


def spread(v, e):
    return mm(jnp.concatenate(split2(v), axis=1), e)


def gather_heads(v, e):
    high, low = split2(v)
    return (mm_t(high, e) + mm_t(low, e))[:, 0:HEADS]


def order(sign):
    return (iota((Q, Q), 0) - iota((Q, Q), 1)) * sign >= 0


def running(v, mask):
    ones = jnp.where(mask, 1.0, 0.0).astype(BF16)
    return sum(mm(ones, part) for part in split3(v))


def softplus(v):
    return jnp.maximum(v, 0.0) + jnp.log1p(jnp.exp(-jnp.abs(v)))


def sigmoid(v):
    return 1.0 / (1.0 + jnp.exp(-v))


def rows_of(k):
    return pl.ds(pl.multiple_of(k * Q, Q), Q)


def block_kernel(
    hidden_hbm, proj_x_hbm, proj_z_hbm, proj_out_hbm, cot_hbm,
    proj_b, proj_c, proj_dt, bias, rate, skip,
    block_out, grad_hidden, grad_x, grad_z, grad_out,
    hidden, proj_x, proj_z, proj_out,
    px_flip, pz_flip, po_flip, small, hidden_t, hidden_flip_t, cot, cot_t, cot_flip_t,
    xs, zs, bs, cs, dts, dos, cums, dts_soft, e_cums, e_rests, dt_wides, dyb, xdt, zacc,
    yi, gi, dcs, dbs, dyy, ext, os, dxs, dzs,
    chunk_state, chunk_grad, chunk_decay, chunk_dot,
    a_msg, a_core, a_pair, a_slots, a_back, a_in,
    b_msg, b_core, b_pair, b_slots, b_back, b_in,
    mix_own, mix_part, mix_send, mix_fwd, mix_recv,
    in_own, in_part, in_send, in_fwd, in_recv,
    g_own, g_send, g_recv, h_own, h_send, h_recv,
    load_sem, send_sem, recv_sem, ready_sem,
):
    seq, ch = lax.axis_index("seq"), lax.axis_index("ch")
    core, y, z = lax.rem(seq, 2), lax.rem(seq // 2, 4), seq // 8
    other = 1 - core
    place = z * 4 + y

    def x_peer(k):
        return (seq, lax.rem(ch + k, 4))

    def zy_peer(dz, dy):
        return (lax.rem(z + dz, 4) * 8 + lax.rem(y + dy, 4) * 2 + core, ch)

    core_peer = (seq + 1 - 2 * core, ch)
    shifts = [(k // 4, k % 4) for k in range(1, PEERS)]

    def remote(src, dst, sem, device):
        return pltpu.make_async_remote_copy(
            src_ref=src,
            dst_ref=dst,
            send_sem=send_sem.at[sem],
            recv_sem=recv_sem.at[sem],
            device_id=device,
            device_id_type=MESH,
        )

    loads = [
        pltpu.make_async_copy(src, dst, load_sem.at[n])
        for n, (src, dst) in enumerate(
            (
                (cot_hbm, cot.at[ch]),
                (hidden_hbm, hidden),
                (proj_x_hbm, proj_x),
                (proj_z_hbm, proj_z),
                (proj_out_hbm, proj_out),
            )
        )
    ]
    for load in loads:
        load.start()

    barrier = pltpu.get_barrier_semaphore()
    y_peers = [zy_peer(0, k) for k in range(1, 4)]
    for device in [x_peer(1), x_peer(3), core_peer] + y_peers + [zy_peer(k, 0) for k in range(1, 4)]:
        pl.semaphore_signal(barrier, inc=1, device_id=device, device_id_type=MESH)
    anti = anti_identity()
    e = spread_matrix()
    small[...] = jnp.zeros_like(small)
    for weight, at in zip((proj_b, proj_c, proj_dt), range(3)):
        n = weight.shape[0]
        small[SMALL[0][at] : SMALL[0][at] + n, :] = weight[...]
        for k in range(BLOCKS):
            here, there = slice(k * Q, (k + 1) * Q), slice(D - (k + 1) * Q, D - k * Q)
            small[SMALL[1][at] : SMALL[1][at] + n, here] = mm(weight[:, there], anti).astype(BF16)
    loads[0].wait()
    pl.semaphore_wait(barrier, 9)
    for device in y_peers:
        pl.semaphore_signal(ready_sem, inc=1, device_id=device, device_id_type=MESH)

    half = [slice(0, Q), slice(Q, L)]
    before, after = lax.rem(ch + 3, 4), lax.rem(ch + 1, 4)

    def cot_copy(n):
        block, rows, to = (
            (ch, half[0], 1), (ch, half[1], 3), (ch, half[1], 1), (ch, half[0], 3),
            (before, half[0], 1), (after, half[1], 3),
        )[n]
        return remote(cot.at[block, rows], cot.at[block, rows], S_COT + n, x_peer(to))

    for n in range(4):
        cot_copy(n).start()

    loads[1].wait()
    ident = identity()
    for k in range(BLOCKS):
        here, there = slice(k * Q, (k + 1) * Q), slice(D - (k + 1) * Q, D - k * Q)
        hidden_t[k] = mm_t(ident, hidden[:, here]).astype(BF16)
        hidden_flip_t[k] = mm_t(anti, hidden[:, there]).astype(BF16)
    for load, source, flip in ((loads[2], proj_x, px_flip), (loads[3], proj_z, pz_flip)):
        load.wait()
        for k in range(BLOCKS):
            here, there = slice(k * Q, (k + 1) * Q), slice(D - (k + 1) * Q, D - k * Q)
            flip[here, :] = mm(anti, source[there, :]).astype(BF16)

    def project_step(k, carry):
        rows = rows_of(k)
        u = hidden[rows, :]
        xs[0, rows, :] = mm(u, proj_x[...])
        zs[0, rows, :] = mm(u, proj_z[...])
        xs[1, rows, :] = mm(u, px_flip[...])
        zs[1, rows, :] = mm(u, pz_flip[...])
        narrow = mm_t(u, small[...])
        for strand in range(2):
            at_b, at_c, at_dt = SMALL[strand]
            bs[strand, rows, :] = narrow[:, at_b : at_b + NS].astype(BF16)
            cs[strand, rows, :] = narrow[:, at_c : at_c + NS].astype(BF16)
            dts[strand, rows, :] = narrow[:, at_dt : at_dt + HEADS] + bias[...]
        return carry

    lax.fori_loop(0, CHUNKS, project_step, 0)

    def state_step(i, carry):
        strand, k = i // CHUNKS, lax.rem(i, CHUNKS)
        rows = rows_of(k)
        dt = softplus(dts[strand, rows, :])
        a = -rate[...] * dt
        cum = running(a, order(1 - 2 * strand))
        total = jnp.sum(a, axis=0, keepdims=True)
        cums[strand, rows, :] = cum
        dts_soft[strand, rows, :] = dt
        e_rest = spread(jnp.exp(total - cum), e)
        dt_wide = spread(dt, e)
        e_cums[strand, rows, :] = spread(jnp.exp(cum), e)
        e_rests[strand, rows, :] = e_rest
        dt_wides[strand, rows, :] = dt_wide
        xd = xs[strand, rows, :] * dt_wide
        xdt[strand, rows, :] = xd.astype(BF16)
        chunk_state[strand, k] = t_mm(bs[strand, rows, :], (xd * e_rest).astype(BF16))
        chunk_decay[strand, k] = jnp.broadcast_to(jnp.exp(spread(total, e)), (8, W))
        return carry

    lax.fori_loop(0, 2 * CHUNKS, state_step, 0)

    for n in range(2):
        cot_copy(n).wait_recv()
        cot_copy(4 + n).start()

    def times(strand):
        return list(range(CHUNKS)) if strand == 0 else list(range(CHUNKS))[::-1]

    def two_halves(dst, rows, value):
        dst[0, rows, :] = value[:, 0:Q]
        dst[1, rows, :] = value[:, Q:]

    decays = []
    for strand in range(2):
        state, decay = chunk_state[strand, times(strand)[0]], chunk_decay[strand, 0]
        for k in times(strand)[1:]:
            state = chunk_decay[strand, k, 0:1, :] * state + chunk_state[strand, k]
        for k in range(1, CHUNKS):
            decay = decay * chunk_decay[strand, k]
        two_halves(a_msg, slice(16 * strand, 16 * strand + NS), state)
        decays.append(decay)
    two_halves(a_msg, slice(32, 40), jnp.where(iota((8, W), 0) == 0, decays[0], decays[1]))

    zero = jnp.zeros((NS, Q), F32)
    a_slots[place] = jnp.zeros_like(a_slots[0])
    b_slots[place] = jnp.zeros_like(b_slots[0])

    class Exchange:
        def __init__(self, base, msg, from_core, pair, slots, back, result, swap):
            self.base, self.msg, self.from_core, self.pair = base, msg, from_core, pair
            self.slots, self.back, self.result, self.swap = slots, back, result, swap

        def to_core(self):
            return remote(self.msg.at[other], self.from_core, self.base, core_peer)

        def to_place(self, dz, dy):
            to = lax.rem(z + dz, 4) * 4 + lax.rem(y + dy, 4)
            kind = jnp.where(to > place, 0, 1)
            return remote(
                self.pair.at[kind], self.slots.at[place], self.base + 4 * dz + dy, zy_peer(dz, dy)
            )

        def to_back(self):
            return remote(self.back, self.result.at[core], self.base + PEERS, core_peer)

        def decay(self, ref, strand):
            return ref[strand : strand + 1, :]

        def both(self):
            mine = (
                self.msg[core, 0:16, :], self.msg[core, 16:32, :],
                a_msg[core, 32 + self.swap : 33 + self.swap, :],
                a_msg[core, 33 - self.swap : 34 - self.swap, :],
            )
            theirs = (
                self.from_core[0:16, :], self.from_core[16:32, :],
                a_core[32 + self.swap : 33 + self.swap, :],
                a_core[33 - self.swap : 34 - self.swap, :],
            )
            return mine, theirs

        def spread_out(self):
            self.to_core().wait_recv()
            mine, theirs = self.both()
            first = [jnp.where(core == 0, m, t) for m, t in zip(mine, theirs)]
            second = [jnp.where(core == 0, t, m) for m, t in zip(mine, theirs)]
            up = second[2] * first[0] + second[0]
            down = first[3] * second[1] + first[1]
            self.pair[0, 0:16, :] = up
            self.pair[1, 0:16, :] = down
            if not self.swap:
                product = jnp.where(
                    iota((8, Q), 0) == 0,
                    jnp.broadcast_to(first[2] * second[2], (8, Q)),
                    jnp.broadcast_to(first[3] * second[3], (8, Q)),
                )
                self.pair[0, 16:24, :] = product
                self.pair[1, 16:24, :] = product
            for dz, dy in shifts:
                self.to_place(dz, dy).start()

        def collect(self):
            for dz, dy in shifts:
                self.to_place(dz, dy).wait_recv()
            up = down = zero
            for j in range(PEERS):
                r = PEERS - 1 - j
                decay_up = a_slots[j, 16 + self.swap : 17 + self.swap, :]
                decay_down = a_slots[r, 17 - self.swap : 18 - self.swap, :]
                up = jnp.where(j < place, decay_up * up + self.slots[j, 0:16, :], up)
                down = jnp.where(r > place, decay_down * down + self.slots[r, 0:16, :], down)
            mine, theirs = self.both()
            self.back[0:16, :] = jnp.where(core == 0, mine[2] * up + mine[0], up)
            self.back[16:32, :] = jnp.where(core == 1, mine[3] * down + mine[1], down)
            self.to_back().start()
            self.result[core, 0:16, :] = jnp.where(core == 1, theirs[2] * up + theirs[0], up)
            self.result[core, 16:32, :] = jnp.where(core == 0, theirs[3] * down + theirs[1], down)

        def take(self):
            self.to_back().wait_recv()
            return [
                jnp.concatenate([self.result[0, rows, :], self.result[1, rows, :]], axis=1)
                for rows in (slice(0, 16), slice(16, 32))
            ]

        def drain(self):
            self.to_core().wait_send()
            self.to_back().wait_send()
            for dz, dy in shifts:
                self.to_place(dz, dy).wait_send()

    round_a = Exchange(S_A, a_msg, a_core, a_pair, a_slots, a_back, a_in, 0)
    round_b = Exchange(S_B, b_msg, b_core, b_pair, b_slots, b_back, b_in, 1)
    round_a.to_core().start()

    lane = iota((Q, 128), 1)

    def within_step(i, carry):
        strand, k = i // CHUNKS, lax.rem(i, CHUNKS)
        rows = rows_of(k)
        mask = order(1 - 2 * strand)
        cum = cums[strand, rows, :]
        cum_t = cum.T
        scores = mm_t(cs[strand, rows, :], bs[strand, rows, :])
        for pair in range(HEADS // 2):
            columns = slice(pair * 128, (pair + 1) * 128)
            x_pair = xdt[strand, rows, columns]
            y_sum = None
            for odd in range(2):
                h = 2 * pair + odd
                own = (lane >= HEAD) if odd else (lane < HEAD)
                x_own = jnp.where(own, x_pair, jnp.zeros((), BF16))
                decay = jnp.exp(
                    jnp.where(mask, cum[:, h : h + 1] - cum_t[h : h + 1, :], -1e30)
                )
                y_new = mm((decay * scores).astype(BF16), x_own)
                y_sum = y_new if y_sum is None else y_sum + y_new
            yi[strand, rows, columns] = y_sum

        @pl.when(i == 0)
        def _():
            pl.semaphore_wait(ready_sem, 3)
            round_a.spread_out()

        return carry

    lax.fori_loop(0, 2 * CHUNKS, within_step, 0)

    loads[4].wait()
    for k in range(BLOCKS):
        here, there = slice(k * Q, (k + 1) * Q), slice(D - (k + 1) * Q, D - k * Q)
        po_flip[:, here] = mm(proj_out[:, there], anti).astype(BF16)
    round_a.collect()

    for n in range(2, 6):
        cot_copy(n).wait_recv()

    def cot_step(k, carry):
        rows = rows_of(k)
        forward = backward = None
        for b in range(BLOCKS):
            cot_t[b, :, rows] = mm_t(ident, cot[b, rows, :]).astype(BF16)
            cot_flip_t[b, :, rows] = mm_t(anti, cot[BLOCKS - 1 - b, rows, :]).astype(BF16)
            columns = slice(b * Q, (b + 1) * Q)
            part = mm_t(cot[b, rows, :], proj_out[:, columns])
            part_flip = mm_t(cot[b, rows, :], po_flip[:, columns])
            forward = part if forward is None else forward + part
            backward = part_flip if backward is None else backward + part_flip
        dos[0, rows, :] = forward.astype(BF16)
        dos[1, rows, :] = backward.astype(BF16)
        return carry

    lax.fori_loop(0, CHUNKS, cot_step, 0)

    def grad_step(i, carry):
        strand, k = i // CHUNKS, lax.rem(i, CHUNKS)
        rows = rows_of(k)
        gate = zs[strand, rows, :]
        dy = dos[strand, rows, :].astype(F32) * (gate * sigmoid(gate))
        dyb[strand, rows, :] = dy.astype(BF16)
        chunk_grad[strand, k] = t_mm(
            cs[strand, rows, :], (dy * e_cums[strand, rows, :]).astype(BF16)
        )
        return carry

    lax.fori_loop(0, 2 * CHUNKS, grad_step, 0)

    for strand in range(2):
        falling = times(strand)[::-1]
        grad = chunk_grad[strand, falling[0]]
        for k in falling[1:]:
            grad = chunk_decay[strand, k, 0:1, :] * grad + chunk_grad[strand, k]
        two_halves(b_msg, slice(16 - 16 * strand, 32 - 16 * strand), grad)
    round_b.to_core().start()

    for strand, state in enumerate(round_a.take()):
        for k in times(strand):
            own_state = chunk_state[strand, k]
            chunk_state[strand, k] = state
            state = chunk_decay[strand, k, 0:1, :] * state + own_state
            chunk_dot[strand, k] = state

    skip_wide = spread(skip[...], e)

    def out_step(i, carry):
        strand, k = i // CHUNKS, lax.rem(i, CHUNKS)
        rows = rows_of(k)
        e_cum = e_cums[strand, rows, :]
        state = chunk_state[strand, k].astype(BF16)
        gate = zs[strand, rows, :]
        d_o = dos[strand, rows, :].astype(F32)
        sig = sigmoid(gate)
        silu = gate * sig
        dy = d_o * silu
        y_part = yi[strand, rows, :] + e_cum * mm(cs[strand, rows, :], state)
        out = y_part + skip_wide * xs[strand, rows, :]
        os[strand, rows, :] = (out * silu).astype(BF16)
        dzs[strand, rows, :] = (d_o * out * (sig + silu * (1.0 - sig))).astype(BF16)
        dcs[strand, rows, :] = mm_t((dy * e_cum).astype(BF16), state)
        dyy[strand, rows, :] = gather_heads(dy * y_part, e)
        yi[strand, rows, :] = skip_wide * dy

        @pl.when(i == 1)
        def _():
            round_b.spread_out()

        return carry

    lax.fori_loop(0, 2 * CHUNKS, out_step, 0)

    class ColumnSum:
        def __init__(self, base, compute, own, part, send, forward, recv):
            self.base, self.compute, self.own, self.part = base, compute, own, part
            self.send, self.forward, self.recv = send, forward, recv

        def copy(self, n):
            src, dst, to = (
                (self.send.at[1, half[0]], self.forward.at[0], 1),
                (self.send.at[1, half[1]], self.forward.at[1], 3),
                (self.send.at[0, half[1]], self.recv.at[0, half[1]], 1),
                (self.send.at[2, half[0]], self.recv.at[1, half[0]], 3),
                (self.send.at[0, half[0]], self.recv.at[0, half[0]], 1),
                (self.send.at[2, half[1]], self.recv.at[1, half[1]], 3),
            )[n]
            return remote(src, dst, self.base + n, x_peer(to))

        def columns(self, r):
            return pl.ds(pl.multiple_of(lax.rem(ch + r, 4) * Q, Q), Q)

        def far(self):
            for n in range(2):
                self.send[1, half[n], :] = self.compute(half[n], self.columns(2)).astype(BF16)
                self.copy(n).start()

        def near(self):
            self.send[0, half[1], :] = self.compute(half[1], self.columns(1)).astype(BF16)
            self.copy(2).start()
            self.send[2, half[0], :] = self.compute(half[0], self.columns(3)).astype(BF16)
            self.copy(3).start()
            self.part[0] = self.compute(half[0], self.columns(1))
            self.part[1] = self.compute(half[1], self.columns(3))

        def middle(self):
            for n, block in ((0, 0), (1, 2)):
                self.copy(n).wait_recv()
                self.send[block, half[n], :] = (
                    self.part[n] + self.forward[n].astype(F32)
                ).astype(BF16)
                self.copy(4 + n).start()

        def own_block(self):
            for n in range(2):
                self.own[half[n], :] = self.compute(half[n], self.columns(0))

        def finish(self, rows):
            return (
                self.own[rows, :]
                + self.recv[0, rows, :].astype(F32)
                + self.recv[1, rows, :].astype(F32)
            )

        def arrived(self):
            for n in range(2, 6):
                self.copy(n).wait_recv()

        def drain(self):
            for n in range(6):
                self.copy(n).wait_send()

    def mix_block(rows, columns):
        return mm(os[0, rows, :], proj_out[:, columns]) + mm(os[1, rows, :], po_flip[:, columns])

    def in_block(rows, columns):
        return (
            mm_t(dxs[0, rows, :], proj_x[columns, :])
            + mm_t(dzs[0, rows, :], proj_z[columns, :])
            + mm_t(dxs[1, rows, :], px_flip[columns, :])
            + mm_t(dzs[1, rows, :], pz_flip[columns, :])
            + mm(ext[rows, :], small[:, columns])
        )

    mix_sum = ColumnSum(S_MIX, mix_block, mix_own, mix_part, mix_send, mix_fwd, mix_recv)
    in_sum = ColumnSum(S_IN, in_block, in_own, in_part, in_send, in_fwd, in_recv)
    mix_sum.far()
    mix_sum.near()

    def g_core_copy(n):
        return remote(g_send.at[n], g_recv.at[n], S_GCORE + n, core_peer)

    def g_peer_copy(n, dz, dy):
        to = lax.rem(z + dz, 4) * 4 + lax.rem(y + dy, 4)
        at = 4 * dz + dy
        return remote(
            h_send.at[n, to], h_recv.at[n, at], S_GPEER + PEERS * n + at, zy_peer(dz, dy)
        )

    def weight_part(n, left, left_flip, right):
        def step(b, carry):
            value = mm(left[b], right[0]) + mm(left_flip[b], right[1])
            value = value.reshape(4, 2, ROWS, W)
            at = pl.ds(pl.multiple_of(b * 4, 4), 4)
            g_own[n, at] = jnp.where(core == 0, value[:, 0], value[:, 1])
            g_send[n, at] = jnp.where(core == 0, value[:, 1], value[:, 0]).astype(BF16)
            return carry

        lax.fori_loop(0, BLOCKS, step, 0)
        g_core_copy(n).start()

    def weight_pair(n):
        g_core_copy(n).wait_recv()

        def pair_sum(i, carry):
            value = g_own[n, i] + g_recv[n, i].astype(F32)
            h_send[n, i] = value.astype(BF16)
            return carry

        lax.fori_loop(0, PEERS, pair_sum, 0)
        h_own[n] = g_own[n, place] + g_recv[n, place].astype(F32)
        for dz, dy in shifts:
            g_peer_copy(n, dz, dy).start()

    weight_part(0, cot_t, cot_flip_t, os)
    weight_part(1, hidden_t, hidden_flip_t, dzs)

    def inner_step(i, carry):
        strand, k = i // CHUNKS, lax.rem(i, CHUNKS)
        rows = rows_of(k)
        mask = order(2 * strand - 1)
        cum = cums[strand, rows, :]
        cum_t = cum.T
        b = bs[strand, rows, :]
        c = cs[strand, rows, :]
        scores = mm_t(b, c)
        for pair in range(HEADS // 2):
            columns = slice(pair * 128, (pair + 1) * 128)
            x_pair, dy_pair = xdt[strand, rows, columns], dyb[strand, rows, columns]
            g_sum = None
            for odd in range(2):
                h = 2 * pair + odd
                own = (lane >= HEAD) if odd else (lane < HEAD)
                dy_own = jnp.where(own, dy_pair, jnp.zeros((), BF16))
                decay = jnp.exp(
                    jnp.where(mask, cum_t[h : h + 1, :] - cum[:, h : h + 1], -1e30)
                )
                cross = mm_t(x_pair, dy_own)
                if h == 0:
                    zacc[...] = decay * cross
                else:
                    zacc[...] += decay * cross
                g_new = mm((decay * scores).astype(BF16), dy_own)
                g_sum = g_new if g_sum is None else g_sum + g_new
            gi[strand, rows, columns] = g_sum
        pairs = zacc[...].astype(BF16)
        dbs[strand, rows, :] = mm(pairs, c)
        dcs[strand, rows, :] += t_mm(pairs, b)

        @pl.when(i == 0)
        def _():
            mix_sum.middle()
            weight_pair(0)

        @pl.when(i == 1)
        def _():
            round_b.collect()

        return carry

    lax.fori_loop(0, 2 * CHUNKS, inner_step, 0)

    mix_sum.own_block()
    weight_pair(1)

    up, down = round_b.take()
    for strand, grad in enumerate((down, up)):
        for k in times(strand)[::-1]:
            own_grad = chunk_grad[strand, k]
            chunk_grad[strand, k] = grad
            chunk_dot[strand, k, 0:8, :] = jnp.broadcast_to(
                jnp.sum(grad * chunk_dot[strand, k], axis=0, keepdims=True), (8, W)
            )
            grad = chunk_decay[strand, k, 0:1, :] * grad + own_grad
    ext[...] = jnp.zeros_like(ext)

    def back_step(k, carry):
        rows = rows_of(k)
        for strand in range(2):
            dt = dts_soft[strand, rows, :]
            e_rest = e_rests[strand, rows, :]
            dt_wide = dt_wides[strand, rows, :]
            grad = chunk_grad[strand, k].astype(BF16)
            x = xs[strand, rows, :]
            gb = gi[strand, rows, :] + e_rest * mm(bs[strand, rows, :], grad)
            dxs[strand, rows, :] = (dt_wide * gb + yi[strand, rows, :]).astype(BF16)
            d_b = dbs[strand, rows, :] + mm_t((x * dt_wide * e_rest).astype(BF16), grad)
            direct = gather_heads(x * gb, e)
            d_cum = dyy[strand, rows, :] - dt * direct
            d_a = running(d_cum, order(2 * strand - 1)) + gather_heads(
                chunk_dot[strand, k, 0:8, :], e
            )[0:1, :]
            d_raw = (direct - rate[...] * d_a) * sigmoid(dts[strand, rows, :])
            at_b, at_c, at_dt = SMALL[strand]
            ext[rows, at_b : at_b + NS] = d_b.astype(BF16)
            ext[rows, at_c : at_c + NS] = dcs[strand, rows, :].astype(BF16)
            ext[rows, at_dt : at_dt + HEADS] = d_raw.astype(BF16)
        return carry

    lax.fori_loop(0, CHUNKS, back_step, 0)

    weight_part(2, hidden_t, hidden_flip_t, dxs)
    in_sum.far()
    weight_pair(2)
    in_sum.near()
    in_sum.middle()
    in_sum.own_block()

    mix_sum.arrived()

    def mix_step(k, carry):
        rows = rows_of(k)
        mine = hidden[rows, pl.ds(pl.multiple_of(ch * Q, Q), Q)].astype(F32)
        block_out[rows, :] = (mine + mix_sum.finish(rows)).astype(BF16)
        return carry

    lax.fori_loop(0, CHUNKS, mix_step, 0)

    def weight_total(n, out):
        total = h_own[n]
        for dz, dy in shifts:
            g_peer_copy(n, dz, dy).wait_recv()
            total = total + h_recv[n, 4 * dz + dy].astype(F32)
        out[...] = total

    weight_total(0, grad_out)
    weight_total(1, grad_z)
    in_sum.arrived()

    def in_step(k, carry):
        rows = rows_of(k)
        grad_hidden[rows, :] = cot[ch, rows, :].astype(F32) + in_sum.finish(rows)
        return carry

    lax.fori_loop(0, CHUNKS, in_step, 0)

    weight_total(2, grad_x)

    for n in range(6):
        cot_copy(n).wait_send()
    round_a.drain()
    round_b.drain()
    mix_sum.drain()
    in_sum.drain()
    for n in range(3):
        g_core_copy(n).wait_send()
        for dz, dy in shifts:
            g_peer_copy(n, dz, dy).wait_send()


def hand_over(*refs):
    sems = refs[10]
    copies = [pltpu.make_async_copy(refs[n], refs[5 + n], sems.at[n]) for n in range(5)]
    for copy in copies:
        copy.start()
    for copy in copies:
        copy.wait()


def shape(*dims, dtype=F32):
    return jax.ShapeDtypeStruct(dims, dtype)


VMEM = pl.BlockSpec(memory_space=pltpu.VMEM)


def body(
    hidden, proj_x, proj_z, proj_b, proj_c, proj_dt, dt_bias, decay_rate, skip_gain, proj_out, cotangent
):
    bias, rate, skip = (v[None, :] for v in (dt_bias, decay_rate, skip_gain))
    vm = pltpu.VMEM
    results = (
        shape(L, Q, dtype=BF16),
        shape(L, Q),
        shape(ROWS, W),
        shape(ROWS, W),
        shape(ROWS, W),
    )
    made = pl.pallas_call(
        block_kernel,
        out_shape=results,
        in_specs=[pl.BlockSpec(memory_space=pl.ANY)] * 5 + [VMEM] * 6,
        out_specs=[VMEM] * 5,
        scratch_shapes=[
            vm((L, D), BF16), vm((D, W), BF16), vm((D, W), BF16), vm((W, D), BF16),
            vm((D, W), BF16), vm((D, W), BF16), vm((W, D), BF16), vm((128, D), BF16),
            vm((BLOCKS, Q, L), BF16), vm((BLOCKS, Q, L), BF16),
            vm((BLOCKS, L, Q), BF16), vm((BLOCKS, Q, L), BF16), vm((BLOCKS, Q, L), BF16),
            vm((2, L, W), F32), vm((2, L, W), F32), vm((2, L, NS), BF16), vm((2, L, NS), BF16),
            vm((2, L, HEADS), F32), vm((2, L, W), BF16), vm((2, L, HEADS), F32),
            vm((2, L, HEADS), F32), vm((2, L, W), F32), vm((2, L, W), F32), vm((2, L, W), F32),
            vm((2, L, W), BF16), vm((2, L, W), BF16), vm((Q, Q), F32),
            vm((2, L, W), F32), vm((2, L, W), F32), vm((2, L, NS), F32), vm((2, L, NS), F32),
            vm((2, L, HEADS), F32),
            vm((L, 128), BF16), vm((2, L, W), BF16), vm((2, L, W), BF16), vm((2, L, W), BF16),
            vm((2, CHUNKS, NS, W), F32), vm((2, CHUNKS, NS, W), F32),
            vm((2, CHUNKS, 8, W), F32), vm((2, CHUNKS, NS, W), F32),
            vm((2, 40, Q), F32), vm((40, Q), F32), vm((2, 24, Q), F32), vm((PEERS, 24, Q), F32),
            vm((32, Q), F32), vm((2, 32, Q), F32),
            vm((2, 32, Q), F32), vm((32, Q), F32), vm((2, 16, Q), F32), vm((PEERS, 16, Q), F32),
            vm((32, Q), F32), vm((2, 32, Q), F32),
            vm((L, Q), F32), vm((2, Q, Q), F32), vm((3, L, Q), BF16), vm((2, Q, Q), BF16),
            vm((2, L, Q), BF16),
            vm((L, Q), F32), vm((2, Q, Q), F32), vm((3, L, Q), BF16), vm((2, Q, Q), BF16),
            vm((2, L, Q), BF16),
            vm((3, PEERS, ROWS, W), F32), vm((3, PEERS, ROWS, W), BF16),
            vm((3, PEERS, ROWS, W), BF16),
            vm((3, ROWS, W), F32), vm((3, PEERS, ROWS, W), BF16),
            vm((3, PEERS, ROWS, W), BF16),
            pltpu.SemaphoreType.DMA((5,)),
            pltpu.SemaphoreType.DMA((S_ALL,)), pltpu.SemaphoreType.DMA((S_ALL,)),
            pltpu.SemaphoreType.REGULAR,
        ],
        compiler_params=pltpu.CompilerParams(
            vmem_limit_bytes=60 * 2**20, collective_id=0, has_side_effects=True
        ),
        name="block",
    )(
        hidden, proj_x, proj_z, proj_out, cotangent,
        proj_b.T, proj_c.T, proj_dt.T, bias, rate, skip,
    )
    *most, grad_out = pl.pallas_call(
        hand_over,
        out_shape=results,
        in_specs=[VMEM] * 5,
        out_specs=[pl.BlockSpec(memory_space=pl.ANY)] * 5,
        scratch_shapes=[pltpu.SemaphoreType.DMA((5,))],
        name="hand_over",
    )(*made)
    return *most, grad_out.T


def solution(mesh):
    return jax.shard_map(
        body,
        mesh=mesh,
        in_specs=(
            P("seq", None),
            P(None, "ch"),
            P(None, "ch"),
            P(),
            P(),
            P(None, "ch"),
            P("ch"),
            P("ch"),
            P("ch"),
            P("ch", None),
            P("seq", "ch"),
        ),
        out_specs=(P("seq", "ch"), P("seq", "ch"), P("seq", "ch"), P("seq", "ch"), P("ch", "seq")),
        check_vma=False,
    )
```

```python
import jax
import jax.numpy as jnp
from jax import lax
from jax.experimental import pallas as pl
from jax.experimental.pallas import tpu as pltpu
from jax.sharding import PartitionSpec as P

L = 512
D = 1024
W = 512
HEADS = 8
HEAD = 64
NS = 16
Q = 256
CHUNKS = L // Q
BLOCKS = D // Q
PEERS = 16
ROWS = 32
F32 = jnp.float32
BF16 = jnp.bfloat16
MESH = pl.DeviceIdType.MESH

LAST = (((1,), (1,)), ((), ()))
FIRST = (((0,), (0,)), ((), ()))

SMALL = ((0, 16, 32), (48, 64, 80))

S_COT, S_MIX, S_IN, S_A, S_B = 0, 6, 12, 18, 36
S_GCORE, S_GPEER = 54, 57
S_ALL = S_GPEER + 3 * 12


def mm(a, b):
    return jnp.dot(a, b, preferred_element_type=F32)


def mm_t(a, b):
    return lax.dot_general(a, b, LAST, preferred_element_type=F32)


def t_mm(a, b):
    return lax.dot_general(a, b, FIRST, preferred_element_type=F32)


def split2(v):
    high = v.astype(BF16)
    return high, (v - high.astype(F32)).astype(BF16)


def split3(v):
    high = v.astype(BF16)
    rest = v - high.astype(F32)
    mid = rest.astype(BF16)
    return high, mid, (rest - mid.astype(F32)).astype(BF16)


def iota(shape, dim):
    return lax.broadcasted_iota(jnp.int32, shape, dim)


def identity():
    return jnp.where(iota((Q, Q), 0) == iota((Q, Q), 1), 1.0, 0.0).astype(BF16)


def anti_identity():
    return jnp.where(iota((Q, Q), 0) + iota((Q, Q), 1) == Q - 1, 1.0, 0.0).astype(BF16)


def spread_matrix():
    head = iota((2 * HEADS, W), 0)
    head = jnp.where(head >= HEADS, head - HEADS, head)
    return jnp.where(iota((2 * HEADS, W), 1) // HEAD == head, 1.0, 0.0).astype(BF16)


def spread(v, e):
    return mm(jnp.concatenate(split2(v), axis=1), e)


def gather_heads(v, e):
    high, low = split2(v)
    return (mm_t(high, e) + mm_t(low, e))[:, 0:HEADS]


def order(sign):
    return (iota((Q, Q), 0) - iota((Q, Q), 1)) * sign >= 0


def running(v, mask):
    ones = jnp.where(mask, 1.0, 0.0).astype(BF16)
    return sum(mm(ones, part) for part in split3(v))


def softplus(v):
    return jnp.maximum(v, 0.0) + jnp.log1p(jnp.exp(-jnp.abs(v)))


def sigmoid(v):
    return 1.0 / (1.0 + jnp.exp(-v))


def rows_of(k):
    return pl.ds(pl.multiple_of(k * Q, Q), Q)


def block_kernel(
    hidden_hbm, proj_x_hbm, proj_z_hbm, proj_out_hbm, cot_hbm,
    proj_b, proj_c, proj_dt, bias, rate, skip,
    block_out, grad_hidden, grad_x, grad_z, grad_out,
    hidden, proj_x, proj_z, proj_out,
    px_flip, pz_flip, po_flip, small, hidden_t, hidden_flip_t, cot, cot_t, cot_flip_t,
    xs, zs, bs, cs, dts, dos, cums, dts_soft, e_cums, e_rests, dt_wides, dyb, xdt, zacc,
    yi, gi, dcs, dbs, dyy, ext, os, dxs, dzs,
    chunk_state, chunk_grad, chunk_decay, chunk_dot,
    a_msg, a_core, a_pair, a_slots, a_back, a_in,
    b_msg, b_core, b_pair, b_slots, b_back, b_in,
    mix_own, mix_part, mix_send, mix_fwd, mix_recv,
    in_own, in_part, in_send, in_fwd, in_recv,
    g_own, g_send, g_recv, h_send, h_recv, t_send, t_recv, t_own,
    load_sem, send_sem, recv_sem, ready_sem,
):
    seq, ch = lax.axis_index("seq"), lax.axis_index("ch")
    core, y, z = lax.rem(seq, 2), lax.rem(seq // 2, 4), seq // 8
    other = 1 - core
    place = z * 4 + y

    def x_peer(k):
        return (seq, lax.rem(ch + k, 4))

    def zy_peer(dz, dy):
        return (lax.rem(z + dz, 4) * 8 + lax.rem(y + dy, 4) * 2 + core, ch)

    core_peer = (seq + 1 - 2 * core, ch)
    shifts = [(k // 4, k % 4) for k in range(1, PEERS)]

    def remote(src, dst, sem, device):
        return pltpu.make_async_remote_copy(
            src_ref=src,
            dst_ref=dst,
            send_sem=send_sem.at[sem],
            recv_sem=recv_sem.at[sem],
            device_id=device,
            device_id_type=MESH,
        )

    loads = [
        pltpu.make_async_copy(src, dst, load_sem.at[n])
        for n, (src, dst) in enumerate(
            (
                (cot_hbm, cot.at[ch]),
                (hidden_hbm, hidden),
                (proj_x_hbm, proj_x),
                (proj_z_hbm, proj_z),
                (proj_out_hbm, proj_out),
            )
        )
    ]
    barrier = pltpu.get_barrier_semaphore()
    y_peers = [zy_peer(0, k) for k in range(1, 4)]
    for device in [x_peer(1), x_peer(3), core_peer] + y_peers + [zy_peer(k, 0) for k in range(1, 4)]:
        pl.semaphore_signal(barrier, inc=1, device_id=device, device_id_type=MESH)
    for load in loads:
        load.start()
    anti = anti_identity()
    e = spread_matrix()
    small[...] = jnp.zeros_like(small)
    for weight, at in zip((proj_b, proj_c, proj_dt), range(3)):
        n = weight.shape[0]
        small[SMALL[0][at] : SMALL[0][at] + n, :] = weight[...]
        for k in range(BLOCKS):
            here, there = slice(k * Q, (k + 1) * Q), slice(D - (k + 1) * Q, D - k * Q)
            small[SMALL[1][at] : SMALL[1][at] + n, here] = mm(weight[:, there], anti).astype(BF16)
    loads[0].wait()
    pl.semaphore_wait(barrier, 9)
    half = [slice(0, Q), slice(Q, L)]
    before, after = lax.rem(ch + 3, 4), lax.rem(ch + 1, 4)

    def cot_copy(n):
        block, rows, to = (
            (ch, half[0], 1), (ch, half[1], 3), (ch, half[1], 1), (ch, half[0], 3),
            (before, half[0], 1), (after, half[1], 3),
        )[n]
        return remote(cot.at[block, rows], cot.at[block, rows], S_COT + n, x_peer(to))

    for n in range(4):
        cot_copy(n).start()
    for device in y_peers:
        pl.semaphore_signal(ready_sem, inc=1, device_id=device, device_id_type=MESH)

    loads[1].wait()
    ident = identity()
    for k in range(BLOCKS):
        here, there = slice(k * Q, (k + 1) * Q), slice(D - (k + 1) * Q, D - k * Q)
        hidden_t[k] = mm_t(ident, hidden[:, here]).astype(BF16)
        hidden_flip_t[k] = mm_t(anti, hidden[:, there]).astype(BF16)
    for load, source, flip in ((loads[2], proj_x, px_flip), (loads[3], proj_z, pz_flip)):
        load.wait()
        for k in range(BLOCKS):
            here, there = slice(k * Q, (k + 1) * Q), slice(D - (k + 1) * Q, D - k * Q)
            flip[here, :] = mm(anti, source[there, :]).astype(BF16)

    def project_step(k, carry):
        rows = rows_of(k)
        u = hidden[rows, :]
        xs[0, rows, :] = mm(u, proj_x[...])
        zs[0, rows, :] = mm(u, proj_z[...])
        xs[1, rows, :] = mm(u, px_flip[...])
        zs[1, rows, :] = mm(u, pz_flip[...])
        narrow = mm_t(u, small[...])
        for strand in range(2):
            at_b, at_c, at_dt = SMALL[strand]
            bs[strand, rows, :] = narrow[:, at_b : at_b + NS].astype(BF16)
            cs[strand, rows, :] = narrow[:, at_c : at_c + NS].astype(BF16)
            dts[strand, rows, :] = narrow[:, at_dt : at_dt + HEADS] + bias[...]
        return carry

    lax.fori_loop(0, CHUNKS, project_step, 0)

    def state_step(i, carry):
        strand, k = i // CHUNKS, lax.rem(i, CHUNKS)
        rows = rows_of(k)
        dt = softplus(dts[strand, rows, :])
        a = -rate[...] * dt
        cum = running(a, order(1 - 2 * strand))
        total = jnp.sum(a, axis=0, keepdims=True)
        cums[strand, rows, :] = cum
        dts_soft[strand, rows, :] = dt
        e_rest = spread(jnp.exp(total - cum), e)
        dt_wide = spread(dt, e)
        e_cums[strand, rows, :] = spread(jnp.exp(cum), e)
        e_rests[strand, rows, :] = e_rest
        dt_wides[strand, rows, :] = dt_wide
        xd = xs[strand, rows, :] * dt_wide
        xdt[strand, rows, :] = xd.astype(BF16)
        chunk_state[strand, k] = t_mm(bs[strand, rows, :], (xd * e_rest).astype(BF16))
        chunk_decay[strand, k] = jnp.broadcast_to(jnp.exp(spread(total, e)), (8, W))
        return carry

    lax.fori_loop(0, 2 * CHUNKS, state_step, 0)

    for n in range(2):
        cot_copy(n).wait_recv()
        cot_copy(4 + n).start()

    def times(strand):
        return list(range(CHUNKS)) if strand == 0 else list(range(CHUNKS))[::-1]

    def two_halves(dst, rows, value):
        dst[0, rows, :] = value[:, 0:Q]
        dst[1, rows, :] = value[:, Q:]

    decays = []
    for strand in range(2):
        state, decay = chunk_state[strand, times(strand)[0]], chunk_decay[strand, 0]
        for k in times(strand)[1:]:
            state = chunk_decay[strand, k, 0:1, :] * state + chunk_state[strand, k]
        for k in range(1, CHUNKS):
            decay = decay * chunk_decay[strand, k]
        two_halves(a_msg, slice(16 * strand, 16 * strand + NS), state)
        decays.append(decay)
    two_halves(a_msg, slice(32, 40), jnp.where(iota((8, W), 0) == 0, decays[0], decays[1]))

    zero = jnp.zeros((NS, Q), F32)
    a_slots[place] = jnp.zeros_like(a_slots[0])
    b_slots[place] = jnp.zeros_like(b_slots[0])

    class Exchange:
        def __init__(self, base, msg, from_core, pair, slots, back, result, swap):
            self.base, self.msg, self.from_core, self.pair = base, msg, from_core, pair
            self.slots, self.back, self.result, self.swap = slots, back, result, swap

        def to_core(self):
            return remote(self.msg.at[other], self.from_core, self.base, core_peer)

        def to_place(self, dz, dy):
            to = lax.rem(z + dz, 4) * 4 + lax.rem(y + dy, 4)
            kind = jnp.where(to > place, 0, 1)
            return remote(
                self.pair.at[kind], self.slots.at[place], self.base + 4 * dz + dy, zy_peer(dz, dy)
            )

        def to_back(self):
            return remote(self.back, self.result.at[core], self.base + PEERS, core_peer)

        def decay(self, ref, strand):
            return ref[strand : strand + 1, :]

        def both(self):
            mine = (
                self.msg[core, 0:16, :], self.msg[core, 16:32, :],
                a_msg[core, 32 + self.swap : 33 + self.swap, :],
                a_msg[core, 33 - self.swap : 34 - self.swap, :],
            )
            theirs = (
                self.from_core[0:16, :], self.from_core[16:32, :],
                a_core[32 + self.swap : 33 + self.swap, :],
                a_core[33 - self.swap : 34 - self.swap, :],
            )
            return mine, theirs

        def spread_out(self):
            self.to_core().wait_recv()
            mine, theirs = self.both()
            first = [jnp.where(core == 0, m, t) for m, t in zip(mine, theirs)]
            second = [jnp.where(core == 0, t, m) for m, t in zip(mine, theirs)]
            up = second[2] * first[0] + second[0]
            down = first[3] * second[1] + first[1]
            self.pair[0, 0:16, :] = up
            self.pair[1, 0:16, :] = down
            if not self.swap:
                product = jnp.where(
                    iota((8, Q), 0) == 0,
                    jnp.broadcast_to(first[2] * second[2], (8, Q)),
                    jnp.broadcast_to(first[3] * second[3], (8, Q)),
                )
                self.pair[0, 16:24, :] = product
                self.pair[1, 16:24, :] = product
            for dz, dy in shifts:
                self.to_place(dz, dy).start()

        def collect(self):
            for dz, dy in shifts:
                self.to_place(dz, dy).wait_recv()
            up = down = zero
            for j in range(PEERS):
                r = PEERS - 1 - j
                decay_up = a_slots[j, 16 + self.swap : 17 + self.swap, :]
                decay_down = a_slots[r, 17 - self.swap : 18 - self.swap, :]
                up = jnp.where(j < place, decay_up * up + self.slots[j, 0:16, :], up)
                down = jnp.where(r > place, decay_down * down + self.slots[r, 0:16, :], down)
            mine, theirs = self.both()
            self.back[0:16, :] = jnp.where(core == 0, mine[2] * up + mine[0], up)
            self.back[16:32, :] = jnp.where(core == 1, mine[3] * down + mine[1], down)
            self.to_back().start()
            self.result[core, 0:16, :] = jnp.where(core == 1, theirs[2] * up + theirs[0], up)
            self.result[core, 16:32, :] = jnp.where(core == 0, theirs[3] * down + theirs[1], down)

        def take(self):
            self.to_back().wait_recv()
            return [
                jnp.concatenate([self.result[0, rows, :], self.result[1, rows, :]], axis=1)
                for rows in (slice(0, 16), slice(16, 32))
            ]

        def drain(self):
            self.to_core().wait_send()
            self.to_back().wait_send()
            for dz, dy in shifts:
                self.to_place(dz, dy).wait_send()

    round_a = Exchange(S_A, a_msg, a_core, a_pair, a_slots, a_back, a_in, 0)
    round_b = Exchange(S_B, b_msg, b_core, b_pair, b_slots, b_back, b_in, 1)
    round_a.to_core().start()

    lane = iota((Q, 128), 1)

    def within_step(i, carry):
        strand, k = i // CHUNKS, lax.rem(i, CHUNKS)
        rows = rows_of(k)
        mask = order(1 - 2 * strand)
        cum = cums[strand, rows, :]
        cum_t = cum.T
        scores = mm_t(cs[strand, rows, :], bs[strand, rows, :])
        for pair in range(HEADS // 2):
            columns = slice(pair * 128, (pair + 1) * 128)
            x_pair = xdt[strand, rows, columns]
            y_sum = None
            for odd in range(2):
                h = 2 * pair + odd
                own = (lane >= HEAD) if odd else (lane < HEAD)
                x_own = jnp.where(own, x_pair, jnp.zeros((), BF16))
                decay = jnp.exp(
                    jnp.where(mask, cum[:, h : h + 1] - cum_t[h : h + 1, :], -1e30)
                )
                y_new = mm((decay * scores).astype(BF16), x_own)
                y_sum = y_new if y_sum is None else y_sum + y_new
            yi[strand, rows, columns] = y_sum

        @pl.when(i == 0)
        def _():
            pl.semaphore_wait(ready_sem, 3)
            round_a.spread_out()

        return carry

    lax.fori_loop(0, 2 * CHUNKS, within_step, 0)

    loads[4].wait()
    for k in range(BLOCKS):
        here, there = slice(k * Q, (k + 1) * Q), slice(D - (k + 1) * Q, D - k * Q)
        po_flip[:, here] = mm(proj_out[:, there], anti).astype(BF16)

    for n in range(2, 6):
        cot_copy(n).wait_recv()

    def cot_step(k, carry):
        rows = rows_of(k)
        forward = backward = None
        for b in range(BLOCKS):
            cot_t[b, :, rows] = mm_t(ident, cot[b, rows, :]).astype(BF16)
            cot_flip_t[b, :, rows] = mm_t(anti, cot[BLOCKS - 1 - b, rows, :]).astype(BF16)
            columns = slice(b * Q, (b + 1) * Q)
            part = mm_t(cot[b, rows, :], proj_out[:, columns])
            part_flip = mm_t(cot[b, rows, :], po_flip[:, columns])
            forward = part if forward is None else forward + part
            backward = part_flip if backward is None else backward + part_flip
        dos[0, rows, :] = forward.astype(BF16)
        dos[1, rows, :] = backward.astype(BF16)
        return carry

    lax.fori_loop(0, CHUNKS, cot_step, 0)

    def grad_step(i, carry):
        strand, k = i // CHUNKS, lax.rem(i, CHUNKS)
        rows = rows_of(k)
        gate = zs[strand, rows, :]
        dy = dos[strand, rows, :].astype(F32) * (gate * sigmoid(gate))
        dyb[strand, rows, :] = dy.astype(BF16)
        chunk_grad[strand, k] = t_mm(
            cs[strand, rows, :], (dy * e_cums[strand, rows, :]).astype(BF16)
        )
        return carry

    lax.fori_loop(0, 2 * CHUNKS, grad_step, 0)

    for strand in range(2):
        falling = times(strand)[::-1]
        grad = chunk_grad[strand, falling[0]]
        for k in falling[1:]:
            grad = chunk_decay[strand, k, 0:1, :] * grad + chunk_grad[strand, k]
        two_halves(b_msg, slice(16 - 16 * strand, 32 - 16 * strand), grad)
    round_b.to_core().start()

    round_a.collect()
    for strand, state in enumerate(round_a.take()):
        for k in times(strand):
            own_state = chunk_state[strand, k]
            chunk_state[strand, k] = state
            state = chunk_decay[strand, k, 0:1, :] * state + own_state
            chunk_dot[strand, k] = state

    skip_wide = spread(skip[...], e)

    def out_step(i, carry):
        strand, k = i // CHUNKS, lax.rem(i, CHUNKS)
        rows = rows_of(k)
        e_cum = e_cums[strand, rows, :]
        state = chunk_state[strand, k].astype(BF16)
        gate = zs[strand, rows, :]
        d_o = dos[strand, rows, :].astype(F32)
        sig = sigmoid(gate)
        silu = gate * sig
        dy = d_o * silu
        y_part = yi[strand, rows, :] + e_cum * mm(cs[strand, rows, :], state)
        out = y_part + skip_wide * xs[strand, rows, :]
        os[strand, rows, :] = (out * silu).astype(BF16)
        dzs[strand, rows, :] = (d_o * out * (sig + silu * (1.0 - sig))).astype(BF16)
        dcs[strand, rows, :] = mm_t((dy * e_cum).astype(BF16), state)
        dyy[strand, rows, :] = gather_heads(dy * y_part, e)
        yi[strand, rows, :] = skip_wide * dy

        @pl.when(i == 1)
        def _():
            round_b.spread_out()

        return carry

    lax.fori_loop(0, 2 * CHUNKS, out_step, 0)

    class ColumnSum:
        def __init__(self, base, compute, own, part, send, forward, recv):
            self.base, self.compute, self.own, self.part = base, compute, own, part
            self.send, self.forward, self.recv = send, forward, recv

        def copy(self, n):
            src, dst, to = (
                (self.send.at[1, half[0]], self.forward.at[0], 1),
                (self.send.at[1, half[1]], self.forward.at[1], 3),
                (self.send.at[0, half[1]], self.recv.at[0, half[1]], 1),
                (self.send.at[2, half[0]], self.recv.at[1, half[0]], 3),
                (self.send.at[0, half[0]], self.recv.at[0, half[0]], 1),
                (self.send.at[2, half[1]], self.recv.at[1, half[1]], 3),
            )[n]
            return remote(src, dst, self.base + n, x_peer(to))

        def columns(self, r):
            return pl.ds(pl.multiple_of(lax.rem(ch + r, 4) * Q, Q), Q)

        def far(self):
            for n in range(2):
                self.send[1, half[n], :] = self.compute(half[n], self.columns(2)).astype(BF16)
                self.copy(n).start()

        def near(self):
            self.send[0, half[1], :] = self.compute(half[1], self.columns(1)).astype(BF16)
            self.copy(2).start()
            self.send[2, half[0], :] = self.compute(half[0], self.columns(3)).astype(BF16)
            self.copy(3).start()
            self.part[0] = self.compute(half[0], self.columns(1))
            self.part[1] = self.compute(half[1], self.columns(3))

        def middle(self):
            for n, block in ((0, 0), (1, 2)):
                self.copy(n).wait_recv()
                self.send[block, half[n], :] = (
                    self.part[n] + self.forward[n].astype(F32)
                ).astype(BF16)
                self.copy(4 + n).start()

        def own_block(self):
            for n in range(2):
                self.own[half[n], :] = self.compute(half[n], self.columns(0))

        def finish(self, rows):
            return (
                self.own[rows, :]
                + self.recv[0, rows, :].astype(F32)
                + self.recv[1, rows, :].astype(F32)
            )

        def arrived(self):
            for n in range(2, 6):
                self.copy(n).wait_recv()

        def drain(self):
            for n in range(6):
                self.copy(n).wait_send()

    def mix_block(rows, columns):
        return mm(os[0, rows, :], proj_out[:, columns]) + mm(os[1, rows, :], po_flip[:, columns])

    def in_block(rows, columns):
        return (
            mm_t(dxs[0, rows, :], proj_x[columns, :])
            + mm_t(dzs[0, rows, :], proj_z[columns, :])
            + mm_t(dxs[1, rows, :], px_flip[columns, :])
            + mm_t(dzs[1, rows, :], pz_flip[columns, :])
            + mm(ext[rows, :], small[:, columns])
        )

    mix_sum = ColumnSum(S_MIX, mix_block, mix_own, mix_part, mix_send, mix_fwd, mix_recv)
    in_sum = ColumnSum(S_IN, in_block, in_own, in_part, in_send, in_fwd, in_recv)

    def g_core_copy(n):
        return remote(g_send.at[n], g_recv.at[n], S_GCORE + n, core_peer)

    def g_copy(n, at):
        stage, over_z, k = at // 6, at % 6 // 3, at % 3 + 1
        peer = zy_peer(k, 0) if over_z != stage else zy_peer(0, k)
        if stage:
            src, dst = t_send.at[n, over_z, k - 1], t_recv.at[n, over_z, k - 1]
        elif over_z:
            src, dst = h_send.at[n, lax.rem(z + k, 4), :, :, Q:W], h_recv.at[n, 1, k - 1]
        else:
            src, dst = h_send.at[n, :, lax.rem(y + k, 4), :, 0:Q], h_recv.at[n, 0, k - 1]
        return remote(src, dst, S_GPEER + 12 * n + at, peer)

    def weight_part(n, left, left_flip, right):
        def step(b, carry):
            value = mm(left[b], right[0]) + mm(left_flip[b], right[1])
            value = value.reshape(4, 2, ROWS, W)
            g_own[n, b] = jnp.where(core == 0, value[:, 0], value[:, 1])
            g_send[n, b] = jnp.where(core == 0, value[:, 1], value[:, 0]).astype(BF16)
            return carry

        lax.fori_loop(0, BLOCKS, step, 0)
        g_core_copy(n).start()

    def weight_pair(n):
        g_core_copy(n).wait_recv()

        def pair_sum(i, carry):
            at = (n, i // 4, lax.rem(i, 4))
            value = g_own[at] + g_recv[at].astype(F32)
            g_own[at] = value
            h_send[at] = value.astype(BF16)
            return carry

        lax.fori_loop(0, PEERS, pair_sum, 0)
        for at in range(6):
            g_copy(n, at).start()

    def weight_middle(n):
        for at in range(6):
            g_copy(n, at).wait_recv()
        for r in (1, 2, 3, 0):
            to_z, to_y = lax.rem(z + r, 4), lax.rem(y + r, 4)
            first, second = g_own[n, to_z, y, :, 0:Q], g_own[n, z, to_y, :, Q:W]
            for k in range(3):
                first = first + h_recv[n, 0, k, to_z].astype(F32)
                second = second + h_recv[n, 1, k, to_y].astype(F32)
            if r:
                t_send[n, 0, r - 1] = first.astype(BF16)
                t_send[n, 1, r - 1] = second.astype(BF16)
                g_copy(n, 6 + r - 1).start()
                g_copy(n, 9 + r - 1).start()
            else:
                t_own[n, 0] = first
                t_own[n, 1] = second

    def weight_total(n, out):
        for at in range(6, 12):
            g_copy(n, at).wait_recv()
        for side in range(2):
            total = t_own[n, side]
            for k in range(3):
                total = total + t_recv[n, side, k].astype(F32)
            out[:, side * Q : (side + 1) * Q] = total

    weight_part(0, cot_t, cot_flip_t, os)
    mix_sum.far()
    mix_sum.near()
    weight_part(1, hidden_t, hidden_flip_t, dzs)
    weight_pair(0)

    def inner_step(i, carry):
        strand, k = i // CHUNKS, lax.rem(i, CHUNKS)
        rows = rows_of(k)
        mask = order(2 * strand - 1)
        cum = cums[strand, rows, :]
        cum_t = cum.T
        b = bs[strand, rows, :]
        c = cs[strand, rows, :]
        scores = mm_t(b, c)
        for pair in range(HEADS // 2):
            columns = slice(pair * 128, (pair + 1) * 128)
            x_pair, dy_pair = xdt[strand, rows, columns], dyb[strand, rows, columns]
            g_sum = None
            for odd in range(2):
                h = 2 * pair + odd
                own = (lane >= HEAD) if odd else (lane < HEAD)
                dy_own = jnp.where(own, dy_pair, jnp.zeros((), BF16))
                decay = jnp.exp(
                    jnp.where(mask, cum_t[h : h + 1, :] - cum[:, h : h + 1], -1e30)
                )
                cross = mm_t(x_pair, dy_own)
                if h == 0:
                    zacc[...] = decay * cross
                else:
                    zacc[...] += decay * cross
                g_new = mm((decay * scores).astype(BF16), dy_own)
                g_sum = g_new if g_sum is None else g_sum + g_new
            gi[strand, rows, columns] = g_sum
        pairs = zacc[...].astype(BF16)
        dbs[strand, rows, :] = mm(pairs, c)
        dcs[strand, rows, :] += t_mm(pairs, b)

        @pl.when(i == 0)
        def _():
            mix_sum.middle()
            weight_pair(1)

        @pl.when(i == 1)
        def _():
            round_b.collect()

        @pl.when(i == 2)
        def _():
            weight_middle(0)

        return carry

    lax.fori_loop(0, 2 * CHUNKS, inner_step, 0)

    mix_sum.own_block()
    weight_middle(1)

    up, down = round_b.take()
    for strand, grad in enumerate((down, up)):
        for k in times(strand)[::-1]:
            own_grad = chunk_grad[strand, k]
            chunk_grad[strand, k] = grad
            chunk_dot[strand, k, 0:8, :] = jnp.broadcast_to(
                jnp.sum(grad * chunk_dot[strand, k], axis=0, keepdims=True), (8, W)
            )
            grad = chunk_decay[strand, k, 0:1, :] * grad + own_grad
    ext[...] = jnp.zeros_like(ext)

    def back_step(k, carry):
        rows = rows_of(k)
        for strand in range(2):
            dt = dts_soft[strand, rows, :]
            e_rest = e_rests[strand, rows, :]
            dt_wide = dt_wides[strand, rows, :]
            grad = chunk_grad[strand, k].astype(BF16)
            x = xs[strand, rows, :]
            gb = gi[strand, rows, :] + e_rest * mm(bs[strand, rows, :], grad)
            dxs[strand, rows, :] = (dt_wide * gb + yi[strand, rows, :]).astype(BF16)
            d_b = dbs[strand, rows, :] + mm_t((x * dt_wide * e_rest).astype(BF16), grad)
            direct = gather_heads(x * gb, e)
            d_cum = dyy[strand, rows, :] - dt * direct
            d_a = running(d_cum, order(2 * strand - 1)) + gather_heads(
                chunk_dot[strand, k, 0:8, :], e
            )[0:1, :]
            d_raw = (direct - rate[...] * d_a) * sigmoid(dts[strand, rows, :])
            at_b, at_c, at_dt = SMALL[strand]
            ext[rows, at_b : at_b + NS] = d_b.astype(BF16)
            ext[rows, at_c : at_c + NS] = dcs[strand, rows, :].astype(BF16)
            ext[rows, at_dt : at_dt + HEADS] = d_raw.astype(BF16)
        return carry

    lax.fori_loop(0, CHUNKS, back_step, 0)

    weight_part(2, hidden_t, hidden_flip_t, dxs)
    in_sum.far()
    weight_pair(2)
    in_sum.near()
    in_sum.middle()
    in_sum.own_block()
    weight_middle(2)

    mix_sum.arrived()

    def mix_step(k, carry):
        rows = rows_of(k)
        mine = hidden[rows, pl.ds(pl.multiple_of(ch * Q, Q), Q)].astype(F32)
        block_out[rows, :] = (mine + mix_sum.finish(rows)).astype(BF16)
        return carry

    lax.fori_loop(0, CHUNKS, mix_step, 0)

    weight_total(0, grad_out)
    weight_total(1, grad_z)
    in_sum.arrived()

    def in_step(k, carry):
        rows = rows_of(k)
        grad_hidden[rows, :] = cot[ch, rows, :].astype(F32) + in_sum.finish(rows)
        return carry

    lax.fori_loop(0, CHUNKS, in_step, 0)

    weight_total(2, grad_x)

    for n in range(6):
        cot_copy(n).wait_send()
    round_a.drain()
    round_b.drain()
    mix_sum.drain()
    in_sum.drain()
    for n in range(3):
        g_core_copy(n).wait_send()
        for at in range(12):
            g_copy(n, at).wait_send()


def hand_over(*refs):
    sems = refs[10]
    copies = [pltpu.make_async_copy(refs[n], refs[5 + n], sems.at[n]) for n in range(5)]
    for copy in copies:
        copy.start()
    for copy in copies:
        copy.wait()


def shape(*dims, dtype=F32):
    return jax.ShapeDtypeStruct(dims, dtype)


VMEM = pl.BlockSpec(memory_space=pltpu.VMEM)


def body(
    hidden, proj_x, proj_z, proj_b, proj_c, proj_dt, dt_bias, decay_rate, skip_gain, proj_out, cotangent
):
    bias, rate, skip = (v[None, :] for v in (dt_bias, decay_rate, skip_gain))
    vm = pltpu.VMEM
    results = (
        shape(L, Q, dtype=BF16),
        shape(L, Q),
        shape(ROWS, W),
        shape(ROWS, W),
        shape(ROWS, W),
    )
    made = pl.pallas_call(
        block_kernel,
        out_shape=results,
        in_specs=[pl.BlockSpec(memory_space=pl.ANY)] * 5 + [VMEM] * 6,
        out_specs=[VMEM] * 5,
        scratch_shapes=[
            vm((L, D), BF16), vm((D, W), BF16), vm((D, W), BF16), vm((W, D), BF16),
            vm((D, W), BF16), vm((D, W), BF16), vm((W, D), BF16), vm((128, D), BF16),
            vm((BLOCKS, Q, L), BF16), vm((BLOCKS, Q, L), BF16),
            vm((BLOCKS, L, Q), BF16), vm((BLOCKS, Q, L), BF16), vm((BLOCKS, Q, L), BF16),
            vm((2, L, W), F32), vm((2, L, W), F32), vm((2, L, NS), BF16), vm((2, L, NS), BF16),
            vm((2, L, HEADS), F32), vm((2, L, W), BF16), vm((2, L, HEADS), F32),
            vm((2, L, HEADS), F32), vm((2, L, W), F32), vm((2, L, W), F32), vm((2, L, W), F32),
            vm((2, L, W), BF16), vm((2, L, W), BF16), vm((Q, Q), F32),
            vm((2, L, W), F32), vm((2, L, W), F32), vm((2, L, NS), F32), vm((2, L, NS), F32),
            vm((2, L, HEADS), F32),
            vm((L, 128), BF16), vm((2, L, W), BF16), vm((2, L, W), BF16), vm((2, L, W), BF16),
            vm((2, CHUNKS, NS, W), F32), vm((2, CHUNKS, NS, W), F32),
            vm((2, CHUNKS, 8, W), F32), vm((2, CHUNKS, NS, W), F32),
            vm((2, 40, Q), F32), vm((40, Q), F32), vm((2, 24, Q), F32), vm((PEERS, 24, Q), F32),
            vm((32, Q), F32), vm((2, 32, Q), F32),
            vm((2, 32, Q), F32), vm((32, Q), F32), vm((2, 16, Q), F32), vm((PEERS, 16, Q), F32),
            vm((32, Q), F32), vm((2, 32, Q), F32),
            vm((L, Q), F32), vm((2, Q, Q), F32), vm((3, L, Q), BF16), vm((2, Q, Q), BF16),
            vm((2, L, Q), BF16),
            vm((L, Q), F32), vm((2, Q, Q), F32), vm((3, L, Q), BF16), vm((2, Q, Q), BF16),
            vm((2, L, Q), BF16),
            vm((3, 4, 4, ROWS, W), F32), vm((3, 4, 4, ROWS, W), BF16),
            vm((3, 4, 4, ROWS, W), BF16), vm((3, 4, 4, ROWS, W), BF16),
            vm((3, 2, 3, 4, ROWS, Q), BF16), vm((3, 2, 3, ROWS, Q), BF16),
            vm((3, 2, 3, ROWS, Q), BF16), vm((3, 2, ROWS, Q), F32),
            pltpu.SemaphoreType.DMA((5,)),
            pltpu.SemaphoreType.DMA((S_ALL,)), pltpu.SemaphoreType.DMA((S_ALL,)),
            pltpu.SemaphoreType.REGULAR,
        ],
        compiler_params=pltpu.CompilerParams(
            vmem_limit_bytes=60 * 2**20, collective_id=0, has_side_effects=True
        ),
        name="block",
    )(
        hidden, proj_x, proj_z, proj_out, cotangent,
        proj_b.T, proj_c.T, proj_dt.T, bias, rate, skip,
    )
    *most, grad_out = pl.pallas_call(
        hand_over,
        out_shape=results,
        in_specs=[VMEM] * 5,
        out_specs=[pl.BlockSpec(memory_space=pl.ANY)] * 5,
        scratch_shapes=[pltpu.SemaphoreType.DMA((5,))],
        name="hand_over",
    )(*made)
    return *most, grad_out.T


def solution(mesh):
    return jax.shard_map(
        body,
        mesh=mesh,
        in_specs=(
            P("seq", None),
            P(None, "ch"),
            P(None, "ch"),
            P(),
            P(),
            P(None, "ch"),
            P("ch"),
            P("ch"),
            P("ch"),
            P("ch", None),
            P("seq", "ch"),
        ),
        out_specs=(P("seq", "ch"), P("seq", "ch"), P("seq", "ch"), P("seq", "ch"), P("ch", "seq")),
        check_vma=False,
    )
```

```python
import jax
import jax.numpy as jnp
from jax import lax
from jax.experimental import pallas as pl
from jax.experimental.pallas import tpu as pltpu
from jax.sharding import PartitionSpec as P

L = 512
D = 1024
W = 512
HEADS = 8
HEAD = 64
NS = 16
Q = 256
CHUNKS = L // Q
BLOCKS = D // Q
PEERS = 16
ROWS = 32
F32 = jnp.float32
BF16 = jnp.bfloat16
MESH = pl.DeviceIdType.MESH

LAST = (((1,), (1,)), ((), ()))
FIRST = (((0,), (0,)), ((), ()))

SMALL = ((0, 16, 32), (48, 64, 80))

S_COT, S_MIX, S_IN, S_A, S_B = 0, 6, 12, 18, 36
S_GCORE, S_GPEER = 54, 57
S_LAST = S_GPEER + 2 * 12
S_ALL = S_LAST + 16


def mm(a, b):
    return jnp.dot(a, b, preferred_element_type=F32)


def mm_t(a, b):
    return lax.dot_general(a, b, LAST, preferred_element_type=F32)


def t_mm(a, b):
    return lax.dot_general(a, b, FIRST, preferred_element_type=F32)


def split2(v):
    high = v.astype(BF16)
    return high, (v - high.astype(F32)).astype(BF16)


def split3(v):
    high = v.astype(BF16)
    rest = v - high.astype(F32)
    mid = rest.astype(BF16)
    return high, mid, (rest - mid.astype(F32)).astype(BF16)


def iota(shape, dim):
    return lax.broadcasted_iota(jnp.int32, shape, dim)


def identity():
    return jnp.where(iota((Q, Q), 0) == iota((Q, Q), 1), 1.0, 0.0).astype(BF16)


def anti_identity():
    return jnp.where(iota((Q, Q), 0) + iota((Q, Q), 1) == Q - 1, 1.0, 0.0).astype(BF16)


def spread_matrix():
    head = iota((2 * HEADS, W), 0)
    head = jnp.where(head >= HEADS, head - HEADS, head)
    return jnp.where(iota((2 * HEADS, W), 1) // HEAD == head, 1.0, 0.0).astype(BF16)


def spread(v, e):
    return mm(jnp.concatenate(split2(v), axis=1), e)


def gather_heads(v, e):
    high, low = split2(v)
    return (mm_t(high, e) + mm_t(low, e))[:, 0:HEADS]


def order(sign):
    return (iota((Q, Q), 0) - iota((Q, Q), 1)) * sign >= 0


def running(v, mask):
    ones = jnp.where(mask, 1.0, 0.0).astype(BF16)
    return sum(mm(ones, part) for part in split3(v))


def softplus(v):
    return jnp.maximum(v, 0.0) + jnp.log1p(jnp.exp(-jnp.abs(v)))


def sigmoid(v):
    return 1.0 / (1.0 + jnp.exp(-v))


def rows_of(k):
    return pl.ds(pl.multiple_of(k * Q, Q), Q)


def block_kernel(
    hidden_hbm, proj_x_hbm, proj_z_hbm, proj_out_hbm, cot_hbm,
    proj_b_hbm, proj_c_hbm, proj_dt_hbm, bias_hbm, rate_hbm, skip_hbm,
    block_out, grad_hidden, grad_x, grad_z, grad_out,
    hidden, proj_x, proj_z, proj_out, proj_b, proj_c, proj_dt, bias, rate, skip,
    px_flip, pz_flip, po_flip, small, hidden_t, hidden_flip_t, cot, cot_t, cot_flip_t,
    xs, zs, bs, cs, dts, dos, cums, dts_soft, e_cums, e_rests, dt_wides, dyb, xdt, zacc,
    yi, gi, dcs, dbs, dyy, ext, os, dxs, dzs,
    chunk_state, chunk_grad, chunk_decay, chunk_dot,
    a_msg, a_core, a_pair, a_slots, a_back, a_in,
    b_msg, b_core, b_pair, b_slots, b_back, b_in,
    mix_own, mix_part, mix_send, mix_fwd, mix_recv,
    in_own, in_part, in_send, in_fwd, in_recv,
    g_own, g_send, g_recv, h_send, h_recv, t_send, t_recv, t_own, last_recv,
    load_sem, send_sem, recv_sem, ready_sem,
):
    seq, ch = lax.axis_index("seq"), lax.axis_index("ch")
    core, y, z = lax.rem(seq, 2), lax.rem(seq // 2, 4), seq // 8
    other = 1 - core
    place = z * 4 + y

    def x_peer(k):
        return (seq, lax.rem(ch + k, 4))

    def zy_peer(dz, dy):
        return (lax.rem(z + dz, 4) * 8 + lax.rem(y + dy, 4) * 2 + core, ch)

    core_peer = (seq + 1 - 2 * core, ch)
    shifts = [(k // 4, k % 4) for k in range(1, PEERS)]

    def remote(src, dst, sem, device):
        return pltpu.make_async_remote_copy(
            src_ref=src,
            dst_ref=dst,
            send_sem=send_sem.at[sem],
            recv_sem=recv_sem.at[sem],
            device_id=device,
            device_id_type=MESH,
        )

    loads = [
        pltpu.make_async_copy(src, dst, load_sem.at[n])
        for n, (src, dst) in enumerate(
            (
                (cot_hbm, cot.at[ch]),
                (hidden_hbm, hidden),
                (proj_x_hbm, proj_x),
                (proj_z_hbm, proj_z),
                (proj_out_hbm, proj_out),
                (proj_b_hbm, proj_b),
                (proj_c_hbm, proj_c),
                (proj_dt_hbm, proj_dt),
                (bias_hbm, bias),
                (rate_hbm, rate),
                (skip_hbm, skip),
            )
        )
    ]
    barrier = pltpu.get_barrier_semaphore()
    near = [zy_peer(0, 1), zy_peer(0, 3), zy_peer(1, 0), zy_peer(3, 0)]
    for device in [x_peer(1), x_peer(3), core_peer] + near:
        pl.semaphore_signal(barrier, inc=1, device_id=device, device_id_type=MESH)
    for load in loads[:1] + loads[5:] + loads[1:5]:
        load.start()
    anti = anti_identity()
    e = spread_matrix()
    loads[0].wait()
    pl.semaphore_wait(barrier, 7)
    half = [slice(0, Q), slice(Q, L)]
    before, after = lax.rem(ch + 3, 4), lax.rem(ch + 1, 4)

    def cot_copy(n):
        block, rows, to = (
            (ch, half[0], 1), (ch, half[1], 3), (ch, half[1], 1), (ch, half[0], 3),
            (before, half[0], 1), (after, half[1], 3),
        )[n]
        return remote(cot.at[block, rows], cot.at[block, rows], S_COT + n, x_peer(to))

    for n in range(4):
        cot_copy(n).start()
    def vouch(n):
        if n:
            pl.semaphore_wait(ready_sem.at[n - 1], 4)
        if n < 3:
            for device in near:
                pl.semaphore_signal(
                    ready_sem.at[n], inc=1, device_id=device, device_id_type=MESH
                )

    vouch(0)
    for load in loads[5:]:
        load.wait()
    small[...] = jnp.zeros_like(small)
    for weight, at in zip((proj_b, proj_c, proj_dt), range(3)):
        n = weight.shape[0]
        small[SMALL[0][at] : SMALL[0][at] + n, :] = weight[...]
        for k in range(BLOCKS):
            here, there = slice(k * Q, (k + 1) * Q), slice(D - (k + 1) * Q, D - k * Q)
            small[SMALL[1][at] : SMALL[1][at] + n, here] = mm(weight[:, there], anti).astype(BF16)
    loads[1].wait()
    ident = identity()
    for k in range(BLOCKS):
        here, there = slice(k * Q, (k + 1) * Q), slice(D - (k + 1) * Q, D - k * Q)
        hidden_t[k] = mm_t(ident, hidden[:, here]).astype(BF16)
        hidden_flip_t[k] = mm_t(anti, hidden[:, there]).astype(BF16)
    for load, source, flip in ((loads[2], proj_x, px_flip), (loads[3], proj_z, pz_flip)):
        load.wait()
        for k in range(BLOCKS):
            here, there = slice(k * Q, (k + 1) * Q), slice(D - (k + 1) * Q, D - k * Q)
            flip[here, :] = mm(anti, source[there, :]).astype(BF16)

    def project_step(k, carry):
        rows = rows_of(k)
        u = hidden[rows, :]
        xs[0, rows, :] = mm(u, proj_x[...])
        zs[0, rows, :] = mm(u, proj_z[...])
        xs[1, rows, :] = mm(u, px_flip[...])
        zs[1, rows, :] = mm(u, pz_flip[...])
        narrow = mm_t(u, small[...])
        for strand in range(2):
            at_b, at_c, at_dt = SMALL[strand]
            bs[strand, rows, :] = narrow[:, at_b : at_b + NS].astype(BF16)
            cs[strand, rows, :] = narrow[:, at_c : at_c + NS].astype(BF16)
            dts[strand, rows, :] = narrow[:, at_dt : at_dt + HEADS] + bias[...]
        return carry

    lax.fori_loop(0, CHUNKS, project_step, 0)
    vouch(1)

    def state_step(i, carry):
        strand, k = i // CHUNKS, lax.rem(i, CHUNKS)
        rows = rows_of(k)
        dt = softplus(dts[strand, rows, :])
        a = -rate[...] * dt
        cum = running(a, order(1 - 2 * strand))
        total = jnp.sum(a, axis=0, keepdims=True)
        cums[strand, rows, :] = cum
        dts_soft[strand, rows, :] = dt
        e_rest = spread(jnp.exp(total - cum), e)
        dt_wide = spread(dt, e)
        e_cums[strand, rows, :] = spread(jnp.exp(cum), e)
        e_rests[strand, rows, :] = e_rest
        dt_wides[strand, rows, :] = dt_wide
        xd = xs[strand, rows, :] * dt_wide
        xdt[strand, rows, :] = xd.astype(BF16)
        chunk_state[strand, k] = t_mm(bs[strand, rows, :], (xd * e_rest).astype(BF16))
        chunk_decay[strand, k] = jnp.broadcast_to(jnp.exp(spread(total, e)), (8, W))
        return carry

    lax.fori_loop(0, 2 * CHUNKS, state_step, 0)
    vouch(2)

    for n in range(2):
        cot_copy(n).wait_recv()
        cot_copy(4 + n).start()

    def times(strand):
        return list(range(CHUNKS)) if strand == 0 else list(range(CHUNKS))[::-1]

    def two_halves(dst, rows, value):
        dst[0, rows, :] = value[:, 0:Q]
        dst[1, rows, :] = value[:, Q:]

    decays = []
    for strand in range(2):
        state, decay = chunk_state[strand, times(strand)[0]], chunk_decay[strand, 0]
        for k in times(strand)[1:]:
            state = chunk_decay[strand, k, 0:1, :] * state + chunk_state[strand, k]
        for k in range(1, CHUNKS):
            decay = decay * chunk_decay[strand, k]
        two_halves(a_msg, slice(16 * strand, 16 * strand + NS), state)
        decays.append(decay)
    two_halves(a_msg, slice(32, 40), jnp.where(iota((8, W), 0) == 0, decays[0], decays[1]))

    zero = jnp.zeros((NS, Q), F32)
    a_slots[place] = jnp.zeros_like(a_slots[0])
    b_slots[place] = jnp.zeros_like(b_slots[0])

    class Exchange:
        def __init__(self, base, msg, from_core, pair, slots, back, result, swap):
            self.base, self.msg, self.from_core, self.pair = base, msg, from_core, pair
            self.slots, self.back, self.result, self.swap = slots, back, result, swap

        def to_core(self):
            return remote(self.msg.at[other], self.from_core, self.base, core_peer)

        def to_place(self, dz, dy):
            to = lax.rem(z + dz, 4) * 4 + lax.rem(y + dy, 4)
            kind = jnp.where(to > place, 0, 1)
            return remote(
                self.pair.at[kind], self.slots.at[place], self.base + 4 * dz + dy, zy_peer(dz, dy)
            )

        def to_back(self):
            return remote(self.back, self.result.at[core], self.base + PEERS, core_peer)

        def decay(self, ref, strand):
            return ref[strand : strand + 1, :]

        def both(self):
            mine = (
                self.msg[core, 0:16, :], self.msg[core, 16:32, :],
                a_msg[core, 32 + self.swap : 33 + self.swap, :],
                a_msg[core, 33 - self.swap : 34 - self.swap, :],
            )
            theirs = (
                self.from_core[0:16, :], self.from_core[16:32, :],
                a_core[32 + self.swap : 33 + self.swap, :],
                a_core[33 - self.swap : 34 - self.swap, :],
            )
            return mine, theirs

        def spread_out(self):
            self.to_core().wait_recv()
            mine, theirs = self.both()
            first = [jnp.where(core == 0, m, t) for m, t in zip(mine, theirs)]
            second = [jnp.where(core == 0, t, m) for m, t in zip(mine, theirs)]
            up = second[2] * first[0] + second[0]
            down = first[3] * second[1] + first[1]
            self.pair[0, 0:16, :] = up
            self.pair[1, 0:16, :] = down
            if not self.swap:
                product = jnp.where(
                    iota((8, Q), 0) == 0,
                    jnp.broadcast_to(first[2] * second[2], (8, Q)),
                    jnp.broadcast_to(first[3] * second[3], (8, Q)),
                )
                self.pair[0, 16:24, :] = product
                self.pair[1, 16:24, :] = product
            for dz, dy in shifts:
                self.to_place(dz, dy).start()

        def collect(self):
            for dz, dy in shifts:
                self.to_place(dz, dy).wait_recv()
            up = down = zero
            for j in range(PEERS):
                r = PEERS - 1 - j
                decay_up = a_slots[j, 16 + self.swap : 17 + self.swap, :]
                decay_down = a_slots[r, 17 - self.swap : 18 - self.swap, :]
                up = jnp.where(j < place, decay_up * up + self.slots[j, 0:16, :], up)
                down = jnp.where(r > place, decay_down * down + self.slots[r, 0:16, :], down)
            mine, theirs = self.both()
            self.back[0:16, :] = jnp.where(core == 0, mine[2] * up + mine[0], up)
            self.back[16:32, :] = jnp.where(core == 1, mine[3] * down + mine[1], down)
            self.to_back().start()
            self.result[core, 0:16, :] = jnp.where(core == 1, theirs[2] * up + theirs[0], up)
            self.result[core, 16:32, :] = jnp.where(core == 0, theirs[3] * down + theirs[1], down)

        def take(self):
            self.to_back().wait_recv()
            return [
                jnp.concatenate([self.result[0, rows, :], self.result[1, rows, :]], axis=1)
                for rows in (slice(0, 16), slice(16, 32))
            ]

        def drain(self):
            self.to_core().wait_send()
            self.to_back().wait_send()
            for dz, dy in shifts:
                self.to_place(dz, dy).wait_send()

    round_a = Exchange(S_A, a_msg, a_core, a_pair, a_slots, a_back, a_in, 0)
    round_b = Exchange(S_B, b_msg, b_core, b_pair, b_slots, b_back, b_in, 1)
    round_a.to_core().start()

    lane = iota((Q, 128), 1)

    def within_step(i, carry):
        strand, k = i // CHUNKS, lax.rem(i, CHUNKS)
        rows = rows_of(k)
        mask = order(1 - 2 * strand)
        cum = cums[strand, rows, :]
        cum_t = cum.T
        scores = mm_t(cs[strand, rows, :], bs[strand, rows, :])
        for pair in range(HEADS // 2):
            columns = slice(pair * 128, (pair + 1) * 128)
            x_pair = xdt[strand, rows, columns]
            y_sum = None
            for odd in range(2):
                h = 2 * pair + odd
                own = (lane >= HEAD) if odd else (lane < HEAD)
                x_own = jnp.where(own, x_pair, jnp.zeros((), BF16))
                decay = jnp.exp(
                    jnp.where(mask, cum[:, h : h + 1] - cum_t[h : h + 1, :], -1e30)
                )
                y_new = mm((decay * scores).astype(BF16), x_own)
                y_sum = y_new if y_sum is None else y_sum + y_new
            yi[strand, rows, columns] = y_sum

        @pl.when(i == 0)
        def _():
            vouch(3)
            round_a.spread_out()

        return carry

    lax.fori_loop(0, 2 * CHUNKS, within_step, 0)

    loads[4].wait()
    for k in range(BLOCKS):
        here, there = slice(k * Q, (k + 1) * Q), slice(D - (k + 1) * Q, D - k * Q)
        po_flip[:, here] = mm(proj_out[:, there], anti).astype(BF16)

    def cot_block(c, rows):
        block = cot[c, rows, :]
        cot_t[c, :, rows] = mm_t(ident, block).astype(BF16)
        cot_flip_t[BLOCKS - 1 - c, :, rows] = mm_t(anti, block).astype(BF16)
        columns = pl.ds(pl.multiple_of(c * Q, Q), Q)
        return mm_t(block, proj_out[:, columns]), mm_t(block, po_flip[:, columns])

    def first_step(k, carry):
        rows = rows_of(k)
        parts = [cot_block(c, rows) for c in (ch, before, after)]
        for strand in range(2):
            gi[strand, rows, :] = sum(part[strand] for part in parts)
        return carry

    def last_step(k, carry):
        rows = rows_of(k)
        parts = cot_block(lax.rem(ch + 2, 4), rows)
        for strand in range(2):
            dos[strand, rows, :] = (gi[strand, rows, :] + parts[strand]).astype(BF16)
        return carry

    for n in range(2, 4):
        cot_copy(n).wait_recv()
    lax.fori_loop(0, CHUNKS, first_step, 0)
    for n in range(4, 6):
        cot_copy(n).wait_recv()
    lax.fori_loop(0, CHUNKS, last_step, 0)

    def grad_step(i, carry):
        strand, k = i // CHUNKS, lax.rem(i, CHUNKS)
        rows = rows_of(k)
        gate = zs[strand, rows, :]
        dy = dos[strand, rows, :].astype(F32) * (gate * sigmoid(gate))
        dyb[strand, rows, :] = dy.astype(BF16)
        chunk_grad[strand, k] = t_mm(
            cs[strand, rows, :], (dy * e_cums[strand, rows, :]).astype(BF16)
        )
        return carry

    lax.fori_loop(0, 2 * CHUNKS, grad_step, 0)

    for strand in range(2):
        falling = times(strand)[::-1]
        grad = chunk_grad[strand, falling[0]]
        for k in falling[1:]:
            grad = chunk_decay[strand, k, 0:1, :] * grad + chunk_grad[strand, k]
        two_halves(b_msg, slice(16 - 16 * strand, 32 - 16 * strand), grad)
    round_b.to_core().start()

    round_a.collect()
    for strand, state in enumerate(round_a.take()):
        for k in times(strand):
            own_state = chunk_state[strand, k]
            chunk_state[strand, k] = state
            state = chunk_decay[strand, k, 0:1, :] * state + own_state
            chunk_dot[strand, k] = state

    skip_wide = spread(skip[...], e)

    def out_step(i, carry):
        strand, k = i // CHUNKS, lax.rem(i, CHUNKS)
        rows = rows_of(k)
        e_cum = e_cums[strand, rows, :]
        state = chunk_state[strand, k].astype(BF16)
        gate = zs[strand, rows, :]
        d_o = dos[strand, rows, :].astype(F32)
        sig = sigmoid(gate)
        silu = gate * sig
        dy = d_o * silu
        y_part = yi[strand, rows, :] + e_cum * mm(cs[strand, rows, :], state)
        out = y_part + skip_wide * xs[strand, rows, :]
        os[strand, rows, :] = (out * silu).astype(BF16)
        dzs[strand, rows, :] = (d_o * out * (sig + silu * (1.0 - sig))).astype(BF16)
        dcs[strand, rows, :] = mm_t((dy * e_cum).astype(BF16), state)
        dyy[strand, rows, :] = gather_heads(dy * y_part, e)
        yi[strand, rows, :] = skip_wide * dy

        @pl.when(i == 1)
        def _():
            round_b.spread_out()

        return carry

    lax.fori_loop(0, 2 * CHUNKS, out_step, 0)

    class ColumnSum:
        def __init__(self, base, compute, own, part, send, forward, recv):
            self.base, self.compute, self.own, self.part = base, compute, own, part
            self.send, self.forward, self.recv = send, forward, recv

        def copy(self, n):
            src, dst, to = (
                (self.send.at[1, half[0]], self.forward.at[0], 1),
                (self.send.at[1, half[1]], self.forward.at[1], 3),
                (self.send.at[0, half[1]], self.recv.at[0, half[1]], 1),
                (self.send.at[2, half[0]], self.recv.at[1, half[0]], 3),
                (self.send.at[0, half[0]], self.recv.at[0, half[0]], 1),
                (self.send.at[2, half[1]], self.recv.at[1, half[1]], 3),
            )[n]
            return remote(src, dst, self.base + n, x_peer(to))

        def columns(self, r):
            return pl.ds(pl.multiple_of(lax.rem(ch + r, 4) * Q, Q), Q)

        def far(self):
            for n in range(2):
                self.send[1, half[n], :] = self.compute(half[n], self.columns(2)).astype(BF16)
                self.copy(n).start()

        def near(self):
            self.send[0, half[1], :] = self.compute(half[1], self.columns(1)).astype(BF16)
            self.copy(2).start()
            self.send[2, half[0], :] = self.compute(half[0], self.columns(3)).astype(BF16)
            self.copy(3).start()
            self.part[0] = self.compute(half[0], self.columns(1))
            self.part[1] = self.compute(half[1], self.columns(3))

        def middle(self):
            for n, block in ((0, 0), (1, 2)):
                self.copy(n).wait_recv()
                self.send[block, half[n], :] = (
                    self.part[n] + self.forward[n].astype(F32)
                ).astype(BF16)
                self.copy(4 + n).start()

        def own_block(self):
            for n in range(2):
                self.own[half[n], :] = self.compute(half[n], self.columns(0))

        def finish(self, rows):
            return (
                self.own[rows, :]
                + self.recv[0, rows, :].astype(F32)
                + self.recv[1, rows, :].astype(F32)
            )

        def arrived(self):
            for n in range(2, 6):
                self.copy(n).wait_recv()

        def drain(self):
            for n in range(6):
                self.copy(n).wait_send()

    def mix_block(rows, columns):
        return mm(os[0, rows, :], proj_out[:, columns]) + mm(os[1, rows, :], po_flip[:, columns])

    def in_block(rows, columns):
        return (
            mm_t(dxs[0, rows, :], proj_x[columns, :])
            + mm_t(dzs[0, rows, :], proj_z[columns, :])
            + mm_t(dxs[1, rows, :], px_flip[columns, :])
            + mm_t(dzs[1, rows, :], pz_flip[columns, :])
            + mm(ext[rows, :], small[:, columns])
        )

    mix_sum = ColumnSum(S_MIX, mix_block, mix_own, mix_part, mix_send, mix_fwd, mix_recv)
    in_sum = ColumnSum(S_IN, in_block, in_own, in_part, in_send, in_fwd, in_recv)

    def g_core_copy(n):
        return remote(g_send.at[n], g_recv.at[n], S_GCORE + n, core_peer)

    def g_copy(n, at):
        stage, over_z, k = at // 6, at % 6 // 3, at % 3 + 1
        peer = zy_peer(k, 0) if over_z != stage else zy_peer(0, k)
        if stage:
            src, dst = t_send.at[n, over_z, k - 1], t_recv.at[n, over_z, k - 1]
        elif over_z:
            src, dst = h_send.at[n, lax.rem(z + k, 4), :, :, Q:W], h_recv.at[n, 1, k - 1]
        else:
            src, dst = h_send.at[n, :, lax.rem(y + k, 4), :, 0:Q], h_recv.at[n, 0, k - 1]
        return remote(src, dst, S_GPEER + 12 * n + at, peer)

    def x_copy(dz, dy):
        at = 4 * dz + dy
        return remote(
            h_send.at[2, lax.rem(z + dz, 4), lax.rem(y + dy, 4)], last_recv.at[at],
            S_LAST + at, zy_peer(dz, dy),
        )

    def weight_part(n, left, left_flip, right):
        def step(b, carry):
            value = mm(left[b], right[0]) + mm(left_flip[b], right[1])
            value = value.reshape(4, 2, ROWS, W)
            g_own[n, b] = jnp.where(core == 0, value[:, 0], value[:, 1])
            g_send[n, b] = jnp.where(core == 0, value[:, 1], value[:, 0]).astype(BF16)
            return carry

        lax.fori_loop(0, BLOCKS, step, 0)
        g_core_copy(n).start()

    def weight_pair(n):
        g_core_copy(n).wait_recv()

        def pair_sum(i, carry):
            at = (n, i // 4, lax.rem(i, 4))
            value = g_own[at] + g_recv[at].astype(F32)
            g_own[at] = value
            h_send[at] = value.astype(BF16)
            return carry

        lax.fori_loop(0, PEERS, pair_sum, 0)
        if n == 2:
            for dz, dy in shifts:
                x_copy(dz, dy).start()
        else:
            for at in range(6):
                g_copy(n, at).start()

    def weight_middle(n):
        for at in range(6):
            g_copy(n, at).wait_recv()
        for r in (1, 2, 3, 0):
            to_z, to_y = lax.rem(z + r, 4), lax.rem(y + r, 4)
            first, second = g_own[n, to_z, y, :, 0:Q], g_own[n, z, to_y, :, Q:W]
            for k in range(3):
                first = first + h_recv[n, 0, k, to_z].astype(F32)
                second = second + h_recv[n, 1, k, to_y].astype(F32)
            if r:
                t_send[n, 0, r - 1] = first.astype(BF16)
                t_send[n, 1, r - 1] = second.astype(BF16)
                g_copy(n, 6 + r - 1).start()
                g_copy(n, 9 + r - 1).start()
            else:
                t_own[n, 0] = first
                t_own[n, 1] = second

    def weight_total(n, out):
        for at in range(6, 12):
            g_copy(n, at).wait_recv()
        for side in range(2):
            total = t_own[n, side]
            for k in range(3):
                total = total + t_recv[n, side, k].astype(F32)
            out[:, side * Q : (side + 1) * Q] = total

    weight_part(0, cot_t, cot_flip_t, os)
    mix_sum.far()
    mix_sum.near()
    weight_part(1, hidden_t, hidden_flip_t, dzs)
    weight_pair(0)

    def inner_step(i, carry):
        strand, k = i // CHUNKS, lax.rem(i, CHUNKS)
        rows = rows_of(k)
        mask = order(2 * strand - 1)
        cum = cums[strand, rows, :]
        cum_t = cum.T
        b = bs[strand, rows, :]
        c = cs[strand, rows, :]
        scores = mm_t(b, c)
        for pair in range(HEADS // 2):
            columns = slice(pair * 128, (pair + 1) * 128)
            x_pair, dy_pair = xdt[strand, rows, columns], dyb[strand, rows, columns]
            g_sum = None
            for odd in range(2):
                h = 2 * pair + odd
                own = (lane >= HEAD) if odd else (lane < HEAD)
                dy_own = jnp.where(own, dy_pair, jnp.zeros((), BF16))
                decay = jnp.exp(
                    jnp.where(mask, cum_t[h : h + 1, :] - cum[:, h : h + 1], -1e30)
                )
                cross = mm_t(x_pair, dy_own)
                if h == 0:
                    zacc[...] = decay * cross
                else:
                    zacc[...] += decay * cross
                g_new = mm((decay * scores).astype(BF16), dy_own)
                g_sum = g_new if g_sum is None else g_sum + g_new
            gi[strand, rows, columns] = g_sum
        pairs = zacc[...].astype(BF16)
        dbs[strand, rows, :] = mm(pairs, c)
        dcs[strand, rows, :] += t_mm(pairs, b)

        @pl.when(i == 0)
        def _():
            mix_sum.middle()
            weight_pair(1)

        @pl.when(i == 1)
        def _():
            round_b.collect()

        @pl.when(i == 2)
        def _():
            weight_middle(0)

        return carry

    lax.fori_loop(0, 2 * CHUNKS, inner_step, 0)

    mix_sum.own_block()
    weight_middle(1)

    up, down = round_b.take()
    for strand, grad in enumerate((down, up)):
        for k in times(strand)[::-1]:
            own_grad = chunk_grad[strand, k]
            chunk_grad[strand, k] = grad
            chunk_dot[strand, k, 0:8, :] = jnp.broadcast_to(
                jnp.sum(grad * chunk_dot[strand, k], axis=0, keepdims=True), (8, W)
            )
            grad = chunk_decay[strand, k, 0:1, :] * grad + own_grad
    ext[...] = jnp.zeros_like(ext)

    def back_step(k, carry):
        rows = rows_of(k)
        for strand in range(2):
            dt = dts_soft[strand, rows, :]
            e_rest = e_rests[strand, rows, :]
            dt_wide = dt_wides[strand, rows, :]
            grad = chunk_grad[strand, k].astype(BF16)
            x = xs[strand, rows, :]
            gb = gi[strand, rows, :] + e_rest * mm(bs[strand, rows, :], grad)
            dxs[strand, rows, :] = (dt_wide * gb + yi[strand, rows, :]).astype(BF16)
            d_b = dbs[strand, rows, :] + mm_t((x * dt_wide * e_rest).astype(BF16), grad)
            direct = gather_heads(x * gb, e)
            d_cum = dyy[strand, rows, :] - dt * direct
            d_a = running(d_cum, order(2 * strand - 1)) + gather_heads(
                chunk_dot[strand, k, 0:8, :], e
            )[0:1, :]
            d_raw = (direct - rate[...] * d_a) * sigmoid(dts[strand, rows, :])
            at_b, at_c, at_dt = SMALL[strand]
            ext[rows, at_b : at_b + NS] = d_b.astype(BF16)
            ext[rows, at_c : at_c + NS] = dcs[strand, rows, :].astype(BF16)
            ext[rows, at_dt : at_dt + HEADS] = d_raw.astype(BF16)
        return carry

    lax.fori_loop(0, CHUNKS, back_step, 0)

    weight_part(2, hidden_t, hidden_flip_t, dxs)
    in_sum.far()
    weight_pair(2)
    in_sum.near()
    in_sum.middle()
    in_sum.own_block()

    mix_sum.arrived()

    def mix_step(k, carry):
        rows = rows_of(k)
        mine = hidden[rows, pl.ds(pl.multiple_of(ch * Q, Q), Q)].astype(F32)
        block_out[rows, :] = (mine + mix_sum.finish(rows)).astype(BF16)
        return carry

    lax.fori_loop(0, CHUNKS, mix_step, 0)

    weight_total(0, grad_out)
    weight_total(1, grad_z)
    in_sum.arrived()

    def in_step(k, carry):
        rows = rows_of(k)
        grad_hidden[rows, :] = cot[ch, rows, :].astype(F32) + in_sum.finish(rows)
        return carry

    lax.fori_loop(0, CHUNKS, in_step, 0)

    total = g_own[2, z, y]
    for dz, dy in shifts:
        x_copy(dz, dy).wait_recv()
        total = total + last_recv[4 * dz + dy].astype(F32)
    grad_x[...] = total

    for n in range(6):
        cot_copy(n).wait_send()
    round_a.drain()
    round_b.drain()
    mix_sum.drain()
    in_sum.drain()
    for n in range(3):
        g_core_copy(n).wait_send()
    for at in range(12):
        g_copy(0, at).wait_send()
        g_copy(1, at).wait_send()
    for dz, dy in shifts:
        x_copy(dz, dy).wait_send()


def hand_over(*refs):
    sems = refs[10]
    copies = [pltpu.make_async_copy(refs[n], refs[5 + n], sems.at[n]) for n in range(5)]
    for copy in copies:
        copy.start()
    for copy in copies:
        copy.wait()


def shape(*dims, dtype=F32):
    return jax.ShapeDtypeStruct(dims, dtype)


VMEM = pl.BlockSpec(memory_space=pltpu.VMEM)


def body(
    hidden, proj_x, proj_z, proj_b, proj_c, proj_dt, dt_bias, decay_rate, skip_gain, proj_out, cotangent
):
    bias, rate, skip = (v[None, :] for v in (dt_bias, decay_rate, skip_gain))
    vm = pltpu.VMEM
    results = (
        shape(L, Q, dtype=BF16),
        shape(L, Q),
        shape(ROWS, W),
        shape(ROWS, W),
        shape(ROWS, W),
    )
    made = pl.pallas_call(
        block_kernel,
        out_shape=results,
        in_specs=[pl.BlockSpec(memory_space=pl.ANY)] * 11,
        out_specs=[VMEM] * 5,
        scratch_shapes=[
            vm((L, D), BF16), vm((D, W), BF16), vm((D, W), BF16), vm((W, D), BF16),
            vm((NS, D), BF16), vm((NS, D), BF16), vm((HEADS, D), BF16),
            vm((1, HEADS), F32), vm((1, HEADS), F32), vm((1, HEADS), F32),
            vm((D, W), BF16), vm((D, W), BF16), vm((W, D), BF16), vm((128, D), BF16),
            vm((BLOCKS, Q, L), BF16), vm((BLOCKS, Q, L), BF16),
            vm((BLOCKS, L, Q), BF16), vm((BLOCKS, Q, L), BF16), vm((BLOCKS, Q, L), BF16),
            vm((2, L, W), F32), vm((2, L, W), F32), vm((2, L, NS), BF16), vm((2, L, NS), BF16),
            vm((2, L, HEADS), F32), vm((2, L, W), BF16), vm((2, L, HEADS), F32),
            vm((2, L, HEADS), F32), vm((2, L, W), F32), vm((2, L, W), F32), vm((2, L, W), F32),
            vm((2, L, W), BF16), vm((2, L, W), BF16), vm((Q, Q), F32),
            vm((2, L, W), F32), vm((2, L, W), F32), vm((2, L, NS), F32), vm((2, L, NS), F32),
            vm((2, L, HEADS), F32),
            vm((L, 128), BF16), vm((2, L, W), BF16), vm((2, L, W), BF16), vm((2, L, W), BF16),
            vm((2, CHUNKS, NS, W), F32), vm((2, CHUNKS, NS, W), F32),
            vm((2, CHUNKS, 8, W), F32), vm((2, CHUNKS, NS, W), F32),
            vm((2, 40, Q), F32), vm((40, Q), F32), vm((2, 24, Q), F32), vm((PEERS, 24, Q), F32),
            vm((32, Q), F32), vm((2, 32, Q), F32),
            vm((2, 32, Q), F32), vm((32, Q), F32), vm((2, 16, Q), F32), vm((PEERS, 16, Q), F32),
            vm((32, Q), F32), vm((2, 32, Q), F32),
            vm((L, Q), F32), vm((2, Q, Q), F32), vm((3, L, Q), BF16), vm((2, Q, Q), BF16),
            vm((2, L, Q), BF16),
            vm((L, Q), F32), vm((2, Q, Q), F32), vm((3, L, Q), BF16), vm((2, Q, Q), BF16),
            vm((2, L, Q), BF16),
            vm((3, 4, 4, ROWS, W), F32), vm((3, 4, 4, ROWS, W), BF16),
            vm((3, 4, 4, ROWS, W), BF16), vm((3, 4, 4, ROWS, W), BF16),
            vm((2, 2, 3, 4, ROWS, Q), BF16), vm((2, 2, 3, ROWS, Q), BF16),
            vm((2, 2, 3, ROWS, Q), BF16), vm((2, 2, ROWS, Q), F32), vm((PEERS, ROWS, W), BF16),
            pltpu.SemaphoreType.DMA((11,)),
            pltpu.SemaphoreType.DMA((S_ALL,)), pltpu.SemaphoreType.DMA((S_ALL,)),
            pltpu.SemaphoreType.REGULAR((3,)),
        ],
        compiler_params=pltpu.CompilerParams(
            vmem_limit_bytes=60 * 2**20, collective_id=0, has_side_effects=True
        ),
        name="block",
    )(
        hidden, proj_x, proj_z, proj_out, cotangent,
        proj_b.T, proj_c.T, proj_dt.T, bias, rate, skip,
    )
    *most, grad_out = pl.pallas_call(
        hand_over,
        out_shape=results,
        in_specs=[VMEM] * 5,
        out_specs=[pl.BlockSpec(memory_space=pl.ANY)] * 5,
        scratch_shapes=[pltpu.SemaphoreType.DMA((5,))],
        name="hand_over",
    )(*made)
    return *most, grad_out.T


def solution(mesh):
    return jax.shard_map(
        body,
        mesh=mesh,
        in_specs=(
            P("seq", None),
            P(None, "ch"),
            P(None, "ch"),
            P(),
            P(),
            P(None, "ch"),
            P("ch"),
            P("ch"),
            P("ch"),
            P("ch", None),
            P("seq", "ch"),
        ),
        out_specs=(P("seq", "ch"), P("seq", "ch"), P("seq", "ch"), P("seq", "ch"), P("ch", "seq")),
        check_vma=False,
    )
```

```python
import jax
import jax.numpy as jnp
from jax import lax
from jax.experimental import pallas as pl
from jax.experimental.pallas import tpu as pltpu
from jax.sharding import PartitionSpec as P

L = 512
D = 1024
W = 512
HEADS = 8
HEAD = 64
NS = 16
Q = 256
CHUNKS = L // Q
BLOCKS = D // Q
PEERS = 16
ROWS = 32
F32 = jnp.float32
BF16 = jnp.bfloat16
MESH = pl.DeviceIdType.MESH

LAST = (((1,), (1,)), ((), ()))
FIRST = (((0,), (0,)), ((), ()))

SMALL = ((0, 16, 32), (48, 64, 80))

S_COT, S_MIX, S_IN, S_A, S_B = 0, 6, 12, 18, 36
S_GCORE, S_GPEER = 54, 57
S_LAST = S_GPEER + 2 * 12
S_ALL = S_LAST + 16


def mm(a, b):
    return jnp.dot(a, b, preferred_element_type=F32)


def mm_t(a, b):
    return lax.dot_general(a, b, LAST, preferred_element_type=F32)


def t_mm(a, b):
    return lax.dot_general(a, b, FIRST, preferred_element_type=F32)


def split2(v):
    high = v.astype(BF16)
    return high, (v - high.astype(F32)).astype(BF16)


def split3(v):
    high = v.astype(BF16)
    rest = v - high.astype(F32)
    mid = rest.astype(BF16)
    return high, mid, (rest - mid.astype(F32)).astype(BF16)


def iota(shape, dim):
    return lax.broadcasted_iota(jnp.int32, shape, dim)


def identity():
    return jnp.where(iota((Q, Q), 0) == iota((Q, Q), 1), 1.0, 0.0).astype(BF16)


def anti_identity():
    return jnp.where(iota((Q, Q), 0) + iota((Q, Q), 1) == Q - 1, 1.0, 0.0).astype(BF16)


def spread_matrix():
    head = iota((2 * HEADS, W), 0)
    head = jnp.where(head >= HEADS, head - HEADS, head)
    return jnp.where(iota((2 * HEADS, W), 1) // HEAD == head, 1.0, 0.0).astype(BF16)


def spread(v, e):
    return mm(jnp.concatenate(split2(v), axis=1), e)


def gather_heads(v, e):
    high, low = split2(v)
    return (mm_t(high, e) + mm_t(low, e))[:, 0:HEADS]


def order(sign):
    return (iota((Q, Q), 0) - iota((Q, Q), 1)) * sign >= 0


def running(v, mask):
    ones = jnp.where(mask, 1.0, 0.0).astype(BF16)
    return sum(mm(ones, part) for part in split3(v))


def softplus(v):
    return jnp.maximum(v, 0.0) + jnp.log1p(jnp.exp(-jnp.abs(v)))


def sigmoid(v):
    return 1.0 / (1.0 + jnp.exp(-v))


def rows_of(k):
    return pl.ds(pl.multiple_of(k * Q, Q), Q)


def block_kernel(
    hidden_hbm, proj_x_hbm, proj_z_hbm, proj_out_hbm, cot_hbm,
    proj_b_hbm, proj_c_hbm, proj_dt_hbm, bias_hbm, rate_hbm, skip_hbm,
    block_out, grad_hidden, grad_x, grad_z, grad_out,
    hidden, proj_x, proj_z, proj_out, proj_b, proj_c, proj_dt, bias, rate, skip,
    px_flip, pz_flip, po_flip, small, hidden_t, hidden_flip_t, cot, cot_t, cot_flip_t,
    xs, zs, bs, cs, dts, dos, cums, dts_soft, e_cums, e_rests, dt_wides, dyb, xdt, zacc, kept_decay,
    yi, dcs, dbs, dyy, ext, os, dzs,
    chunk_state, chunk_grad, chunk_decay, chunk_dot,
    a_msg, a_core, a_pair, a_slots, a_back, a_in,
    b_msg, b_core, b_pair, b_slots, b_back, b_in,
    mix_own, mix_part, mix_send, mix_fwd, mix_recv,
    in_own, in_part, in_send, in_fwd, in_recv,
    g_own, g_send, g_recv, h_send, h_recv, t_send, t_recv, t_own, last_recv,
    load_sem, send_sem, recv_sem, ready_sem,
):
    gi, dxs = zs, dos
    seq, ch = lax.axis_index("seq"), lax.axis_index("ch")
    core, y, z = lax.rem(seq, 2), lax.rem(seq // 2, 4), seq // 8
    other = 1 - core
    place = z * 4 + y

    def x_peer(k):
        return (seq, lax.rem(ch + k, 4))

    def zy_peer(dz, dy):
        return (lax.rem(z + dz, 4) * 8 + lax.rem(y + dy, 4) * 2 + core, ch)

    core_peer = (seq + 1 - 2 * core, ch)
    shifts = [(k // 4, k % 4) for k in range(1, PEERS)]

    def remote(src, dst, sem, device):
        return pltpu.make_async_remote_copy(
            src_ref=src,
            dst_ref=dst,
            send_sem=send_sem.at[sem],
            recv_sem=recv_sem.at[sem],
            device_id=device,
            device_id_type=MESH,
        )

    loads = [
        pltpu.make_async_copy(src, dst, load_sem.at[n])
        for n, (src, dst) in enumerate(
            (
                (cot_hbm, cot.at[ch]),
                (hidden_hbm, hidden),
                (proj_x_hbm, proj_x),
                (proj_z_hbm, proj_z),
                (proj_out_hbm, proj_out),
                (proj_b_hbm, proj_b),
                (proj_c_hbm, proj_c),
                (proj_dt_hbm, proj_dt),
                (bias_hbm, bias),
                (rate_hbm, rate),
                (skip_hbm, skip),
            )
        )
    ]
    barrier = pltpu.get_barrier_semaphore()
    near = [zy_peer(0, 1), zy_peer(0, 3), zy_peer(1, 0), zy_peer(3, 0)]
    for device in [x_peer(1), x_peer(3), core_peer] + near:
        pl.semaphore_signal(barrier, inc=1, device_id=device, device_id_type=MESH)
    for load in loads[:1] + loads[5:] + loads[1:5]:
        load.start()
    anti = anti_identity()
    e = spread_matrix()
    half = [slice(0, Q), slice(Q, L)]
    before, after = lax.rem(ch + 3, 4), lax.rem(ch + 1, 4)

    def cot_copy(n):
        block, rows, to = (
            (ch, half[0], 1), (ch, half[1], 3), (ch, half[1], 1), (ch, half[0], 3),
            (before, half[0], 1), (after, half[1], 3),
        )[n]
        return remote(cot.at[block, rows], cot.at[block, rows], S_COT + n, x_peer(to))

    def vouch(n):
        if n:
            pl.semaphore_wait(ready_sem.at[n - 1], 4)
        if n < 3:
            for device in near:
                pl.semaphore_signal(
                    ready_sem.at[n], inc=1, device_id=device, device_id_type=MESH
                )

    for load in loads[5:]:
        load.wait()
    small[...] = jnp.zeros_like(small)
    for weight, at in zip((proj_b, proj_c, proj_dt), range(3)):
        n = weight.shape[0]
        small[SMALL[0][at] : SMALL[0][at] + n, :] = weight[...]
        for k in range(BLOCKS):
            here, there = slice(k * Q, (k + 1) * Q), slice(D - (k + 1) * Q, D - k * Q)
            small[SMALL[1][at] : SMALL[1][at] + n, here] = mm(weight[:, there], anti).astype(BF16)
    loads[1].wait()
    ident = identity()
    for k in range(BLOCKS):
        here, there = slice(k * Q, (k + 1) * Q), slice(D - (k + 1) * Q, D - k * Q)
        hidden_t[k] = mm_t(ident, hidden[:, here]).astype(BF16)
        hidden_flip_t[k] = mm_t(anti, hidden[:, there]).astype(BF16)
    for load, source, flip in ((loads[2], proj_x, px_flip), (loads[3], proj_z, pz_flip)):
        load.wait()
        for k in range(BLOCKS):
            here, there = slice(k * Q, (k + 1) * Q), slice(D - (k + 1) * Q, D - k * Q)
            flip[here, :] = mm(anti, source[there, :]).astype(BF16)

    def project_step(k, carry):
        rows = rows_of(k)
        u = hidden[rows, :]
        xs[0, rows, :] = mm(u, proj_x[...])
        zs[0, rows, :] = mm(u, proj_z[...])
        xs[1, rows, :] = mm(u, px_flip[...])
        zs[1, rows, :] = mm(u, pz_flip[...])
        narrow = mm_t(u, small[...])
        for strand in range(2):
            at_b, at_c, at_dt = SMALL[strand]
            bs[strand, rows, :] = narrow[:, at_b : at_b + NS].astype(BF16)
            cs[strand, rows, :] = narrow[:, at_c : at_c + NS].astype(BF16)
            dts[strand, rows, :] = narrow[:, at_dt : at_dt + HEADS] + bias[...]
        return carry

    lax.fori_loop(0, CHUNKS, project_step, 0)
    loads[0].wait()
    pl.semaphore_wait(barrier, 7)
    for n in range(4):
        cot_copy(n).start()
    vouch(0)

    def state_step(i, carry):
        strand, k = i // CHUNKS, lax.rem(i, CHUNKS)
        rows = rows_of(k)
        dt = softplus(dts[strand, rows, :])
        a = -rate[...] * dt
        cum = running(a, order(1 - 2 * strand))
        total = jnp.sum(a, axis=0, keepdims=True)
        cums[strand, rows, :] = cum
        dts_soft[strand, rows, :] = dt
        e_rest = spread(jnp.exp(total - cum), e)
        dt_wide = spread(dt, e)
        e_cums[strand, rows, :] = spread(jnp.exp(cum), e)
        e_rests[strand, rows, :] = e_rest
        dt_wides[strand, rows, :] = dt_wide
        xd = xs[strand, rows, :] * dt_wide
        xdt[strand, rows, :] = xd.astype(BF16)
        chunk_state[strand, k] = t_mm(bs[strand, rows, :], (xd * e_rest).astype(BF16))
        chunk_decay[strand, k] = jnp.broadcast_to(jnp.exp(spread(total, e)), (8, W))
        return carry

    lax.fori_loop(0, 2 * CHUNKS, state_step, 0)
    vouch(1)

    def times(strand):
        return list(range(CHUNKS)) if strand == 0 else list(range(CHUNKS))[::-1]

    def two_halves(dst, rows, value):
        dst[0, rows, :] = value[:, 0:Q]
        dst[1, rows, :] = value[:, Q:]

    decays = []
    for strand in range(2):
        state, decay = chunk_state[strand, times(strand)[0]], chunk_decay[strand, 0]
        for k in times(strand)[1:]:
            state = chunk_decay[strand, k, 0:1, :] * state + chunk_state[strand, k]
        for k in range(1, CHUNKS):
            decay = decay * chunk_decay[strand, k]
        two_halves(a_msg, slice(16 * strand, 16 * strand + NS), state)
        decays.append(decay)
    two_halves(a_msg, slice(32, 40), jnp.where(iota((8, W), 0) == 0, decays[0], decays[1]))

    zero = jnp.zeros((NS, Q), F32)
    a_slots[place] = jnp.zeros_like(a_slots[0])
    b_slots[place] = jnp.zeros_like(b_slots[0])

    class Exchange:
        def __init__(self, base, msg, from_core, pair, slots, back, result, swap):
            self.base, self.msg, self.from_core, self.pair = base, msg, from_core, pair
            self.slots, self.back, self.result, self.swap = slots, back, result, swap

        def to_core(self):
            return remote(self.msg.at[other], self.from_core, self.base, core_peer)

        def to_place(self, dz, dy):
            to = lax.rem(z + dz, 4) * 4 + lax.rem(y + dy, 4)
            kind = jnp.where(to > place, 0, 1)
            return remote(
                self.pair.at[kind], self.slots.at[place], self.base + 4 * dz + dy, zy_peer(dz, dy)
            )

        def to_back(self):
            return remote(self.back, self.result.at[core], self.base + PEERS, core_peer)

        def decay(self, ref, strand):
            return ref[strand : strand + 1, :]

        def both(self):
            mine = (
                self.msg[core, 0:16, :], self.msg[core, 16:32, :],
                a_msg[core, 32 + self.swap : 33 + self.swap, :],
                a_msg[core, 33 - self.swap : 34 - self.swap, :],
            )
            theirs = (
                self.from_core[0:16, :], self.from_core[16:32, :],
                a_core[32 + self.swap : 33 + self.swap, :],
                a_core[33 - self.swap : 34 - self.swap, :],
            )
            return mine, theirs

        def spread_out(self):
            self.to_core().wait_recv()
            mine, theirs = self.both()
            first = [jnp.where(core == 0, m, t) for m, t in zip(mine, theirs)]
            second = [jnp.where(core == 0, t, m) for m, t in zip(mine, theirs)]
            up = second[2] * first[0] + second[0]
            down = first[3] * second[1] + first[1]
            self.pair[0, 0:16, :] = up
            self.pair[1, 0:16, :] = down
            if not self.swap:
                product = jnp.where(
                    iota((8, Q), 0) == 0,
                    jnp.broadcast_to(first[2] * second[2], (8, Q)),
                    jnp.broadcast_to(first[3] * second[3], (8, Q)),
                )
                self.pair[0, 16:24, :] = product
                self.pair[1, 16:24, :] = product
            for dz, dy in shifts:
                self.to_place(dz, dy).start()

        def collect(self):
            for dz, dy in shifts:
                self.to_place(dz, dy).wait_recv()
            up = down = zero
            for j in range(PEERS):
                r = PEERS - 1 - j
                decay_up = a_slots[j, 16 + self.swap : 17 + self.swap, :]
                decay_down = a_slots[r, 17 - self.swap : 18 - self.swap, :]
                up = jnp.where(j < place, decay_up * up + self.slots[j, 0:16, :], up)
                down = jnp.where(r > place, decay_down * down + self.slots[r, 0:16, :], down)
            mine, theirs = self.both()
            self.back[0:16, :] = jnp.where(core == 0, mine[2] * up + mine[0], up)
            self.back[16:32, :] = jnp.where(core == 1, mine[3] * down + mine[1], down)
            self.to_back().start()
            self.result[core, 0:16, :] = jnp.where(core == 1, theirs[2] * up + theirs[0], up)
            self.result[core, 16:32, :] = jnp.where(core == 0, theirs[3] * down + theirs[1], down)

        def take(self):
            self.to_back().wait_recv()
            return [
                jnp.concatenate([self.result[0, rows, :], self.result[1, rows, :]], axis=1)
                for rows in (slice(0, 16), slice(16, 32))
            ]

        def drain(self):
            self.to_core().wait_send()
            self.to_back().wait_send()
            for dz, dy in shifts:
                self.to_place(dz, dy).wait_send()

    round_a = Exchange(S_A, a_msg, a_core, a_pair, a_slots, a_back, a_in, 0)
    round_b = Exchange(S_B, b_msg, b_core, b_pair, b_slots, b_back, b_in, 1)
    round_a.to_core().start()

    lane = iota((Q, 128), 1)

    def within_step(i, carry):
        strand, k = i // CHUNKS, lax.rem(i, CHUNKS)
        rows = rows_of(k)
        mask = order(2 * strand - 1)
        cum = cums[strand, rows, :]
        cum_t = cum.T
        scores = mm_t(bs[strand, rows, :], cs[strand, rows, :])
        for pair in range(HEADS // 2):
            columns = slice(pair * 128, (pair + 1) * 128)
            x_pair = xdt[strand, rows, columns]
            y_sum = None
            for odd in range(2):
                h = 2 * pair + odd
                own = (lane >= HEAD) if odd else (lane < HEAD)
                x_own = jnp.where(own, x_pair, jnp.zeros((), BF16))
                decay = jnp.exp(
                    jnp.where(mask, cum_t[h : h + 1, :] - cum[:, h : h + 1], -1e30)
                )
                mixing = (decay * scores).astype(BF16)
                kept_decay[i, h] = decay.astype(BF16)
                y_new = t_mm(mixing, x_own)
                y_sum = y_new if y_sum is None else y_sum + y_new
            yi[strand, rows, columns] = y_sum

        @pl.when(i == 0)
        def _():
            vouch(2)
            for n in range(2):
                cot_copy(n).wait_recv()
                cot_copy(4 + n).start()

        @pl.when(i == 1)
        def _():
            vouch(3)
            round_a.spread_out()

        return carry

    lax.fori_loop(0, 2 * CHUNKS, within_step, 0)

    loads[4].wait()
    for k in range(BLOCKS):
        here, there = slice(k * Q, (k + 1) * Q), slice(D - (k + 1) * Q, D - k * Q)
        po_flip[:, here] = mm(proj_out[:, there], anti).astype(BF16)

    def cot_block(c, rows):
        block = cot[c, rows, :]
        cot_t[c, :, rows] = mm_t(ident, block).astype(BF16)
        cot_flip_t[BLOCKS - 1 - c, :, rows] = mm_t(anti, block).astype(BF16)
        columns = pl.ds(pl.multiple_of(c * Q, Q), Q)
        return mm_t(block, proj_out[:, columns]), mm_t(block, po_flip[:, columns])

    def first_step(k, carry):
        rows = rows_of(k)
        parts = [cot_block(c, rows) for c in (ch, before, after)]
        for strand in range(2):
            value = sum(part[strand] for part in parts)
            g_own[strand, pl.ds(2 * k, 2)] = value.reshape(2, 4, ROWS, W)
        return carry

    def last_step(k, carry):
        rows = rows_of(k)
        parts = cot_block(lax.rem(ch + 2, 4), rows)
        for strand in range(2):
            early = g_own[strand, pl.ds(2 * k, 2)].reshape(Q, W)
            dos[strand, rows, :] = (early + parts[strand]).astype(BF16)
        return carry

    for n in range(2, 4):
        cot_copy(n).wait_recv()
    lax.fori_loop(0, CHUNKS, first_step, 0)
    for n in range(4, 6):
        cot_copy(n).wait_recv()
    lax.fori_loop(0, CHUNKS, last_step, 0)

    def grad_step(i, carry):
        strand, k = i // CHUNKS, lax.rem(i, CHUNKS)
        rows = rows_of(k)
        gate = zs[strand, rows, :]
        dy = dos[strand, rows, :].astype(F32) * (gate * sigmoid(gate))
        dyb[strand, rows, :] = dy.astype(BF16)
        chunk_grad[strand, k] = t_mm(
            cs[strand, rows, :], (dy * e_cums[strand, rows, :]).astype(BF16)
        )
        return carry

    lax.fori_loop(0, 2 * CHUNKS, grad_step, 0)

    for strand in range(2):
        falling = times(strand)[::-1]
        grad = chunk_grad[strand, falling[0]]
        for k in falling[1:]:
            grad = chunk_decay[strand, k, 0:1, :] * grad + chunk_grad[strand, k]
        two_halves(b_msg, slice(16 - 16 * strand, 32 - 16 * strand), grad)
    round_b.to_core().start()

    round_a.collect()
    for strand, state in enumerate(round_a.take()):
        for k in times(strand):
            own_state = chunk_state[strand, k]
            chunk_state[strand, k] = state
            state = chunk_decay[strand, k, 0:1, :] * state + own_state
            chunk_dot[strand, k] = state

    skip_wide = spread(skip[...], e)

    def out_step(i, carry):
        strand, k = i // CHUNKS, lax.rem(i, CHUNKS)
        rows = rows_of(k)
        e_cum = e_cums[strand, rows, :]
        state = chunk_state[strand, k].astype(BF16)
        gate = zs[strand, rows, :]
        d_o = dos[strand, rows, :].astype(F32)
        sig = sigmoid(gate)
        silu = gate * sig
        dy = d_o * silu
        y_part = yi[strand, rows, :] + e_cum * mm(cs[strand, rows, :], state)
        out = y_part + skip_wide * xs[strand, rows, :]
        os[strand, rows, :] = (out * silu).astype(BF16)
        dzs[strand, rows, :] = (d_o * out * (sig + silu * (1.0 - sig))).astype(BF16)
        dcs[strand, rows, :] = mm_t((dy * e_cum).astype(BF16), state)
        dyy[strand, rows, :] = gather_heads(dy * y_part, e)
        yi[strand, rows, :] = skip_wide * dy

        @pl.when(i == 1)
        def _():
            round_b.spread_out()

        return carry

    lax.fori_loop(0, 2 * CHUNKS, out_step, 0)

    class ColumnSum:
        def __init__(self, base, compute, own, part, send, forward, recv):
            self.base, self.compute, self.own, self.part = base, compute, own, part
            self.send, self.forward, self.recv = send, forward, recv

        def copy(self, n):
            src, dst, to = (
                (self.send.at[1, half[0]], self.forward.at[0], 1),
                (self.send.at[1, half[1]], self.forward.at[1], 3),
                (self.send.at[0, half[1]], self.recv.at[0, half[1]], 1),
                (self.send.at[2, half[0]], self.recv.at[1, half[0]], 3),
                (self.send.at[0, half[0]], self.recv.at[0, half[0]], 1),
                (self.send.at[2, half[1]], self.recv.at[1, half[1]], 3),
            )[n]
            return remote(src, dst, self.base + n, x_peer(to))

        def columns(self, r):
            return pl.ds(pl.multiple_of(lax.rem(ch + r, 4) * Q, Q), Q)

        def far(self):
            for n in range(2):
                self.send[1, half[n], :] = self.compute(half[n], self.columns(2)).astype(BF16)
                self.copy(n).start()

        def near(self):
            self.send[0, half[1], :] = self.compute(half[1], self.columns(1)).astype(BF16)
            self.copy(2).start()
            self.send[2, half[0], :] = self.compute(half[0], self.columns(3)).astype(BF16)
            self.copy(3).start()
            self.part[0] = self.compute(half[0], self.columns(1))
            self.part[1] = self.compute(half[1], self.columns(3))

        def middle(self):
            for n, block in ((0, 0), (1, 2)):
                self.copy(n).wait_recv()
                self.send[block, half[n], :] = (
                    self.part[n] + self.forward[n].astype(F32)
                ).astype(BF16)
                self.copy(4 + n).start()

        def own_block(self):
            for n in range(2):
                self.own[half[n], :] = self.compute(half[n], self.columns(0))

        def finish(self, rows):
            return (
                self.own[rows, :]
                + self.recv[0, rows, :].astype(F32)
                + self.recv[1, rows, :].astype(F32)
            )

        def arrived(self):
            for n in range(2, 6):
                self.copy(n).wait_recv()

        def drain(self):
            for n in range(6):
                self.copy(n).wait_send()

    def mix_block(rows, columns):
        return mm(os[0, rows, :], proj_out[:, columns]) + mm(os[1, rows, :], po_flip[:, columns])

    def in_block(rows, columns):
        return (
            mm_t(dxs[0, rows, :], proj_x[columns, :])
            + mm_t(dzs[0, rows, :], proj_z[columns, :])
            + mm_t(dxs[1, rows, :], px_flip[columns, :])
            + mm_t(dzs[1, rows, :], pz_flip[columns, :])
            + mm(ext[rows, :], small[:, columns])
        )

    mix_sum = ColumnSum(S_MIX, mix_block, mix_own, mix_part, mix_send, mix_fwd, mix_recv)
    in_sum = ColumnSum(S_IN, in_block, in_own, in_part, in_send, in_fwd, in_recv)

    def g_core_copy(n):
        return remote(g_send.at[n], g_recv.at[n], S_GCORE + n, core_peer)

    def g_copy(n, at):
        stage, over_z, k = at // 6, at % 6 // 3, at % 3 + 1
        peer = zy_peer(k, 0) if over_z != stage else zy_peer(0, k)
        if stage:
            src, dst = t_send.at[n, over_z, k - 1], t_recv.at[n, over_z, k - 1]
        elif over_z:
            src, dst = h_send.at[n, lax.rem(z + k, 4), :, :, Q:W], h_recv.at[n, 1, k - 1]
        else:
            src, dst = h_send.at[n, :, lax.rem(y + k, 4), :, 0:Q], h_recv.at[n, 0, k - 1]
        return remote(src, dst, S_GPEER + 12 * n + at, peer)

    def x_copy(dz, dy):
        at = 4 * dz + dy
        return remote(
            h_send.at[2, lax.rem(z + dz, 4), lax.rem(y + dy, 4)], last_recv.at[at],
            S_LAST + at, zy_peer(dz, dy),
        )

    def weight_part(n, left, left_flip, right):
        def step(b, carry):
            value = mm(left[b], right[0]) + mm(left_flip[b], right[1])
            value = value.reshape(4, 2, ROWS, W)
            g_own[n, b] = jnp.where(core == 0, value[:, 0], value[:, 1])
            g_send[n, b] = jnp.where(core == 0, value[:, 1], value[:, 0]).astype(BF16)
            return carry

        lax.fori_loop(0, BLOCKS, step, 0)
        g_core_copy(n).start()

    def weight_pair(n):
        g_core_copy(n).wait_recv()

        def pair_sum(i, carry):
            at = (n, i // 4, lax.rem(i, 4))
            value = g_own[at] + g_recv[at].astype(F32)
            g_own[at] = value
            h_send[at] = value.astype(BF16)
            return carry

        lax.fori_loop(0, PEERS, pair_sum, 0)
        if n == 2:
            for dz, dy in shifts:
                x_copy(dz, dy).start()
        else:
            for at in range(6):
                g_copy(n, at).start()

    def weight_middle(n):
        for at in range(6):
            g_copy(n, at).wait_recv()
        for r in (1, 2, 3, 0):
            to_z, to_y = lax.rem(z + r, 4), lax.rem(y + r, 4)
            first, second = g_own[n, to_z, y, :, 0:Q], g_own[n, z, to_y, :, Q:W]
            for k in range(3):
                first = first + h_recv[n, 0, k, to_z].astype(F32)
                second = second + h_recv[n, 1, k, to_y].astype(F32)
            if r:
                t_send[n, 0, r - 1] = first.astype(BF16)
                t_send[n, 1, r - 1] = second.astype(BF16)
                g_copy(n, 6 + r - 1).start()
                g_copy(n, 9 + r - 1).start()
            else:
                t_own[n, 0] = first
                t_own[n, 1] = second

    def weight_total(n, out):
        for at in range(6, 12):
            g_copy(n, at).wait_recv()
        for side in range(2):
            total = t_own[n, side]
            for k in range(3):
                total = total + t_recv[n, side, k].astype(F32)
            out[:, side * Q : (side + 1) * Q] = total

    weight_part(0, cot_t, cot_flip_t, os)
    mix_sum.far()
    mix_sum.near()
    weight_part(1, hidden_t, hidden_flip_t, dzs)
    weight_pair(0)

    def inner_step(i, carry):
        strand, k = i // CHUNKS, lax.rem(i, CHUNKS)
        rows = rows_of(k)
        b = bs[strand, rows, :]
        c = cs[strand, rows, :]
        scores = mm_t(b, c)
        for pair in range(HEADS // 2):
            columns = slice(pair * 128, (pair + 1) * 128)
            x_pair, dy_pair = xdt[strand, rows, columns], dyb[strand, rows, columns]
            g_sum = None
            for odd in range(2):
                h = 2 * pair + odd
                own = (lane >= HEAD) if odd else (lane < HEAD)
                dy_own = jnp.where(own, dy_pair, jnp.zeros((), BF16))
                decay = kept_decay[i, h].astype(F32)
                part = decay * mm_t(x_pair, dy_own)
                if h == 0:
                    zacc[...] = part
                else:
                    zacc[...] += part
                g_new = mm((decay * scores).astype(BF16), dy_own)
                g_sum = g_new if g_sum is None else g_sum + g_new
            gi[strand, rows, columns] = g_sum
        pairs = zacc[...].astype(BF16)
        dbs[strand, rows, :] = mm(pairs, c)
        dcs[strand, rows, :] += t_mm(pairs, b)

        @pl.when(i == 0)
        def _():
            mix_sum.middle()
            weight_pair(1)

        @pl.when(i == 1)
        def _():
            round_b.collect()

        @pl.when(i == 2)
        def _():
            weight_middle(0)

        return carry

    lax.fori_loop(0, 2 * CHUNKS, inner_step, 0)

    mix_sum.own_block()
    weight_middle(1)

    up, down = round_b.take()
    for strand, grad in enumerate((down, up)):
        for k in times(strand)[::-1]:
            own_grad = chunk_grad[strand, k]
            chunk_grad[strand, k] = grad
            chunk_dot[strand, k, 0:8, :] = jnp.broadcast_to(
                jnp.sum(grad * chunk_dot[strand, k], axis=0, keepdims=True), (8, W)
            )
            grad = chunk_decay[strand, k, 0:1, :] * grad + own_grad
    ext[...] = jnp.zeros_like(ext)

    def back_step(k, carry):
        rows = rows_of(k)
        for strand in range(2):
            dt = dts_soft[strand, rows, :]
            e_rest = e_rests[strand, rows, :]
            dt_wide = dt_wides[strand, rows, :]
            grad = chunk_grad[strand, k].astype(BF16)
            x = xs[strand, rows, :]
            gb = gi[strand, rows, :] + e_rest * mm(bs[strand, rows, :], grad)
            dxs[strand, rows, :] = (dt_wide * gb + yi[strand, rows, :]).astype(BF16)
            d_b = dbs[strand, rows, :] + mm_t((x * dt_wide * e_rest).astype(BF16), grad)
            direct = gather_heads(x * gb, e)
            d_cum = dyy[strand, rows, :] - dt * direct
            d_a = running(d_cum, order(2 * strand - 1)) + gather_heads(
                chunk_dot[strand, k, 0:8, :], e
            )[0:1, :]
            d_raw = (direct - rate[...] * d_a) * sigmoid(dts[strand, rows, :])
            at_b, at_c, at_dt = SMALL[strand]
            ext[rows, at_b : at_b + NS] = d_b.astype(BF16)
            ext[rows, at_c : at_c + NS] = dcs[strand, rows, :].astype(BF16)
            ext[rows, at_dt : at_dt + HEADS] = d_raw.astype(BF16)
        return carry

    lax.fori_loop(0, CHUNKS, back_step, 0)

    weight_part(2, hidden_t, hidden_flip_t, dxs)
    in_sum.far()
    weight_pair(2)
    in_sum.near()
    in_sum.middle()
    in_sum.own_block()

    mix_sum.arrived()

    def mix_step(k, carry):
        rows = rows_of(k)
        mine = hidden[rows, pl.ds(pl.multiple_of(ch * Q, Q), Q)].astype(F32)
        block_out[rows, :] = (mine + mix_sum.finish(rows)).astype(BF16)
        return carry

    lax.fori_loop(0, CHUNKS, mix_step, 0)

    weight_total(0, grad_out)
    weight_total(1, grad_z)
    in_sum.arrived()

    def in_step(k, carry):
        rows = rows_of(k)
        grad_hidden[rows, :] = cot[ch, rows, :].astype(F32) + in_sum.finish(rows)
        return carry

    lax.fori_loop(0, CHUNKS, in_step, 0)

    total = g_own[2, z, y]
    for dz, dy in shifts:
        x_copy(dz, dy).wait_recv()
        total = total + last_recv[4 * dz + dy].astype(F32)
    grad_x[...] = total

    for n in range(6):
        cot_copy(n).wait_send()
    round_a.drain()
    round_b.drain()
    mix_sum.drain()
    in_sum.drain()
    for n in range(3):
        g_core_copy(n).wait_send()
    for at in range(12):
        g_copy(0, at).wait_send()
        g_copy(1, at).wait_send()
    for dz, dy in shifts:
        x_copy(dz, dy).wait_send()


def hand_over(*refs):
    sems = refs[10]
    copies = [pltpu.make_async_copy(refs[n], refs[5 + n], sems.at[n]) for n in range(5)]
    for copy in copies:
        copy.start()
    for copy in copies:
        copy.wait()


def shape(*dims, dtype=F32):
    return jax.ShapeDtypeStruct(dims, dtype)


VMEM = pl.BlockSpec(memory_space=pltpu.VMEM)


def body(
    hidden, proj_x, proj_z, proj_b, proj_c, proj_dt, dt_bias, decay_rate, skip_gain, proj_out, cotangent
):
    bias, rate, skip = (v[None, :] for v in (dt_bias, decay_rate, skip_gain))
    vm = pltpu.VMEM
    results = (
        shape(L, Q, dtype=BF16),
        shape(L, Q),
        shape(ROWS, W),
        shape(ROWS, W),
        shape(ROWS, W),
    )
    made = pl.pallas_call(
        block_kernel,
        out_shape=results,
        in_specs=[pl.BlockSpec(memory_space=pl.ANY)] * 11,
        out_specs=[VMEM] * 5,
        scratch_shapes=[
            vm((L, D), BF16), vm((D, W), BF16), vm((D, W), BF16), vm((W, D), BF16),
            vm((NS, D), BF16), vm((NS, D), BF16), vm((HEADS, D), BF16),
            vm((1, HEADS), F32), vm((1, HEADS), F32), vm((1, HEADS), F32),
            vm((D, W), BF16), vm((D, W), BF16), vm((W, D), BF16), vm((128, D), BF16),
            vm((BLOCKS, Q, L), BF16), vm((BLOCKS, Q, L), BF16),
            vm((BLOCKS, L, Q), BF16), vm((BLOCKS, Q, L), BF16), vm((BLOCKS, Q, L), BF16),
            vm((2, L, W), F32), vm((2, L, W), F32), vm((2, L, NS), BF16), vm((2, L, NS), BF16),
            vm((2, L, HEADS), F32), vm((2, L, W), BF16), vm((2, L, HEADS), F32),
            vm((2, L, HEADS), F32), vm((2, L, W), F32), vm((2, L, W), F32), vm((2, L, W), F32),
            vm((2, L, W), BF16), vm((2, L, W), BF16), vm((Q, Q), F32),
            vm((2 * CHUNKS, HEADS, Q, Q), BF16),
            vm((2, L, W), F32), vm((2, L, NS), F32), vm((2, L, NS), F32),
            vm((2, L, HEADS), F32),
            vm((L, 128), BF16), vm((2, L, W), BF16), vm((2, L, W), BF16),
            vm((2, CHUNKS, NS, W), F32), vm((2, CHUNKS, NS, W), F32),
            vm((2, CHUNKS, 8, W), F32), vm((2, CHUNKS, NS, W), F32),
            vm((2, 40, Q), F32), vm((40, Q), F32), vm((2, 24, Q), F32), vm((PEERS, 24, Q), F32),
            vm((32, Q), F32), vm((2, 32, Q), F32),
            vm((2, 32, Q), F32), vm((32, Q), F32), vm((2, 16, Q), F32), vm((PEERS, 16, Q), F32),
            vm((32, Q), F32), vm((2, 32, Q), F32),
            vm((L, Q), F32), vm((2, Q, Q), F32), vm((3, L, Q), BF16), vm((2, Q, Q), BF16),
            vm((2, L, Q), BF16),
            vm((L, Q), F32), vm((2, Q, Q), F32), vm((3, L, Q), BF16), vm((2, Q, Q), BF16),
            vm((2, L, Q), BF16),
            vm((3, 4, 4, ROWS, W), F32), vm((3, 4, 4, ROWS, W), BF16),
            vm((3, 4, 4, ROWS, W), BF16), vm((3, 4, 4, ROWS, W), BF16),
            vm((2, 2, 3, 4, ROWS, Q), BF16), vm((2, 2, 3, ROWS, Q), BF16),
            vm((2, 2, 3, ROWS, Q), BF16), vm((2, 2, ROWS, Q), F32), vm((PEERS, ROWS, W), BF16),
            pltpu.SemaphoreType.DMA((11,)),
            pltpu.SemaphoreType.DMA((S_ALL,)), pltpu.SemaphoreType.DMA((S_ALL,)),
            pltpu.SemaphoreType.REGULAR((3,)),
        ],
        compiler_params=pltpu.CompilerParams(
            vmem_limit_bytes=60 * 2**20, collective_id=0, has_side_effects=True
        ),
        name="block",
    )(
        hidden, proj_x, proj_z, proj_out, cotangent,
        proj_b.T, proj_c.T, proj_dt.T, bias, rate, skip,
    )
    *most, grad_out = pl.pallas_call(
        hand_over,
        out_shape=results,
        in_specs=[VMEM] * 5,
        out_specs=[pl.BlockSpec(memory_space=pl.ANY)] * 5,
        scratch_shapes=[pltpu.SemaphoreType.DMA((5,))],
        name="hand_over",
    )(*made)
    return *most, grad_out.T


def solution(mesh):
    return jax.shard_map(
        body,
        mesh=mesh,
        in_specs=(
            P("seq", None),
            P(None, "ch"),
            P(None, "ch"),
            P(),
            P(),
            P(None, "ch"),
            P("ch"),
            P("ch"),
            P("ch"),
            P("ch", None),
            P("seq", "ch"),
        ),
        out_specs=(P("seq", "ch"), P("seq", "ch"), P("seq", "ch"), P("seq", "ch"), P("ch", "seq")),
        check_vma=False,
    )
```

```python
import jax
import jax.numpy as jnp
from jax import lax
from jax.experimental import pallas as pl
from jax.experimental.pallas import tpu as pltpu
from jax.sharding import PartitionSpec as P

L = 512
D = 1024
W = 512
HEADS = 8
HEAD = 64
NS = 16
Q = 256
CHUNKS = L // Q
BLOCKS = D // Q
PEERS = 16
ROWS = 32
F32 = jnp.float32
BF16 = jnp.bfloat16
MESH = pl.DeviceIdType.MESH

LAST = (((1,), (1,)), ((), ()))
FIRST = (((0,), (0,)), ((), ()))

SMALL = ((0, 16, 32), (48, 64, 80))

S_COT, S_MIX, S_IN, S_A, S_B = 0, 6, 12, 18, 36
S_GCORE, S_GPEER = 54, 57
S_LAST = S_GPEER + 2 * 12
S_ALL = S_LAST + 16


def mm(a, b):
    return jnp.dot(a, b, preferred_element_type=F32)


def mm_t(a, b):
    return lax.dot_general(a, b, LAST, preferred_element_type=F32)


def t_mm(a, b):
    return lax.dot_general(a, b, FIRST, preferred_element_type=F32)


def split2(v):
    high = v.astype(BF16)
    return high, (v - high.astype(F32)).astype(BF16)


def split3(v):
    high = v.astype(BF16)
    rest = v - high.astype(F32)
    mid = rest.astype(BF16)
    return high, mid, (rest - mid.astype(F32)).astype(BF16)


def iota(shape, dim):
    return lax.broadcasted_iota(jnp.int32, shape, dim)


def identity():
    return jnp.where(iota((Q, Q), 0) == iota((Q, Q), 1), 1.0, 0.0).astype(BF16)


def anti_identity():
    return jnp.where(iota((Q, Q), 0) + iota((Q, Q), 1) == Q - 1, 1.0, 0.0).astype(BF16)


def spread_matrix():
    head = iota((2 * HEADS, W), 0)
    head = jnp.where(head >= HEADS, head - HEADS, head)
    return jnp.where(iota((2 * HEADS, W), 1) // HEAD == head, 1.0, 0.0).astype(BF16)


def spread(v, e):
    return mm(jnp.concatenate(split2(v), axis=1), e)


def gather_heads(v, e):
    high, low = split2(v)
    return (mm_t(high, e) + mm_t(low, e))[:, 0:HEADS]


def order(sign):
    return (iota((Q, Q), 0) - iota((Q, Q), 1)) * sign >= 0


def running(v, mask):
    ones = jnp.where(mask, 1.0, 0.0).astype(BF16)
    return sum(mm(ones, part) for part in split3(v))


def softplus(v):
    return jnp.maximum(v, 0.0) + jnp.log1p(jnp.exp(-jnp.abs(v)))


def sigmoid(v):
    return 1.0 / (1.0 + jnp.exp(-v))


def rows_of(k):
    return pl.ds(pl.multiple_of(k * Q, Q), Q)


def block_kernel(
    hidden_hbm, proj_x_hbm, proj_z_hbm, proj_out_hbm, cot_hbm,
    proj_b_hbm, proj_c_hbm, proj_dt_hbm, bias_hbm, rate_hbm, skip_hbm,
    block_out, grad_hidden, grad_x, grad_z, grad_out,
    hidden, proj_x, proj_z, proj_out, proj_b, proj_c, proj_dt, bias, rate, skip,
    px_flip, pz_flip, po_flip, small, hidden_t, hidden_flip_t, cot, cot_t, cot_flip_t,
    xs, zs, bs, cs, dts, dos, cums, dts_soft, e_cums, e_rests, dt_wides, dyb, xdt, zacc, kept_decay,
    yi, dcs, dbs, dyy, ext, os, dzs,
    chunk_state, chunk_grad, chunk_decay, chunk_dot,
    a_msg, a_core, a_pair, a_slots, a_back, a_in,
    b_msg, b_core, b_pair, b_slots, b_back, b_in,
    mix_own, mix_part, mix_send, mix_fwd, mix_recv,
    in_own, in_part, in_send, in_fwd, in_recv,
    g_own, g_send, g_recv, h_send, h_recv, t_send, t_recv, t_own, last_recv,
    load_sem, send_sem, recv_sem, ready_sem,
):
    gi, dxs = zs, dos
    seq, ch = lax.axis_index("seq"), lax.axis_index("ch")
    core, y, z = lax.rem(seq, 2), lax.rem(seq // 2, 4), seq // 8
    other = 1 - core
    place = z * 4 + y

    def x_peer(k):
        return (seq, lax.rem(ch + k, 4))

    def zy_peer(dz, dy):
        return (lax.rem(z + dz, 4) * 8 + lax.rem(y + dy, 4) * 2 + core, ch)

    core_peer = (seq + 1 - 2 * core, ch)
    shifts = [(k // 4, k % 4) for k in range(1, PEERS)]

    def remote(src, dst, sem, device):
        return pltpu.make_async_remote_copy(
            src_ref=src,
            dst_ref=dst,
            send_sem=send_sem.at[sem],
            recv_sem=recv_sem.at[sem],
            device_id=device,
            device_id_type=MESH,
        )

    loads = [
        pltpu.make_async_copy(src, dst, load_sem.at[n])
        for n, (src, dst) in enumerate(
            (
                (cot_hbm, cot.at[ch]),
                (hidden_hbm, hidden),
                (proj_x_hbm, proj_x),
                (proj_z_hbm, proj_z),
                (proj_out_hbm, proj_out),
                (proj_b_hbm, proj_b),
                (proj_c_hbm, proj_c),
                (proj_dt_hbm, proj_dt),
                (bias_hbm, bias),
                (rate_hbm, rate),
                (skip_hbm, skip),
            )
        )
    ]
    barrier = pltpu.get_barrier_semaphore()
    near = [zy_peer(0, 1), zy_peer(0, 3), zy_peer(1, 0), zy_peer(3, 0)]
    for device in [x_peer(1), x_peer(3), core_peer] + near:
        pl.semaphore_signal(barrier, inc=1, device_id=device, device_id_type=MESH)
    for load in loads[:1] + loads[5:] + loads[1:5]:
        load.start()
    anti = anti_identity()
    e = spread_matrix()
    half = [slice(0, Q), slice(Q, L)]
    before, after = lax.rem(ch + 3, 4), lax.rem(ch + 1, 4)

    def cot_copy(n):
        block, rows, to = (
            (ch, half[0], 1), (ch, half[1], 3), (ch, half[1], 1), (ch, half[0], 3),
            (before, half[0], 1), (after, half[1], 3),
        )[n]
        return remote(cot.at[block, rows], cot.at[block, rows], S_COT + n, x_peer(to))

    def vouch(n):
        if n:
            pl.semaphore_wait(ready_sem.at[n - 1], 4)
        if n < 3:
            for device in near:
                pl.semaphore_signal(
                    ready_sem.at[n], inc=1, device_id=device, device_id_type=MESH
                )

    for load in loads[5:]:
        load.wait()
    small[...] = jnp.zeros_like(small)
    for weight, at in zip((proj_b, proj_c, proj_dt), range(3)):
        n = weight.shape[0]
        small[SMALL[0][at] : SMALL[0][at] + n, :] = weight[...]
        for k in range(BLOCKS):
            here, there = slice(k * Q, (k + 1) * Q), slice(D - (k + 1) * Q, D - k * Q)
            small[SMALL[1][at] : SMALL[1][at] + n, here] = mm(weight[:, there], anti).astype(BF16)
    loads[1].wait()
    ident = identity()
    for k in range(BLOCKS):
        here, there = slice(k * Q, (k + 1) * Q), slice(D - (k + 1) * Q, D - k * Q)
        hidden_t[k] = mm_t(ident, hidden[:, here]).astype(BF16)
        hidden_flip_t[k] = mm_t(anti, hidden[:, there]).astype(BF16)
    for load, source, flip in ((loads[2], proj_x, px_flip), (loads[3], proj_z, pz_flip)):
        load.wait()
        for k in range(BLOCKS):
            here, there = slice(k * Q, (k + 1) * Q), slice(D - (k + 1) * Q, D - k * Q)
            flip[here, :] = mm(anti, source[there, :]).astype(BF16)

    def project_step(k, carry):
        rows = rows_of(k)
        u = hidden[rows, :]
        xs[0, rows, :] = mm(u, proj_x[...])
        zs[0, rows, :] = mm(u, proj_z[...])
        xs[1, rows, :] = mm(u, px_flip[...])
        zs[1, rows, :] = mm(u, pz_flip[...])
        narrow = mm_t(u, small[...])
        for strand in range(2):
            at_b, at_c, at_dt = SMALL[strand]
            bs[strand, rows, :] = narrow[:, at_b : at_b + NS].astype(BF16)
            cs[strand, rows, :] = narrow[:, at_c : at_c + NS].astype(BF16)
            dts[strand, rows, :] = narrow[:, at_dt : at_dt + HEADS] + bias[...]
        return carry

    lax.fori_loop(0, CHUNKS, project_step, 0)
    loads[0].wait()
    pl.semaphore_wait(barrier, 7)
    for n in range(4):
        cot_copy(n).start()
    vouch(0)

    def state_step(i, carry):
        strand, k = i // CHUNKS, lax.rem(i, CHUNKS)
        rows = rows_of(k)
        dt = softplus(dts[strand, rows, :])
        a = -rate[...] * dt
        cum = running(a, order(1 - 2 * strand))
        total = jnp.sum(a, axis=0, keepdims=True)
        cums[strand, rows, :] = cum
        dts_soft[strand, rows, :] = dt
        e_rest = spread(jnp.exp(total - cum), e)
        dt_wide = spread(dt, e)
        e_cums[strand, rows, :] = spread(jnp.exp(cum), e)
        e_rests[strand, rows, :] = e_rest
        dt_wides[strand, rows, :] = dt_wide
        xd = xs[strand, rows, :] * dt_wide
        xdt[strand, rows, :] = xd.astype(BF16)
        chunk_state[strand, k] = t_mm(bs[strand, rows, :], (xd * e_rest).astype(BF16))
        chunk_decay[strand, k] = jnp.broadcast_to(jnp.exp(spread(total, e)), (8, W))
        return carry

    lax.fori_loop(0, 2 * CHUNKS, state_step, 0)
    vouch(1)

    def times(strand):
        return list(range(CHUNKS)) if strand == 0 else list(range(CHUNKS))[::-1]

    def two_halves(dst, rows, value):
        dst[0, rows, :] = value[:, 0:Q]
        dst[1, rows, :] = value[:, Q:]

    decays = []
    for strand in range(2):
        state, decay = chunk_state[strand, times(strand)[0]], chunk_decay[strand, 0]
        for k in times(strand)[1:]:
            state = chunk_decay[strand, k, 0:1, :] * state + chunk_state[strand, k]
        for k in range(1, CHUNKS):
            decay = decay * chunk_decay[strand, k]
        two_halves(a_msg, slice(16 * strand, 16 * strand + NS), state)
        decays.append(decay)
    two_halves(a_msg, slice(32, 40), jnp.where(iota((8, W), 0) == 0, decays[0], decays[1]))

    zero = jnp.zeros((NS, Q), F32)
    a_slots[place] = jnp.zeros_like(a_slots[0])
    b_slots[place] = jnp.zeros_like(b_slots[0])

    class Exchange:
        def __init__(self, base, msg, from_core, pair, slots, back, result, swap):
            self.base, self.msg, self.from_core, self.pair = base, msg, from_core, pair
            self.slots, self.back, self.result, self.swap = slots, back, result, swap

        def to_core(self):
            return remote(self.msg.at[other], self.from_core, self.base, core_peer)

        def to_place(self, dz, dy):
            to = lax.rem(z + dz, 4) * 4 + lax.rem(y + dy, 4)
            kind = jnp.where(to > place, 0, 1)
            return remote(
                self.pair.at[kind], self.slots.at[place], self.base + 4 * dz + dy, zy_peer(dz, dy)
            )

        def to_back(self):
            return remote(self.back, self.result.at[core], self.base + PEERS, core_peer)

        def decay(self, ref, strand):
            return ref[strand : strand + 1, :]

        def both(self):
            mine = (
                self.msg[core, 0:16, :], self.msg[core, 16:32, :],
                a_msg[core, 32 + self.swap : 33 + self.swap, :],
                a_msg[core, 33 - self.swap : 34 - self.swap, :],
            )
            theirs = (
                self.from_core[0:16, :], self.from_core[16:32, :],
                a_core[32 + self.swap : 33 + self.swap, :],
                a_core[33 - self.swap : 34 - self.swap, :],
            )
            return mine, theirs

        def spread_out(self):
            self.to_core().wait_recv()
            mine, theirs = self.both()
            first = [jnp.where(core == 0, m, t) for m, t in zip(mine, theirs)]
            second = [jnp.where(core == 0, t, m) for m, t in zip(mine, theirs)]
            up = second[2] * first[0] + second[0]
            down = first[3] * second[1] + first[1]
            self.pair[0, 0:16, :] = up
            self.pair[1, 0:16, :] = down
            if not self.swap:
                product = jnp.where(
                    iota((8, Q), 0) == 0,
                    jnp.broadcast_to(first[2] * second[2], (8, Q)),
                    jnp.broadcast_to(first[3] * second[3], (8, Q)),
                )
                self.pair[0, 16:24, :] = product
                self.pair[1, 16:24, :] = product
            for dz, dy in shifts:
                self.to_place(dz, dy).start()

        def collect(self):
            for dz, dy in shifts:
                self.to_place(dz, dy).wait_recv()
            up = down = zero
            for j in range(PEERS):
                r = PEERS - 1 - j
                decay_up = a_slots[j, 16 + self.swap : 17 + self.swap, :]
                decay_down = a_slots[r, 17 - self.swap : 18 - self.swap, :]
                up = jnp.where(j < place, decay_up * up + self.slots[j, 0:16, :], up)
                down = jnp.where(r > place, decay_down * down + self.slots[r, 0:16, :], down)
            mine, theirs = self.both()
            self.back[0:16, :] = jnp.where(core == 0, mine[2] * up + mine[0], up)
            self.back[16:32, :] = jnp.where(core == 1, mine[3] * down + mine[1], down)
            self.to_back().start()
            self.result[core, 0:16, :] = jnp.where(core == 1, theirs[2] * up + theirs[0], up)
            self.result[core, 16:32, :] = jnp.where(core == 0, theirs[3] * down + theirs[1], down)

        def take(self):
            self.to_back().wait_recv()
            return [
                jnp.concatenate([self.result[0, rows, :], self.result[1, rows, :]], axis=1)
                for rows in (slice(0, 16), slice(16, 32))
            ]

        def drain(self):
            self.to_core().wait_send()
            self.to_back().wait_send()
            for dz, dy in shifts:
                self.to_place(dz, dy).wait_send()

    round_a = Exchange(S_A, a_msg, a_core, a_pair, a_slots, a_back, a_in, 0)
    round_b = Exchange(S_B, b_msg, b_core, b_pair, b_slots, b_back, b_in, 1)
    round_a.to_core().start()

    lane = iota((Q, 128), 1)

    def within_step(i, carry):
        strand, k = i // CHUNKS, lax.rem(i, CHUNKS)
        rows = rows_of(k)
        mask = order(2 * strand - 1)
        cum = cums[strand, rows, :]
        cum_t = cum.T
        scores = mm_t(bs[strand, rows, :], cs[strand, rows, :])
        for pair in range(HEADS // 2):
            columns = slice(pair * 128, (pair + 1) * 128)
            x_pair = xdt[strand, rows, columns]
            y_sum = None
            for odd in range(2):
                h = 2 * pair + odd
                own = (lane >= HEAD) if odd else (lane < HEAD)
                x_own = jnp.where(own, x_pair, jnp.zeros((), BF16))
                decay = jnp.exp(
                    jnp.where(mask, cum_t[h : h + 1, :] - cum[:, h : h + 1], -1e30)
                )
                mixing = (decay * scores).astype(BF16)
                kept_decay[i, h] = decay.astype(BF16)
                y_new = t_mm(mixing, x_own)
                y_sum = y_new if y_sum is None else y_sum + y_new
            yi[strand, rows, columns] = y_sum

        @pl.when(i == 0)
        def _():
            vouch(2)
            for n in range(2):
                cot_copy(n).wait_recv()
                cot_copy(4 + n).start()

        @pl.when(i == 1)
        def _():
            vouch(3)
            round_a.spread_out()

        return carry

    lax.fori_loop(0, 2 * CHUNKS, within_step, 0)

    loads[4].wait()
    for k in range(BLOCKS):
        here, there = slice(k * Q, (k + 1) * Q), slice(D - (k + 1) * Q, D - k * Q)
        po_flip[:, here] = mm(proj_out[:, there], anti).astype(BF16)

    def cot_block(c, rows):
        block = cot[c, rows, :]
        cot_t[c, :, rows] = mm_t(ident, block).astype(BF16)
        cot_flip_t[BLOCKS - 1 - c, :, rows] = mm_t(anti, block).astype(BF16)
        columns = pl.ds(pl.multiple_of(c * Q, Q), Q)
        return mm_t(block, proj_out[:, columns]), mm_t(block, po_flip[:, columns])

    def first_step(k, carry):
        rows = rows_of(k)
        parts = [cot_block(c, rows) for c in (ch, before, after)]
        for strand in range(2):
            value = sum(part[strand] for part in parts)
            g_own[strand, pl.ds(2 * k, 2)] = value.reshape(2, 4, ROWS, W)
        return carry

    def last_step(k, carry):
        rows = rows_of(k)
        parts = cot_block(lax.rem(ch + 2, 4), rows)
        for strand in range(2):
            early = g_own[strand, pl.ds(2 * k, 2)].reshape(Q, W)
            dos[strand, rows, :] = (early + parts[strand]).astype(BF16)
        return carry

    for n in range(2, 4):
        cot_copy(n).wait_recv()
    lax.fori_loop(0, CHUNKS, first_step, 0)
    for n in range(4, 6):
        cot_copy(n).wait_recv()
    lax.fori_loop(0, CHUNKS, last_step, 0)

    def grad_step(i, carry):
        strand, k = i // CHUNKS, lax.rem(i, CHUNKS)
        rows = rows_of(k)
        gate = zs[strand, rows, :]
        dy = dos[strand, rows, :].astype(F32) * (gate * sigmoid(gate))
        dyb[strand, rows, :] = dy.astype(BF16)
        chunk_grad[strand, k] = t_mm(
            cs[strand, rows, :], (dy * e_cums[strand, rows, :]).astype(BF16)
        )
        return carry

    lax.fori_loop(0, 2 * CHUNKS, grad_step, 0)

    for strand in range(2):
        falling = times(strand)[::-1]
        grad = chunk_grad[strand, falling[0]]
        for k in falling[1:]:
            grad = chunk_decay[strand, k, 0:1, :] * grad + chunk_grad[strand, k]
        two_halves(b_msg, slice(16 - 16 * strand, 32 - 16 * strand), grad)
    round_b.to_core().start()

    round_a.collect()
    for strand, state in enumerate(round_a.take()):
        for k in times(strand):
            own_state = chunk_state[strand, k]
            chunk_state[strand, k] = state
            state = chunk_decay[strand, k, 0:1, :] * state + own_state
            chunk_dot[strand, k] = state

    skip_wide = spread(skip[...], e)

    def out_step(i, carry):
        strand, k = i // CHUNKS, lax.rem(i, CHUNKS)
        rows = rows_of(k)
        e_cum = e_cums[strand, rows, :]
        state = chunk_state[strand, k].astype(BF16)
        gate = zs[strand, rows, :]
        d_o = dos[strand, rows, :].astype(F32)
        sig = sigmoid(gate)
        silu = gate * sig
        dy = d_o * silu
        y_part = yi[strand, rows, :] + e_cum * mm(cs[strand, rows, :], state)
        out = y_part + skip_wide * xs[strand, rows, :]
        os[strand, rows, :] = (out * silu).astype(BF16)
        dzs[strand, rows, :] = (d_o * out * (sig + silu * (1.0 - sig))).astype(BF16)
        dcs[strand, rows, :] = mm_t((dy * e_cum).astype(BF16), state)
        dyy[strand, rows, :] = gather_heads(dy * y_part, e)
        yi[strand, rows, :] = skip_wide * dy

        @pl.when(i == 1)
        def _():
            round_b.spread_out()

        return carry

    lax.fori_loop(0, 2 * CHUNKS, out_step, 0)

    class ColumnSum:
        def __init__(self, base, compute, own, part, send, forward, recv):
            self.base, self.compute, self.own, self.part = base, compute, own, part
            self.send, self.forward, self.recv = send, forward, recv

        def copy(self, n):
            src, dst, to = (
                (self.send.at[1, half[0]], self.forward.at[0], 1),
                (self.send.at[1, half[1]], self.forward.at[1], 3),
                (self.send.at[0, half[1]], self.recv.at[0, half[1]], 1),
                (self.send.at[2, half[0]], self.recv.at[1, half[0]], 3),
                (self.send.at[0, half[0]], self.recv.at[0, half[0]], 1),
                (self.send.at[2, half[1]], self.recv.at[1, half[1]], 3),
            )[n]
            return remote(src, dst, self.base + n, x_peer(to))

        def columns(self, r):
            return pl.ds(pl.multiple_of(lax.rem(ch + r, 4) * Q, Q), Q)

        def far(self):
            for n in range(2):
                self.send[1, half[n], :] = self.compute(half[n], self.columns(2)).astype(BF16)
                self.copy(n).start()

        def near(self):
            self.send[0, half[1], :] = self.compute(half[1], self.columns(1)).astype(BF16)
            self.copy(2).start()
            self.send[2, half[0], :] = self.compute(half[0], self.columns(3)).astype(BF16)
            self.copy(3).start()
            self.part[0] = self.compute(half[0], self.columns(1))
            self.part[1] = self.compute(half[1], self.columns(3))

        def middle(self):
            for n, block in ((0, 0), (1, 2)):
                self.copy(n).wait_recv()
                self.send[block, half[n], :] = (
                    self.part[n] + self.forward[n].astype(F32)
                ).astype(BF16)
                self.copy(4 + n).start()

        def own_block(self):
            for n in range(2):
                self.own[half[n], :] = self.compute(half[n], self.columns(0))

        def finish(self, rows):
            return (
                self.own[rows, :]
                + self.recv[0, rows, :].astype(F32)
                + self.recv[1, rows, :].astype(F32)
            )

        def arrived(self):
            for n in range(2, 6):
                self.copy(n).wait_recv()

        def drain(self):
            for n in range(6):
                self.copy(n).wait_send()

    def mix_block(rows, columns):
        return mm(os[0, rows, :], proj_out[:, columns]) + mm(os[1, rows, :], po_flip[:, columns])

    def in_block(rows, columns):
        return (
            mm_t(dxs[0, rows, :], proj_x[columns, :])
            + mm_t(dzs[0, rows, :], proj_z[columns, :])
            + mm_t(dxs[1, rows, :], px_flip[columns, :])
            + mm_t(dzs[1, rows, :], pz_flip[columns, :])
            + mm(ext[rows, :], small[:, columns])
        )

    mix_sum = ColumnSum(S_MIX, mix_block, mix_own, mix_part, mix_send, mix_fwd, mix_recv)
    in_sum = ColumnSum(S_IN, in_block, in_own, in_part, in_send, in_fwd, in_recv)

    def g_core_copy(n):
        return remote(g_send.at[n], g_recv.at[n], S_GCORE + n, core_peer)

    def g_copy(n, at):
        stage, over_z, k = at // 6, at % 6 // 3, at % 3 + 1
        peer = zy_peer(k, 0) if over_z != stage else zy_peer(0, k)
        if stage:
            src, dst = t_send.at[n, over_z, k - 1], t_recv.at[n, over_z, k - 1]
        elif over_z:
            src, dst = h_send.at[n, lax.rem(z + k, 4), :, :, Q:W], h_recv.at[n, 1, k - 1]
        else:
            src, dst = h_send.at[n, :, lax.rem(y + k, 4), :, 0:Q], h_recv.at[n, 0, k - 1]
        return remote(src, dst, S_GPEER + 12 * n + at, peer)

    def x_copy(dz, dy):
        at = 4 * dz + dy
        return remote(
            h_send.at[2, lax.rem(z + dz, 4), lax.rem(y + dy, 4)], last_recv.at[at],
            S_LAST + at, zy_peer(dz, dy),
        )

    def weight_part(n, left, left_flip, right):
        def step(b, carry):
            value = mm(left[b], right[0]) + mm(left_flip[b], right[1])
            value = value.reshape(4, 2, ROWS, W)
            g_own[n, b] = jnp.where(core == 0, value[:, 0], value[:, 1])
            g_send[n, b] = jnp.where(core == 0, value[:, 1], value[:, 0]).astype(BF16)
            return carry

        lax.fori_loop(0, BLOCKS, step, 0)
        g_core_copy(n).start()

    def weight_pair(n):
        g_core_copy(n).wait_recv()

        def pair_sum(i, carry):
            at = (n, i // 4, lax.rem(i, 4))
            value = g_own[at] + g_recv[at].astype(F32)
            g_own[at] = value
            h_send[at] = value.astype(BF16)
            return carry

        lax.fori_loop(0, PEERS, pair_sum, 0)
        if n == 2:
            for dz, dy in shifts:
                x_copy(dz, dy).start()
        else:
            for at in range(6):
                g_copy(n, at).start()

    def weight_middle(n):
        for at in range(6):
            g_copy(n, at).wait_recv()
        for r in (1, 2, 3, 0):
            to_z, to_y = lax.rem(z + r, 4), lax.rem(y + r, 4)
            first, second = g_own[n, to_z, y, :, 0:Q], g_own[n, z, to_y, :, Q:W]
            for k in range(3):
                first = first + h_recv[n, 0, k, to_z].astype(F32)
                second = second + h_recv[n, 1, k, to_y].astype(F32)
            if r:
                t_send[n, 0, r - 1] = first.astype(BF16)
                t_send[n, 1, r - 1] = second.astype(BF16)
                g_copy(n, 6 + r - 1).start()
                g_copy(n, 9 + r - 1).start()
            else:
                t_own[n, 0] = first
                t_own[n, 1] = second

    def weight_total(n, out):
        for at in range(6, 12):
            g_copy(n, at).wait_recv()
        for side in range(2):
            total = t_own[n, side]
            for k in range(3):
                total = total + t_recv[n, side, k].astype(F32)
            out[:, side * Q : (side + 1) * Q] = total

    weight_part(0, cot_t, cot_flip_t, os)
    mix_sum.far()
    mix_sum.near()
    weight_part(1, hidden_t, hidden_flip_t, dzs)
    weight_pair(0)

    def inner_step(i, carry):
        strand, k = i // CHUNKS, lax.rem(i, CHUNKS)
        rows = rows_of(k)
        b = bs[strand, rows, :]
        c = cs[strand, rows, :]
        scores = mm_t(b, c)
        for pair in range(HEADS // 2):
            columns = slice(pair * 128, (pair + 1) * 128)
            x_pair, dy_pair = xdt[strand, rows, columns], dyb[strand, rows, columns]
            g_sum = None
            for odd in range(2):
                h = 2 * pair + odd
                own = (lane >= HEAD) if odd else (lane < HEAD)
                dy_own = jnp.where(own, dy_pair, jnp.zeros((), BF16))
                decay = kept_decay[i, h].astype(F32)
                part = decay * mm_t(x_pair, dy_own)
                if h == 0:
                    zacc[...] = part
                else:
                    zacc[...] += part
                g_new = mm((decay * scores).astype(BF16), dy_own)
                g_sum = g_new if g_sum is None else g_sum + g_new
            gi[strand, rows, columns] = g_sum
        pairs = zacc[...].astype(BF16)
        dbs[strand, rows, :] = mm(pairs, c)
        dcs[strand, rows, :] += t_mm(pairs, b)

        @pl.when(i == 1)
        def _():
            mix_sum.middle()
            weight_pair(1)

        @pl.when(i == 2)
        def _():
            round_b.collect()

        return carry

    lax.fori_loop(0, 2 * CHUNKS, inner_step, 0)

    mix_sum.own_block()

    up, down = round_b.take()
    for strand, grad in enumerate((down, up)):
        for k in times(strand)[::-1]:
            own_grad = chunk_grad[strand, k]
            chunk_grad[strand, k] = grad
            chunk_dot[strand, k, 0:8, :] = jnp.broadcast_to(
                jnp.sum(grad * chunk_dot[strand, k], axis=0, keepdims=True), (8, W)
            )
            grad = chunk_decay[strand, k, 0:1, :] * grad + own_grad
    ext[...] = jnp.zeros_like(ext)

    def back_step(k, carry):
        rows = rows_of(k)
        for strand in range(2):
            dt = dts_soft[strand, rows, :]
            e_rest = e_rests[strand, rows, :]
            dt_wide = dt_wides[strand, rows, :]
            grad = chunk_grad[strand, k].astype(BF16)
            x = xs[strand, rows, :]
            gb = gi[strand, rows, :] + e_rest * mm(bs[strand, rows, :], grad)
            dxs[strand, rows, :] = (dt_wide * gb + yi[strand, rows, :]).astype(BF16)
            d_b = dbs[strand, rows, :] + mm_t((x * dt_wide * e_rest).astype(BF16), grad)
            direct = gather_heads(x * gb, e)
            d_cum = dyy[strand, rows, :] - dt * direct
            d_a = running(d_cum, order(2 * strand - 1)) + gather_heads(
                chunk_dot[strand, k, 0:8, :], e
            )[0:1, :]
            d_raw = (direct - rate[...] * d_a) * sigmoid(dts[strand, rows, :])
            at_b, at_c, at_dt = SMALL[strand]
            ext[rows, at_b : at_b + NS] = d_b.astype(BF16)
            ext[rows, at_c : at_c + NS] = dcs[strand, rows, :].astype(BF16)
            ext[rows, at_dt : at_dt + HEADS] = d_raw.astype(BF16)
        return carry

    lax.fori_loop(0, CHUNKS, back_step, 0)

    weight_part(2, hidden_t, hidden_flip_t, dxs)
    in_sum.far()
    in_sum.near()
    weight_pair(2)
    in_sum.middle()
    in_sum.own_block()
    weight_middle(0)
    weight_middle(1)

    mix_sum.arrived()

    def mix_step(k, carry):
        rows = rows_of(k)
        mine = hidden[rows, pl.ds(pl.multiple_of(ch * Q, Q), Q)].astype(F32)
        block_out[rows, :] = (mine + mix_sum.finish(rows)).astype(BF16)
        return carry

    lax.fori_loop(0, CHUNKS, mix_step, 0)

    weight_total(0, grad_out)
    weight_total(1, grad_z)
    in_sum.arrived()

    def in_step(k, carry):
        rows = rows_of(k)
        grad_hidden[rows, :] = cot[ch, rows, :].astype(F32) + in_sum.finish(rows)
        return carry

    lax.fori_loop(0, CHUNKS, in_step, 0)

    total = g_own[2, z, y]
    for dz, dy in shifts:
        x_copy(dz, dy).wait_recv()
        total = total + last_recv[4 * dz + dy].astype(F32)
    grad_x[...] = total

    for n in range(6):
        cot_copy(n).wait_send()
    round_a.drain()
    round_b.drain()
    mix_sum.drain()
    in_sum.drain()
    for n in range(3):
        g_core_copy(n).wait_send()
    for at in range(12):
        g_copy(0, at).wait_send()
        g_copy(1, at).wait_send()
    for dz, dy in shifts:
        x_copy(dz, dy).wait_send()


def hand_over(*refs):
    sems = refs[10]
    copies = [pltpu.make_async_copy(refs[n], refs[5 + n], sems.at[n]) for n in range(5)]
    for copy in copies:
        copy.start()
    for copy in copies:
        copy.wait()


def shape(*dims, dtype=F32):
    return jax.ShapeDtypeStruct(dims, dtype)


VMEM = pl.BlockSpec(memory_space=pltpu.VMEM)


def body(
    hidden, proj_x, proj_z, proj_b, proj_c, proj_dt, dt_bias, decay_rate, skip_gain, proj_out, cotangent
):
    bias, rate, skip = (v[None, :] for v in (dt_bias, decay_rate, skip_gain))
    vm = pltpu.VMEM
    results = (
        shape(L, Q, dtype=BF16),
        shape(L, Q),
        shape(ROWS, W),
        shape(ROWS, W),
        shape(ROWS, W),
    )
    made = pl.pallas_call(
        block_kernel,
        out_shape=results,
        in_specs=[pl.BlockSpec(memory_space=pl.ANY)] * 11,
        out_specs=[VMEM] * 5,
        scratch_shapes=[
            vm((L, D), BF16), vm((D, W), BF16), vm((D, W), BF16), vm((W, D), BF16),
            vm((NS, D), BF16), vm((NS, D), BF16), vm((HEADS, D), BF16),
            vm((1, HEADS), F32), vm((1, HEADS), F32), vm((1, HEADS), F32),
            vm((D, W), BF16), vm((D, W), BF16), vm((W, D), BF16), vm((128, D), BF16),
            vm((BLOCKS, Q, L), BF16), vm((BLOCKS, Q, L), BF16),
            vm((BLOCKS, L, Q), BF16), vm((BLOCKS, Q, L), BF16), vm((BLOCKS, Q, L), BF16),
            vm((2, L, W), F32), vm((2, L, W), F32), vm((2, L, NS), BF16), vm((2, L, NS), BF16),
            vm((2, L, HEADS), F32), vm((2, L, W), BF16), vm((2, L, HEADS), F32),
            vm((2, L, HEADS), F32), vm((2, L, W), F32), vm((2, L, W), F32), vm((2, L, W), F32),
            vm((2, L, W), BF16), vm((2, L, W), BF16), vm((Q, Q), F32),
            vm((2 * CHUNKS, HEADS, Q, Q), BF16),
            vm((2, L, W), F32), vm((2, L, NS), F32), vm((2, L, NS), F32),
            vm((2, L, HEADS), F32),
            vm((L, 128), BF16), vm((2, L, W), BF16), vm((2, L, W), BF16),
            vm((2, CHUNKS, NS, W), F32), vm((2, CHUNKS, NS, W), F32),
            vm((2, CHUNKS, 8, W), F32), vm((2, CHUNKS, NS, W), F32),
            vm((2, 40, Q), F32), vm((40, Q), F32), vm((2, 24, Q), F32), vm((PEERS, 24, Q), F32),
            vm((32, Q), F32), vm((2, 32, Q), F32),
            vm((2, 32, Q), F32), vm((32, Q), F32), vm((2, 16, Q), F32), vm((PEERS, 16, Q), F32),
            vm((32, Q), F32), vm((2, 32, Q), F32),
            vm((L, Q), F32), vm((2, Q, Q), F32), vm((3, L, Q), BF16), vm((2, Q, Q), BF16),
            vm((2, L, Q), BF16),
            vm((L, Q), F32), vm((2, Q, Q), F32), vm((3, L, Q), BF16), vm((2, Q, Q), BF16),
            vm((2, L, Q), BF16),
            vm((3, 4, 4, ROWS, W), F32), vm((3, 4, 4, ROWS, W), BF16),
            vm((3, 4, 4, ROWS, W), BF16), vm((3, 4, 4, ROWS, W), BF16),
            vm((2, 2, 3, 4, ROWS, Q), BF16), vm((2, 2, 3, ROWS, Q), BF16),
            vm((2, 2, 3, ROWS, Q), BF16), vm((2, 2, ROWS, Q), F32), vm((PEERS, ROWS, W), BF16),
            pltpu.SemaphoreType.DMA((11,)),
            pltpu.SemaphoreType.DMA((S_ALL,)), pltpu.SemaphoreType.DMA((S_ALL,)),
            pltpu.SemaphoreType.REGULAR((3,)),
        ],
        compiler_params=pltpu.CompilerParams(
            vmem_limit_bytes=60 * 2**20, collective_id=0, has_side_effects=True
        ),
        name="block",
    )(
        hidden, proj_x, proj_z, proj_out, cotangent,
        proj_b.T, proj_c.T, proj_dt.T, bias, rate, skip,
    )
    *most, grad_out = pl.pallas_call(
        hand_over,
        out_shape=results,
        in_specs=[VMEM] * 5,
        out_specs=[pl.BlockSpec(memory_space=pl.ANY)] * 5,
        scratch_shapes=[pltpu.SemaphoreType.DMA((5,))],
        name="hand_over",
    )(*made)
    return *most, grad_out.T


def solution(mesh):
    return jax.shard_map(
        body,
        mesh=mesh,
        in_specs=(
            P("seq", None),
            P(None, "ch"),
            P(None, "ch"),
            P(),
            P(),
            P(None, "ch"),
            P("ch"),
            P("ch"),
            P("ch"),
            P("ch", None),
            P("seq", "ch"),
        ),
        out_specs=(P("seq", "ch"), P("seq", "ch"), P("seq", "ch"), P("seq", "ch"), P("ch", "seq")),
        check_vma=False,
    )
```
